32 devices in a mesh: group: 2 (over y), dom: 4 (over z), row: 4 (over x, core).
Axes of the slice: x: 2, y: 2, z: 4, core: 2. Of those that a mesh axis runs over, the one named last changes fastest.
Arguments:
- state: bfloat16 [8, 16, 10752], P(('group', 'dom'), 'row'), parts along dimension 0, may hold values from -6 to 6
- prev_pred: bfloat16 [8, 16, 10752], P(('group', 'dom'), 'row'), parts along dimension 0, may hold values from -6 to 6
- ancestors: int32 [8], P('group'), parts along dimension 0, may hold values from 0 to 3, as said below
- timestep: int32 [2], P('group'), parts along dimension 0, may hold values from 50 to 949
- w_in: bfloat16 [168, 256], replicated, may hold values from -0.5 to 0.5
- w_time: bfloat16 [256, 256], replicated, may hold values from -0.375 to 0.375
- w_qkv: bfloat16 [2, 256, 768], replicated, may hold values from -0.375 to 0.375
- w_attn_out: bfloat16 [2, 256, 256], replicated, may hold values from -0.375 to 0.375
- w_up: bfloat16 [2, 256, 1024], replicated, may hold values from -0.375 to 0.375
- w_down: bfloat16 [2, 1024, 256], replicated, may hold values from -0.1875 to 0.1875
- w_out: bfloat16 [256, 84], replicated, may hold values from -0.375 to 0.375
Outputs:
- new_state: bfloat16 [8, 16, 10752], P(('group', 'dom'), 'row'), parts along dimension 0
- new_pred: bfloat16 [8, 16, 10752], P(('group', 'dom'), 'row'), parts along dimension 0
The draws below stay inside these ranges and needn't reach their ends.
There are 2 independent parts, one for each index of `group`. The reference program is written for one: setup_inputs(seed, part) draws one part's arguments, and reference() takes and returns one part's arrays. A program takes and returns all parts, laid end to end along the dimension named above; an argument that names none is the same for every part. Nothing has to cross between parts.
Inputs may be any that keep to these rules, and one draw needn't show every extreme that they name: ancestors[j] is the particle of the same group whose state particle j takes; the list never falls.
All inputs are finite; a program needn't handle non-finite values.
Results may differ from the reference program's by a relative error of at most 0.018.
Values may be sent and summed in bfloat16 or wider, within the bound.
No kernel may reach another device: no remote copies, remote signals or barrier semaphores. Data moves between devices by JAX's collectives and lax.ppermute only.
A program may use at most 64 MiB of HBM per device.

```python
import math
import jax
import jax.numpy as jnp
from jax import lax

D = 256
HEADS = 8
FF = 1024
CH = 84
COLS = 128
BLOCKS = 2
STEPS = 1000
STRIDE = 20
PARTICLES = 4
HEIGHT = 16


def draw_ancestors(key, part):
    base_key = jax.random.fold_in(key, 17)
    score_key, offset_key = jax.random.split(base_key)
    levels = jax.random.randint(score_key, (PARTICLES,), 0, 8)
    masses = jnp.left_shift(jnp.ones_like(levels), levels).astype(jnp.int32)
    totals = jnp.cumsum(masses).astype(jnp.int32)
    overall = totals[-1]
    offset = jax.random.randint(offset_key, (), 0, overall)
    points = jnp.arange(PARTICLES, dtype=jnp.int32) * overall + offset
    lineage = jnp.sum((totals[None, :] * PARTICLES <= points[:, None]).astype(jnp.int32), axis=1)
    return lineage.astype(jnp.int32)


def block_scale(key, extent, cuts, low, top_value):
    def one(position, shards_of):
        steps = jax.random.uniform(jax.random.fold_in(jax.random.fold_in(key, 6), position), (shards_of,), jnp.float32, low / len(cuts), top_value / len(cuts))
        return jnp.repeat(jnp.exp(steps), extent[position] // shards_of).reshape((-1,) + (1,) * (len(extent) - position - 1))

    gain = one(*cuts[0])
    for cut in cuts[1:]:
        gain = gain * one(*cut)
    return gain


def gaussian(key, extent, spread, bound, cuts=(), kind=jnp.bfloat16):
    gain = block_scale(key, extent, cuts, -0.22, 0.18) if cuts else 1.0
    values = jax.random.normal(key, extent, jnp.float32) * spread * gain
    return jnp.minimum(jnp.maximum(values, -bound), bound).astype(kind)


def setup_inputs(seed: int = 0, part: int = 0) -> dict:
    key_of = jax.random.split(jax.random.key(seed), 12)
    part_keys = jax.random.split(jax.random.fold_in(key_of[11], part), 12)
    state = gaussian(part_keys[0], (PARTICLES, HEIGHT, COLS * CH), 1.0, 6.0, ((0, 4), (1, 4)))
    prev_pred = gaussian(part_keys[1], (PARTICLES, HEIGHT, COLS * CH), 1.0, 6.0, ((0, 4), (1, 4)))
    ancestors = draw_ancestors(jax.random.fold_in(jax.random.fold_in(key_of[11], part), 71), part)
    timestep = jax.random.randint(part_keys[3], (1,), 50, 950).astype(jnp.int32)
    w_in = gaussian(key_of[4], (2 * CH, D), (2 * CH) ** -0.5, 0.5)
    w_time = gaussian(key_of[5], (D, D), D ** -0.5, 0.375)
    w_qkv = gaussian(key_of[6], (BLOCKS, D, 3 * D), D ** -0.5, 0.375)
    w_attn_out = gaussian(key_of[7], (BLOCKS, D, D), D ** -0.5, 0.375)
    w_up = gaussian(key_of[8], (BLOCKS, D, FF), D ** -0.5, 0.375)
    w_down = gaussian(key_of[9], (BLOCKS, FF, D), FF ** -0.5, 0.1875)
    w_out = gaussian(key_of[10], (D, CH), D ** -0.5, 0.375)
    return {"state": state, "prev_pred": prev_pred, "ancestors": ancestors, "timestep": timestep, "w_in": w_in, "w_time": w_time, "w_qkv": w_qkv, "w_attn_out": w_attn_out, "w_up": w_up, "w_down": w_down, "w_out": w_out}


def rms_round(values_in):
    widened = values_in.astype(jnp.float32)
    scaled = widened * lax.rsqrt(lax.optimization_barrier(jnp.mean(widened * widened, axis=-1, keepdims=True)) + 1e-06)
    return scaled.astype(jnp.bfloat16)

def unit_rows(values_in):
    return values_in * lax.rsqrt(lax.optimization_barrier(jnp.mean(values_in * values_in, axis=-1, keepdims=True)) + 1e-06)

def rotate(values_in, span_len):
    half_size = values_in.shape[-1] // 2
    places = jnp.arange(span_len, dtype=jnp.float32)
    rates = jnp.exp(-math.log(10000.0) * jnp.arange(half_size, dtype=jnp.float32) / half_size)
    angles = places[:, None] * rates[None, :]
    cos_part = jnp.cos(angles)[:, None, None, :]
    sin_part = jnp.sin(angles)[:, None, None, :]
    leading = values_in[..., :half_size]
    trailing = values_in[..., half_size:]
    return jnp.concatenate([leading * cos_part - trailing * sin_part, leading * sin_part + trailing * cos_part], axis=-1)

def attend(normed, weight_qkv, weight_out):
    batch_size, span_len, side_len, model_width = normed.shape
    head_size = model_width // HEADS
    joined = jnp.dot(normed, weight_qkv, preferred_element_type=jnp.float32)
    queries = unit_rows(joined[..., :model_width]).reshape(batch_size, span_len, side_len, HEADS, head_size)
    key_rows = unit_rows(joined[..., model_width:2 * model_width]).reshape(batch_size, span_len, side_len, HEADS, head_size)
    values = joined[..., 2 * model_width:].astype(jnp.bfloat16).reshape(batch_size, span_len, side_len, HEADS, head_size)
    queries = rotate(queries, span_len).astype(jnp.bfloat16)
    key_rows = rotate(key_rows, span_len).astype(jnp.bfloat16)
    scores = jnp.einsum('blmhe,bkmhe->bmhlk', queries.astype(jnp.float32), key_rows.astype(jnp.float32)) / math.sqrt(head_size)
    weights = jnp.exp(scores)
    shares = (weights / lax.optimization_barrier(jnp.sum(weights, axis=-1, keepdims=True))).astype(jnp.bfloat16)
    mixture = jnp.einsum('bmhlk,bkmhe->blmhe', shares.astype(jnp.float32), values.astype(jnp.float32))
    mixture = mixture.astype(jnp.bfloat16).reshape(batch_size, span_len, side_len, model_width)
    return jnp.dot(mixture, weight_out, preferred_element_type=jnp.float32)

def mix_tokens(hidden, weight_qkv, weight_out):
    return (hidden.astype(jnp.float32) + attend(rms_round(hidden), weight_qkv, weight_out)).astype(jnp.bfloat16)

def feed_forward(hidden, weight_up, weight_down):
    lifted = jnp.dot(rms_round(hidden), weight_up, preferred_element_type=jnp.float32)
    gated = jax.nn.gelu(lifted, approximate=True).astype(jnp.bfloat16)
    return (hidden.astype(jnp.float32) + jnp.dot(gated, weight_down, preferred_element_type=jnp.float32)).astype(jnp.bfloat16)

def level(moment):
    cosine = jnp.cos((moment / STEPS + 0.008) / 1.008 * math.pi / 2.0)
    return cosine * cosine

def time_vector(timestep, w_time):
    moment = timestep[0].astype(jnp.float32)
    half_size = w_time.shape[0] // 2
    rates = jnp.exp(-math.log(10000.0) * jnp.arange(half_size, dtype=jnp.float32) / half_size)
    embedded = jnp.concatenate([jnp.sin(moment * rates), jnp.cos(moment * rates)])
    return jnp.dot(embedded, w_time.astype(jnp.float32), precision=lax.Precision.HIGHEST)

def reference(state, prev_pred, ancestors, timestep, w_in, w_time, w_qkv, w_attn_out, w_up, w_down, w_out):
    offset_vec = time_vector(timestep, w_time)
    moment = timestep[0].astype(jnp.float32)
    level_now = level(moment)
    level_next = level(moment - STRIDE)
    chosen_state = jnp.take(state, ancestors, axis=0)
    chosen_prev = jnp.take(prev_pred, ancestors, axis=0)

    def denoise(pieces):
        state_rows, prev_rows = pieces
        height_len = state_rows.shape[0]
        joined = jnp.concatenate([state_rows.reshape(height_len, COLS, CH), prev_rows.reshape(height_len, COLS, CH)], axis=-1)
        hidden = (jnp.dot(joined, w_in, preferred_element_type=jnp.float32) + offset_vec).astype(jnp.bfloat16)
        hidden = hidden[:, :, None, :]
        hidden = mix_tokens(hidden, w_qkv[0], w_attn_out[0])
        hidden = feed_forward(hidden, w_up[0], w_down[0])
        hidden = hidden.reshape(1, height_len, COLS, hidden.shape[-1])
        hidden = mix_tokens(hidden, w_qkv[1], w_attn_out[1])
        hidden = feed_forward(hidden, w_up[1], w_down[1])
        predicted = jnp.dot(rms_round(hidden), w_out, preferred_element_type=jnp.float32).astype(jnp.bfloat16)
        predicted = predicted.reshape(height_len, COLS * CH)
        widened = state_rows.astype(jnp.float32)
        pred_wide = predicted.astype(jnp.float32)
        noise_est = (widened - jnp.sqrt(level_now) * pred_wide) / jnp.sqrt(1.0 - level_now)
        updated = (jnp.sqrt(level_next) * pred_wide + jnp.sqrt(1.0 - level_next) * noise_est).astype(jnp.bfloat16)
        return (updated, predicted)
    new_state, new_pred = lax.map(denoise, (chosen_state, chosen_prev))
    return (new_state, new_pred)
```

```python
import functools
import math

import jax
import jax.numpy as jnp
import numpy as np
from jax import lax
from jax.experimental import pallas as pl
from jax.experimental.pallas import tpu as pltpu
from jax.sharding import PartitionSpec as P

HEADS = 8
STEPS = 1000
STRIDE = 20
EPS = 1e-06
LANES = 128
VMEM_LIMIT = 48 * 1024 * 1024
F32 = jnp.float32
BF16 = jnp.bfloat16


def dot(lhs, rhs):
    return jnp.dot(lhs, rhs, preferred_element_type=F32)


def dot_nt(lhs, rhs):
    return lax.dot_general(lhs, rhs, (((1,), (1,)), ((), ())), preferred_element_type=F32)


def rms_scale(wide):
    return lax.rsqrt(jnp.mean(wide * wide, axis=-1, keepdims=True) + EPS)


def rms_round(values_in):
    wide = values_in.astype(F32)
    return (wide * rms_scale(wide)).astype(BF16)


def gelu(values_in):
    return jax.nn.gelu(values_in, approximate=True)


def feed_forward(hidden, w_up, w_down):
    gated = gelu(dot(rms_round(hidden), w_up)).astype(BF16)
    return (hidden.astype(F32) + dot(gated, w_down)).astype(BF16)


def lane_ids(shape):
    return lax.broadcasted_iota(jnp.int32, shape, len(shape) - 1)


def shuffle_matrix(width, source_of):
    rows = lax.broadcasted_iota(jnp.int32, (width, width), 0)
    cols = lax.broadcasted_iota(jnp.int32, (width, width), 1)
    return jnp.where(rows == source_of(cols), 1.0, 0.0).astype(BF16)


def tile_halves(half, j):
    tile, lane = j // LANES, j % LANES
    side, rest = lane // (LANES // 2), lane % (LANES // 2)
    return tile * LANES + (rest // half) * 2 * half + side * half + rest % half


def full_halves(width, half, j):
    side, rest = j // (width // 2), j % (width // 2)
    return (rest // half) * 2 * half + side * half + rest % half


def rotary_angles(count, half, lanes):
    rates = np.exp(-math.log(10000.0) * np.arange(half) / half)
    return np.arange(count)[:, None] * rates[np.arange(lanes) % half][None, :]


def unpack_tokens(flat_ref, out_ref, cols, chan):
    count = flat_ref.shape[0]
    lane = lane_ids((count, LANES))
    for col in range(cols):
        tile, shift = divmod(col * chan, LANES)
        piece = flat_ref[:, tile * LANES : (tile + 1) * LANES]
        if shift + chan > LANES:
            after = flat_ref[:, (tile + 1) * LANES : (tile + 2) * LANES]
            piece = jnp.where(lane >= shift, piece, after)
        if shift:
            piece = pltpu.roll(piece, LANES - shift, 1)
        out_ref[pl.ds(col, count, stride=cols), :] = piece


def pack_tokens(tok_ref, out_ref, rows, cols, chan):
    lane = lane_ids((rows, LANES))
    moved = {}

    def shifted(col):
        if col not in moved:
            piece = tok_ref[pl.ds(col, rows, stride=cols), :]
            shift = (col * chan) % LANES
            moved[col] = pltpu.roll(piece, shift, 1) if shift else piece
        return moved[col]

    for tile in range(cols * chan // LANES):
        first, last = tile * LANES // chan, ((tile + 1) * LANES - 1) // chan
        whole = shifted(last)
        for col in range(last - 1, first - 1, -1):
            whole = jnp.where(lane < (col + 1) * chan - tile * LANES, shifted(col), whole)
        out_ref[0, :, tile * LANES : (tile + 1) * LANES] = whole.astype(BF16)


def row_kernel(
    rows, cols, chan,
    state_ref, prev_ref, temb_ref, w_in_ref, w_qkv_ref, w_ao_ref, w_up_ref, w_down_ref, cos_ref, sin_ref,
    out_ref,
    flat_scr, tok_scr,
):
    width = out_ref.shape[-1]
    head = width // HEADS
    half = head // 2
    flat_scr[:rows, :] = state_ref[0].astype(F32)
    flat_scr[rows:, :] = prev_ref[0].astype(F32)
    unpack_tokens(flat_scr, tok_scr, cols, chan)
    count = rows * cols
    w_in = w_in_ref[...].astype(F32)
    blank = jnp.zeros((LANES - chan, width), F32)
    w_state = jnp.concatenate([w_in[:chan], blank], axis=0).astype(BF16)
    w_prev = jnp.concatenate([w_in[chan:], blank], axis=0).astype(BF16)
    hidden = dot(tok_scr[:count].astype(BF16), w_state) + dot(tok_scr[count:].astype(BF16), w_prev)
    hidden = (hidden + temb_ref[...]).astype(BF16)

    pick = shuffle_matrix(width, functools.partial(tile_halves, half))
    w_q = dot(w_qkv_ref[0, :, :width], pick).astype(BF16)
    w_k = dot(w_qkv_ref[0, :, width : 2 * width], pick).astype(BF16)
    w_v = w_qkv_ref[0, :, 2 * width :]
    normed = rms_round(hidden)
    cos, sin = cos_ref[...], sin_ref[...]
    lane = lane_ids((cols, LANES))
    per_tile = LANES // head
    pair = per_tile // 2

    def spin(part):
        scaled = part * rms_scale(part)
        tiles = []
        for t in range(width // LANES):
            piece = scaled[:, t * LANES : (t + 1) * LANES].reshape(rows, cols, LANES)
            swapped = pltpu.roll(piece, LANES // 2, 2)
            tiles.append(piece * cos[None] + swapped * sin[None])
        return tiles

    scale = 1.0 / math.sqrt(head)
    queries = [(x * scale).astype(BF16) for x in spin(dot(normed, w_q))]
    keys = [x.astype(BF16) for x in spin(dot(normed, w_k))]
    values = dot(normed, w_v).astype(BF16).reshape(rows, cols, width)

    mixtures = []
    for row in range(rows):
        outs = []
        for t in range(width // LANES):
            q_tile, k_tile = queries[t][row], keys[t][row]
            v_tile = values[row, :, t * LANES : (t + 1) * LANES]
            results = []
            for side in range(2):
                k_parts, v_parts = [], []
                for n in range(side * pair, (side + 1) * pair):
                    own = (lane % (LANES // 2)) // half == n
                    k_parts.append(jnp.where(own, k_tile, jnp.zeros_like(k_tile)))
                    ones = jnp.where((lane // head) == (n + pair) % per_tile, 1.0, 0.0).astype(BF16)
                    v_parts.append(jnp.where(lane // head == n, v_tile, ones))
                score = dot_nt(q_tile, jnp.concatenate(k_parts, axis=0))
                results.append(dot(jnp.exp(score).astype(BF16), jnp.concatenate(v_parts, axis=0)))
            low = lane < LANES // 2
            top = jnp.where(low, results[0], results[1])
            bottom = pltpu.roll(jnp.where(low, results[1], results[0]), LANES // 2, 1)
            outs.append(top / bottom)
        mixtures.append(jnp.concatenate(outs, axis=-1))
    mixture = jnp.concatenate(mixtures, axis=0).astype(BF16)
    hidden = (hidden.astype(F32) + dot(mixture, w_ao_ref[0])).astype(BF16)
    out_ref[...] = feed_forward(hidden, w_up_ref[0], w_down_ref[0])


def column_kernel(
    blocks, rows, cols, chan,
    me_ref, *refs,
):
    h_refs = refs[:blocks]
    w_qkv_ref, w_ao_ref, w_up_ref, w_down_ref, w_out_ref, cos_ref, sin_ref, out_ref, k_scr, v_scr, tok_scr = refs[blocks:]
    width = h_refs[0].shape[-1]
    head = width // HEADS
    half = head // 2
    wide = width // 2
    pick = shuffle_matrix(width, functools.partial(full_halves, width, half))
    w_q = dot(w_qkv_ref[0, :, :width], pick).astype(BF16)
    w_k = dot(w_qkv_ref[0, :, width : 2 * width], pick).astype(BF16)
    w_v = dot(w_qkv_ref[0, :, 2 * width :], pick).astype(BF16)
    w_ao = lax.dot_general(pick, w_ao_ref[0], (((0,), (0,)), ((), ())), preferred_element_type=F32).astype(BF16)

    def spin(part, block, factor):
        scaled = part * (rms_scale(part) * factor)
        scaled = scaled.reshape(rows, cols, width)
        first = lax.bitwise_xor(me_ref[0], block) * rows
        left, right = [], []
        for row in range(rows):
            cos, sin = cos_ref[pl.ds(first + row, 1), :], sin_ref[pl.ds(first + row, 1), :]
            a, c = scaled[row, :, :wide], scaled[row, :, wide:]
            left.append((a * cos - c * sin).astype(BF16))
            right.append((a * sin + c * cos).astype(BF16))
        return left, right

    own = h_refs[0][...]
    q_left, q_right = spin(dot(rms_round(own), w_q), 0, 1.0 / math.sqrt(head))
    q_left, q_right = jnp.stack(q_left), jnp.stack(q_right)
    for block in range(blocks):
        normed = rms_round(h_refs[block][...])
        left, right = spin(dot(normed, w_k), block, 1.0)
        for row in range(rows):
            k_scr[block * rows + row, :, :wide] = left[row]
            k_scr[block * rows + row, :, wide:] = right[row]
        v_scr[block * rows : (block + 1) * rows] = dot(normed, w_v).astype(BF16).reshape(rows, cols, width)

    ids0 = lax.broadcasted_iota(jnp.int32, (width, width), 0)
    ids1 = lax.broadcasted_iota(jnp.int32, (width, width), 1)
    gather = jnp.where(ids0 // half == ids1 // half, 1.0, 0.0).astype(BF16)
    num_left = jnp.zeros((rows, cols, wide), F32)
    num_right = jnp.zeros((rows, cols, wide), F32)
    den = jnp.zeros((rows, cols, wide), F32)
    for two in range(blocks * rows // 2):
        prods = []
        for key in (2 * two, 2 * two + 1):
            prods.append(q_left * k_scr[key, :, :wide][None] + q_right * k_scr[key, :, wide:][None])
        score = dot(jnp.concatenate(prods, axis=-1).reshape(rows * cols, width), gather)
        weight = jnp.exp(score).reshape(rows, cols, width)
        for side, key in enumerate((2 * two, 2 * two + 1)):
            share = weight[..., side * wide : (side + 1) * wide]
            num_left += share * v_scr[key, :, :wide].astype(F32)[None]
            num_right += share * v_scr[key, :, wide:].astype(F32)[None]
            den += share
    mixture = jnp.concatenate([num_left / den, num_right / den], axis=-1).astype(BF16)
    hidden = (own.astype(F32) + dot(mixture.reshape(rows * cols, width), w_ao)).astype(BF16)
    hidden = feed_forward(hidden, w_up_ref[0], w_down_ref[0])
    tok_scr[:, :chan] = dot(rms_round(hidden), w_out_ref[...])
    pack_tokens(tok_scr, out_ref, rows, cols, chan)


def finish_kernel(count, pick_ref, coef_ref, state_ref, *refs):
    preds = refs[:count]
    new_state_ref, new_pred_ref = refs[count:]
    chosen = preds[0][...]
    for k in range(1, count):
        chosen = jnp.where(pick_ref[1] == k, preds[k][...], chosen)
    new_pred_ref[...] = chosen
    new_state_ref[...] = (coef_ref[0] * chosen.astype(F32) + coef_ref[1] * state_ref[...].astype(F32)).astype(BF16)


def level(moment):
    cosine = jnp.cos((moment / STEPS + 0.008) / 1.008 * math.pi / 2.0)
    return cosine * cosine


def time_vector(timestep, w_time):
    moment = timestep[0].astype(F32)
    half_size = w_time.shape[0] // 2
    rates = jnp.exp(-math.log(10000.0) * jnp.arange(half_size, dtype=F32) / half_size)
    embedded = jnp.concatenate([jnp.sin(moment * rates), jnp.cos(moment * rates)])
    return jnp.dot(embedded, w_time.astype(F32), precision=lax.Precision.HIGHEST)


VMEM_SPEC = pl.BlockSpec(memory_space=pltpu.VMEM)
SMEM_SPEC = pl.BlockSpec(memory_space=pltpu.SMEM)


def exchange(value, axis, size):
    blocks = [value]
    step = size // 2
    order = [0]
    while step:
        pairs = [(i, i ^ step) for i in range(size)]
        blocks = blocks + [lax.ppermute(b, axis, pairs) for b in blocks]
        order = order + [o ^ step for o in order]
        step //= 2
    return [blocks[order.index(b)] for b in range(size)]


def make(mesh):
    n_dom, n_row = mesh.shape["dom"], mesh.shape["row"]

    def per_device(
        state, prev_pred, ancestors, timestep, w_in, w_time, w_qkv, w_attn_out, w_up, w_down, w_out
    ):
        rows, flat = state.shape[1], state.shape[2]
        chan, width = w_out.shape[1], w_out.shape[0]
        cols = flat // chan
        head = width // HEADS
        half = head // 2
        offset_vec = time_vector(timestep, w_time)
        moment = timestep[0].astype(F32)
        now, after = level(moment), level(moment - STRIDE)
        keep = jnp.sqrt(1.0 - after) / jnp.sqrt(1.0 - now)
        coefs = jnp.stack([jnp.sqrt(after) - keep * jnp.sqrt(now), keep])
        all_states = lax.all_gather(state, "dom", tiled=True)
        my_dom = lax.axis_index("dom")
        mine = ancestors[my_dom]
        params = pltpu.CompilerParams(vmem_limit_bytes=VMEM_LIMIT)

        along = rotary_angles(cols, half, LANES)
        sign = np.where(np.arange(LANES) < LANES // 2, -1.0, 1.0)
        block_of = lambda i: lambda *_: (i, 0, 0)
        per_block = lambda arr, i: pl.BlockSpec((1,) + arr.shape[1:], block_of(i))
        whole = lambda arr: pl.BlockSpec(arr.shape, lambda *_: (0,) * arr.ndim)
        tables = [jnp.asarray(np.cos(along), F32), jnp.asarray(np.sin(along) * sign, F32)]
        temb = offset_vec[None, :]
        hidden = pl.pallas_call(
            functools.partial(row_kernel, rows, cols, chan),
            grid=(1,),
            out_shape=jax.ShapeDtypeStruct((rows * cols, width), BF16),
            in_specs=[
                whole(state), whole(prev_pred), whole(temb), whole(w_in),
                per_block(w_qkv, 0), per_block(w_attn_out, 0), per_block(w_up, 0), per_block(w_down, 0),
                whole(tables[0]), whole(tables[1]),
            ],
            out_specs=pl.BlockSpec((rows * cols, width), lambda *_: (0, 0)),
            scratch_shapes=[
                pltpu.VMEM((2 * rows, flat), F32),
                pltpu.VMEM((2 * rows * cols, LANES), F32),
            ],
            compiler_params=params,
            name="row_block",
        )(state, prev_pred, temb, w_in, w_qkv, w_attn_out, w_up, w_down, *tables)

        blocks = exchange(hidden, "row", n_row)
        down = rotary_angles(n_row * rows, half, width // 2)
        tables = [jnp.asarray(np.cos(down), F32), jnp.asarray(np.sin(down), F32)]
        me = lax.axis_index("row").astype(jnp.int32)[None]
        own_pred = pl.pallas_call(
            functools.partial(column_kernel, n_row, rows, cols, chan),
            grid=(1,),
            out_shape=jax.ShapeDtypeStruct((1, rows, flat), BF16),
            in_specs=[SMEM_SPEC]
            + [whole(hidden)] * n_row
            + [
                per_block(w_qkv, 1), per_block(w_attn_out, 1), per_block(w_up, 1), per_block(w_down, 1),
                whole(w_out), whole(tables[0]), whole(tables[1]),
            ],
            out_specs=pl.BlockSpec((1, rows, flat), lambda *_: (0, 0, 0)),
            scratch_shapes=[
                pltpu.VMEM((n_row * rows, cols, width), BF16),
                pltpu.VMEM((n_row * rows, cols, width), BF16),
                pltpu.VMEM((rows * cols, LANES), F32),
            ],
            compiler_params=params,
            name="column_block",
        )(me, *blocks, w_qkv, w_attn_out, w_up, w_down, w_out, *tables)

        if n_dom & (n_dom - 1) == 0 and n_dom <= 8:
            preds = [own_pred] + [
                lax.ppermute(own_pred, "dom", [(i, i ^ k) for i in range(n_dom)]) for k in range(1, n_dom)
            ]
            choice = jnp.bitwise_xor(mine, my_dom)
        else:
            preds = [lax.dynamic_index_in_dim(lax.all_gather(own_pred, "dom"), mine, 0, keepdims=False)]
            choice = jnp.zeros_like(mine)
        shape = jax.ShapeDtypeStruct(state.shape, BF16)
        picks = jnp.stack([mine, choice]).astype(jnp.int32)
        return pl.pallas_call(
            functools.partial(finish_kernel, len(preds)),
            out_shape=(shape, shape),
            grid_spec=pltpu.PrefetchScalarGridSpec(
                num_scalar_prefetch=1,
                grid=(1,),
                in_specs=[SMEM_SPEC, pl.BlockSpec(state.shape, lambda _, pick: (pick[0], 0, 0))]
                + [pl.BlockSpec(state.shape, lambda *_: (0, 0, 0))] * len(preds),
                out_specs=[pl.BlockSpec(state.shape, lambda *_: (0, 0, 0))] * 2,
            ),
            compiler_params=params,
            name="finish",
        )(picks, coefs, all_states, *preds)

    return per_device


def solution(mesh):
    spread = P(("group", "dom"), "row", None)
    return jax.shard_map(
        make(mesh),
        mesh=mesh,
        in_specs=(spread, spread, P("group"), P("group")) + (P(),) * 7,
        out_specs=(spread, spread),
        check_vma=False,
    )
```

```python
import functools
import math

import jax
import jax.numpy as jnp
import numpy as np
from jax import lax
from jax.experimental import pallas as pl
from jax.experimental.pallas import tpu as pltpu
from jax.sharding import PartitionSpec as P

HEADS = 8
STEPS = 1000
STRIDE = 20
EPS = 1e-06
LANES = 128
VMEM_LIMIT = 32 * 1024 * 1024
ROW_VMEM_LIMIT = 62 * 1024 * 1024
WORK_UNIT = 1 << 30
F32 = jnp.float32
BF16 = jnp.bfloat16


def dot(lhs, rhs):
    return jnp.dot(lhs, rhs, preferred_element_type=F32)


def dot_nt(lhs, rhs):
    return lax.dot_general(lhs, rhs, (((1,), (1,)), ((), ())), preferred_element_type=F32)


def rms_scale(wide):
    return lax.rsqrt(jnp.mean(wide * wide, axis=-1, keepdims=True) + EPS)


def rms_round(values_in):
    wide = values_in.astype(F32)
    return (wide * rms_scale(wide)).astype(BF16)


def gelu(values_in):
    return jax.nn.gelu(values_in, approximate=True)


def feed_forward(hidden, w_up, w_down):
    gated = gelu(dot(rms_round(hidden), w_up)).astype(BF16)
    return (hidden.astype(F32) + dot(gated, w_down)).astype(BF16)


def lane_ids(shape):
    return lax.broadcasted_iota(jnp.int32, shape, len(shape) - 1)


def shuffle_matrix(width, source_of):
    rows = lax.broadcasted_iota(jnp.int32, (width, width), 0)
    cols = lax.broadcasted_iota(jnp.int32, (width, width), 1)
    return jnp.where(rows == source_of(cols), 1.0, 0.0).astype(BF16)


def tile_halves(half, j):
    tile, lane = j // LANES, j % LANES
    side, rest = lane // (LANES // 2), lane % (LANES // 2)
    return tile * LANES + (rest // half) * 2 * half + side * half + rest % half


def full_halves(width, half, j):
    side, rest = j // (width // 2), j % (width // 2)
    return (rest // half) * 2 * half + side * half + rest % half


def rotary_angles(count, half, lanes):
    rates = np.exp(-math.log(10000.0) * np.arange(half) / half)
    return np.arange(count)[:, None] * rates[np.arange(lanes) % half][None, :]


def unpack_tokens(flat_ref, out_ref, cols, chan):
    count = flat_ref.shape[0]
    lane = lane_ids((count, LANES))
    for col in range(cols):
        tile, shift = divmod(col * chan, LANES)
        piece = flat_ref[:, tile * LANES : (tile + 1) * LANES]
        if shift + chan > LANES:
            after = flat_ref[:, (tile + 1) * LANES : (tile + 2) * LANES]
            piece = jnp.where(lane >= shift, piece, after)
        if shift:
            piece = pltpu.roll(piece, LANES - shift, 1)
        out_ref[pl.ds(col, count, stride=cols), :] = piece


def pack_tokens(tok_ref, out_ref, rows, cols, chan):
    lane = lane_ids((rows, LANES))
    moved = {}

    def shifted(col):
        if col not in moved:
            piece = tok_ref[pl.ds(col, rows, stride=cols), :]
            shift = (col * chan) % LANES
            moved[col] = pltpu.roll(piece, shift, 1) if shift else piece
        return moved[col]

    for tile in range(cols * chan // LANES):
        first, last = tile * LANES // chan, ((tile + 1) * LANES - 1) // chan
        whole = shifted(last)
        for col in range(last - 1, first - 1, -1):
            whole = jnp.where(lane < (col + 1) * chan - tile * LANES, shifted(col), whole)
        out_ref[0, :, tile * LANES : (tile + 1) * LANES] = whole.astype(BF16)


def time_vector(moment, w_time):
    half = w_time.shape[0] // 2
    rates = jnp.exp(lane_ids((1, half)).astype(F32) * (-math.log(10000.0) / half))
    angles = moment * rates
    embedded = jnp.concatenate([jnp.sin(angles), jnp.cos(angles)], axis=-1)
    first = embedded.astype(BF16)
    rest = embedded - first.astype(F32)
    second = rest.astype(BF16)
    third = (rest - second.astype(F32)).astype(BF16)
    return dot(first, w_time) + dot(second, w_time) + dot(third, w_time)


def row_kernel(
    rows, cols, chan,
    time_ref, state_ref, prev_ref, w_time_ref, w_in_ref, w_qkv_ref, w_ao_ref, w_up_ref, w_down_ref, cos_ref, sin_ref,
    out_ref,
    time_scr, state_scr, prev_scr, w_time_scr, w_in_scr, w_qkv_scr, w_ao_scr, w_up_scr, w_down_scr, cos_scr, sin_scr,
    flat_scr, tok_scr, sems,
):
    sources = (
        time_ref, state_ref, prev_ref, w_time_ref, w_in_ref, w_qkv_ref.at[0], cos_ref, sin_ref,
        w_ao_ref.at[0], w_up_ref.at[0], w_down_ref.at[0],
    )
    targets = (
        time_scr, state_scr, prev_scr, w_time_scr, w_in_scr, w_qkv_scr, cos_scr, sin_scr,
        w_ao_scr, w_up_scr, w_down_scr,
    )
    copies = [pltpu.make_async_copy(s, t, sems.at[i]) for i, (s, t) in enumerate(zip(sources, targets))]
    for copy in copies:
        copy.start()
    width = out_ref.shape[-1]
    head = width // HEADS
    half = head // 2
    copies[0].wait()
    copies[1].wait()
    flat_scr[:rows, :] = state_scr[0].astype(F32)
    copies[2].wait()
    flat_scr[rows:, :] = prev_scr[0].astype(F32)
    unpack_tokens(flat_scr, tok_scr, cols, chan)
    count = rows * cols
    copies[3].wait()
    offset_vec = time_vector(time_scr[0].astype(F32), w_time_scr[...])
    copies[4].wait()
    w_in = w_in_scr[...].astype(F32)
    blank = jnp.zeros((LANES - chan, width), F32)
    w_state = jnp.concatenate([w_in[:chan], blank], axis=0).astype(BF16)
    w_prev = jnp.concatenate([w_in[chan:], blank], axis=0).astype(BF16)
    hidden = dot(tok_scr[:count].astype(BF16), w_state) + dot(tok_scr[count:].astype(BF16), w_prev)
    hidden = (hidden + offset_vec).astype(BF16)

    copies[5].wait()
    copies[6].wait()
    copies[7].wait()
    pick = shuffle_matrix(width, functools.partial(tile_halves, half))
    w_q = dot(w_qkv_scr[:, :width], pick).astype(BF16)
    w_k = dot(w_qkv_scr[:, width : 2 * width], pick).astype(BF16)
    w_v = w_qkv_scr[:, 2 * width :]
    normed = rms_round(hidden)
    cos, sin = cos_scr[...], sin_scr[...]
    lane = lane_ids((cols, LANES))
    per_tile = LANES // head
    pair = per_tile // 2

    def spin(part):
        scaled = part * rms_scale(part)
        tiles = []
        for t in range(width // LANES):
            piece = scaled[:, t * LANES : (t + 1) * LANES].reshape(rows, cols, LANES)
            swapped = pltpu.roll(piece, LANES // 2, 2)
            tiles.append(piece * cos[None] + swapped * sin[None])
        return tiles

    scale = 1.0 / math.sqrt(head)
    queries = [(x * scale).astype(BF16) for x in spin(dot(normed, w_q))]
    keys = [x.astype(BF16) for x in spin(dot(normed, w_k))]
    values = dot(normed, w_v).astype(BF16).reshape(rows, cols, width)

    mixtures = []
    for row in range(rows):
        outs = []
        for t in range(width // LANES):
            q_tile, k_tile = queries[t][row], keys[t][row]
            v_tile = values[row, :, t * LANES : (t + 1) * LANES]
            results = []
            for side in range(2):
                k_parts, v_parts = [], []
                for n in range(side * pair, (side + 1) * pair):
                    own = (lane % (LANES // 2)) // half == n
                    k_parts.append(jnp.where(own, k_tile, jnp.zeros_like(k_tile)))
                    ones = jnp.where((lane // head) == (n + pair) % per_tile, 1.0, 0.0).astype(BF16)
                    v_parts.append(jnp.where(lane // head == n, v_tile, ones))
                score = dot_nt(q_tile, jnp.concatenate(k_parts, axis=0))
                results.append(dot(jnp.exp(score).astype(BF16), jnp.concatenate(v_parts, axis=0)))
            low = lane < LANES // 2
            top = jnp.where(low, results[0], results[1])
            bottom = pltpu.roll(jnp.where(low, results[1], results[0]), LANES // 2, 1)
            outs.append(top / bottom)
        mixtures.append(jnp.concatenate(outs, axis=-1))
    mixture = jnp.concatenate(mixtures, axis=0).astype(BF16)
    copies[8].wait()
    hidden = (hidden.astype(F32) + dot(mixture, w_ao_scr[...])).astype(BF16)
    copies[9].wait()
    copies[10].wait()
    out_ref[...] = feed_forward(hidden, w_up_scr[...], w_down_scr[...])


def project_keys(rows, cols, half, me_ref, block, h_ref, w_k, w_v, cos_ref, sin_ref):
    wide = HEADS * half
    normed = rms_round(h_ref[...])
    left, right = turn_rows(rows, cols, wide, me_ref, block, dot(normed, w_k), 1.0, cos_ref, sin_ref)
    values = dot(normed, w_v).astype(BF16).reshape(rows, cols, 2 * wide)
    return left, right, values


def turn_rows(rows, cols, wide, me_ref, block, part, factor, cos_ref, sin_ref):
    scaled = part * (rms_scale(part) * factor)
    scaled = scaled.reshape(rows, cols, 2 * wide)
    first = lax.bitwise_xor(me_ref[0], block) * rows
    left, right = [], []
    for row in range(rows):
        cos, sin = cos_ref[pl.ds(first + row, 1), :], sin_ref[pl.ds(first + row, 1), :]
        a, c = scaled[row, :, :wide], scaled[row, :, wide:]
        left.append((a * cos - c * sin).astype(BF16))
        right.append((a * sin + c * cos).astype(BF16))
    return left, right


def mix_rows(rows, cols, half, q_left, q_right, keys, totals):
    wide = HEADS * half
    width = 2 * wide
    ids0 = lax.broadcasted_iota(jnp.int32, (width, width), 0)
    ids1 = lax.broadcasted_iota(jnp.int32, (width, width), 1)
    gather = jnp.where(ids0 // half == ids1 // half, 1.0, 0.0).astype(BF16)
    num_left, num_right, den = totals
    for two in range(0, len(keys), 2):
        prods = [q_left * k_l[None] + q_right * k_r[None] for k_l, k_r, _ in keys[two : two + 2]]
        score = dot(jnp.concatenate(prods, axis=-1).reshape(rows * cols, width), gather)
        weight = jnp.exp(score).reshape(rows, cols, width)
        for side, (_, _, value) in enumerate(keys[two : two + 2]):
            share = weight[..., side * wide : (side + 1) * wide]
            num_left += share * value[:, :wide].astype(F32)[None]
            num_right += share * value[:, wide:].astype(F32)[None]
            den += share
    return num_left, num_right, den


def all_keys(rows, cols, half, me_ref, blocks, h_refs, w_k, w_v, cos_ref, sin_ref):
    keys = []
    for block, h_ref in zip(blocks, h_refs):
        left, right, values = project_keys(rows, cols, half, me_ref, block, h_ref, w_k, w_v, cos_ref, sin_ref)
        keys += [(left[row], right[row], values[row]) for row in range(rows)]
    return keys


def level(moment):
    cosine = jnp.cos((moment / STEPS + 0.008) / 1.008 * math.pi / 2.0)
    return cosine * cosine


def early_kernel(blocks, rows, cols, me_ref, time_ref, *refs):
    h_refs = refs[: len(blocks)]
    w_qkv_ref, w_ao_ref, cos_ref, sin_ref = refs[len(blocks) : len(blocks) + 4]
    q_ref, left_ref, right_ref, den_ref, w_kv_ref, w_o_ref, coef_ref = refs[len(blocks) + 4 :]
    width = h_refs[0].shape[-1]
    head = width // HEADS
    half = head // 2
    wide = width // 2
    pick = shuffle_matrix(width, functools.partial(full_halves, width, half))
    w_q = dot(w_qkv_ref[1, :, :width], pick).astype(BF16)
    w_k = dot(w_qkv_ref[1, :, width : 2 * width], pick).astype(BF16)
    w_v = dot(w_qkv_ref[1, :, 2 * width :], pick).astype(BF16)
    w_kv_ref[:, :width] = w_k
    w_kv_ref[:, width:] = w_v
    w_o_ref[...] = lax.dot_general(
        pick, w_ao_ref[1], (((0,), (0,)), ((), ())), preferred_element_type=F32
    ).astype(BF16)
    part = dot(rms_round(h_refs[0][...]), w_q)
    left, right = turn_rows(rows, cols, wide, me_ref, 0, part, 1.0 / math.sqrt(head), cos_ref, sin_ref)
    q_left, q_right = jnp.stack(left), jnp.stack(right)
    q_ref[:, :, :wide] = q_left
    q_ref[:, :, wide:] = q_right
    keys = all_keys(rows, cols, half, me_ref, blocks, h_refs, w_k, w_v, cos_ref, sin_ref)
    totals = (jnp.zeros((rows, cols, wide), F32),) * 3
    left_ref[...], right_ref[...], den_ref[...] = mix_rows(rows, cols, half, q_left, q_right, keys, totals)
    moment = jnp.full((1, LANES), time_ref[0].astype(F32))
    now, after = level(moment), level(moment - STRIDE)
    keep = jnp.sqrt(1.0 - after) / jnp.sqrt(1.0 - now)
    coef_ref[0:1, :] = jnp.sqrt(after) - keep * jnp.sqrt(now)
    coef_ref[1:2, :] = keep


def late_kernel(blocks, rows, cols, chan, me_ref, own_ref, *refs):
    h_refs = refs[: len(blocks)]
    (
        q_ref, left_ref, right_ref, den_ref, w_kv_ref, w_o_ref, w_up_ref, w_down_ref, w_out_ref, cos_ref, sin_ref,
        out_ref, tok_scr,
    ) = refs[len(blocks) :]
    width = own_ref.shape[-1]
    half = width // HEADS // 2
    wide = width // 2
    keys = all_keys(
        rows, cols, half, me_ref, blocks, h_refs, w_kv_ref[:, :width], w_kv_ref[:, width:], cos_ref, sin_ref
    )
    left, right, den = mix_rows(
        rows, cols, half, q_ref[:, :, :wide], q_ref[:, :, wide:], keys,
        (left_ref[...], right_ref[...], den_ref[...]),
    )
    mixture = jnp.concatenate([left / den, right / den], axis=-1).astype(BF16)
    hidden = (own_ref[...].astype(F32) + dot(mixture.reshape(rows * cols, width), w_o_ref[...])).astype(BF16)
    hidden = feed_forward(hidden, w_up_ref[1], w_down_ref[1])
    tok_scr[:, :chan] = lax.dot_general(
        rms_round(hidden), w_out_ref[...], (((1,), (1,)), ((), ())), preferred_element_type=F32
    )
    pack_tokens(tok_scr, out_ref, rows, cols, chan)


def finish_kernel(count, dom_ref, anc_ref, coef_ref, *refs):
    states, preds = refs[:count], refs[count : 2 * count]
    new_state_ref, new_pred_ref, state_scr, sems = refs[2 * count :]
    pick = lax.bitwise_xor(anc_ref[dom_ref[0]], dom_ref[0])
    for k in range(count):

        def write(k=k):
            copy_pred = pltpu.make_async_copy(preds[k], new_pred_ref, sems.at[0])
            copy_pred.start()
            state_scr[...] = (
                coef_ref[0:1, 0:1][None] * preds[k][...].astype(F32)
                + coef_ref[1:2, 0:1][None] * states[k][...].astype(F32)
            ).astype(BF16)
            copy_state = pltpu.make_async_copy(state_scr, new_state_ref, sems.at[1])
            copy_state.start()
            copy_pred.wait()
            copy_state.wait()

        if count > 1:
            pl.when(pick == k)(write)
        else:
            write()


VMEM_SPEC = pl.BlockSpec(memory_space=pltpu.VMEM)
SMEM_SPEC = pl.BlockSpec(memory_space=pltpu.SMEM)
HBM_SPEC = pl.BlockSpec(memory_space=pltpu.HBM)


def cube(value, axis, size, bits):
    blocks = [value]
    step = bits // 2
    order = [0]
    while step:
        pairs = [(i, i ^ step) for i in range(size)]
        blocks = blocks + [lax.ppermute(b, axis, pairs) for b in blocks]
        order = order + [o ^ step for o in order]
        step //= 2
    return [blocks[order.index(b)] for b in range(bits)]


def kernel_call(body, name, operands, specs, outs, work, scratch=(), out_specs=None, limit=VMEM_LIMIT):
    single = not isinstance(outs, (list, tuple))
    if out_specs is None:
        out_specs = VMEM_SPEC if single else [VMEM_SPEC] * len(outs)
    return pl.pallas_call(
        body,
        out_shape=outs,
        in_specs=specs,
        out_specs=out_specs,
        scratch_shapes=list(scratch),
        compiler_params=pltpu.CompilerParams(vmem_limit_bytes=limit),
        cost_estimate=pl.CostEstimate(flops=work, bytes_accessed=0, transcendentals=0),
        name=name,
    )(*operands)


def make(mesh):
    n_dom, n_row = mesh.shape["dom"], mesh.shape["row"]

    def per_device(
        state, prev_pred, ancestors, timestep, w_in, w_time, w_qkv, w_attn_out, w_up, w_down, w_out
    ):
        rows, flat = state.shape[1], state.shape[2]
        chan, width = w_out.shape[1], w_out.shape[0]
        cols = flat // chan
        head = width // HEADS
        half = head // 2
        like = jax.ShapeDtypeStruct

        along = rotary_angles(cols, half, LANES)
        sign = np.where(np.arange(LANES) < LANES // 2, -1.0, 1.0)
        tables = [jnp.asarray(np.cos(along), F32), jnp.asarray(np.sin(along) * sign, F32)]
        scratch = [pltpu.SMEM(timestep.shape, jnp.int32)]
        for arr in (state, prev_pred, w_time, w_in):
            scratch.append(pltpu.VMEM(arr.shape, arr.dtype))
        for arr in (w_qkv, w_attn_out, w_up, w_down):
            scratch.append(pltpu.VMEM(arr.shape[1:], arr.dtype))
        for arr in tables:
            scratch.append(pltpu.VMEM(arr.shape, arr.dtype))
        scratch += [
            pltpu.VMEM((2 * rows, flat), F32),
            pltpu.VMEM((2 * rows * cols, LANES), F32),
            pltpu.SemaphoreType.DMA((11,)),
        ]
        hidden = kernel_call(
            functools.partial(row_kernel, rows, cols, chan), "row_block",
            (timestep, state, prev_pred, w_time, w_in, w_qkv, w_attn_out, w_up, w_down, *tables),
            [HBM_SPEC] * 11,
            like((rows * cols, width), BF16),
            5 * WORK_UNIT,
            scratch,
            limit=ROW_VMEM_LIMIT,
        )

        top = n_row // 2
        early = cube(hidden, "row", n_row, top)
        late = cube(lax.ppermute(hidden, "row", [(i, i ^ top) for i in range(n_row)]), "row", n_row, top)
        early_ids, late_ids = list(range(top)), list(range(top, n_row))
        down = rotary_angles(n_row * rows, half, width // 2)
        tables = [jnp.asarray(np.cos(down), F32), jnp.asarray(np.sin(down), F32)]
        me = lax.axis_index("row").astype(jnp.int32)[None]
        piece = like((rows, cols, width // 2), F32)
        *sums, w_kv, w_o, coefs = kernel_call(
            functools.partial(early_kernel, early_ids, rows, cols), "column_early",
            (me, timestep, *early, w_qkv, w_attn_out, *tables),
            [SMEM_SPEC] * 2 + [VMEM_SPEC] * (top + 4),
            [
                like((rows, cols, width), BF16), piece, piece, piece,
                like((width, 2 * width), BF16), like((width, width), BF16), like((2, LANES), F32),
            ],
            3 * WORK_UNIT,
        )
        own_pred = kernel_call(
            functools.partial(late_kernel, late_ids, rows, cols, chan), "column_late",
            (me, hidden, *late, *sums, w_kv, w_o, w_up, w_down, w_out.T, *tables),
            [SMEM_SPEC] + [VMEM_SPEC] * (top + 12),
            like((1, rows, flat), BF16),
            5 * WORK_UNIT,
            [pltpu.VMEM((rows * cols, LANES), F32)],
        )

        my_dom = lax.axis_index("dom").astype(jnp.int32)
        if n_dom & (n_dom - 1) == 0 and n_dom <= 8:
            state_late, _ = lax.optimization_barrier((state, hidden))
            states, preds = [
                [x] + [lax.ppermute(x, "dom", [(i, i ^ k) for i in range(n_dom)]) for k in range(1, n_dom)]
                for x in (state_late, own_pred)
            ]
        else:
            states, preds = [
                [lax.dynamic_index_in_dim(lax.all_gather(x, "dom"), ancestors[my_dom], 0, keepdims=False)]
                for x in (state, own_pred)
            ]
        shape = like(state.shape, BF16)
        return kernel_call(
            functools.partial(finish_kernel, len(preds)), "finish",
            (my_dom[None], ancestors, coefs, *states, *preds),
            [SMEM_SPEC] * 2 + [VMEM_SPEC] * (1 + 2 * len(preds)),
            (shape, shape),
            WORK_UNIT,
            [pltpu.VMEM(state.shape, BF16), pltpu.SemaphoreType.DMA((2,))],
            (HBM_SPEC, HBM_SPEC),
        )

    return per_device


def solution(mesh):
    spread = P(("group", "dom"), "row", None)
    return jax.shard_map(
        make(mesh),
        mesh=mesh,
        in_specs=(spread, spread, P("group"), P("group")) + (P(),) * 7,
        out_specs=(spread, spread),
        check_vma=False,
    )
```

```python
import functools
import math

import jax
import jax.numpy as jnp
import numpy as np
from jax import lax
from jax.experimental import pallas as pl
from jax.experimental.pallas import tpu as pltpu
from jax.sharding import PartitionSpec as P

HEADS = 8
STEPS = 1000
STRIDE = 20
EPS = 1e-06
LANES = 128
VMEM_LIMIT = 32 * 1024 * 1024
ROW_VMEM_LIMIT = 62 * 1024 * 1024
WORK_UNIT = 1 << 30
F32 = jnp.float32
BF16 = jnp.bfloat16


def dot(lhs, rhs):
    return jnp.dot(lhs, rhs, preferred_element_type=F32)


def dot_nt(lhs, rhs):
    return lax.dot_general(lhs, rhs, (((1,), (1,)), ((), ())), preferred_element_type=F32)


def rms_scale(wide):
    return lax.rsqrt(jnp.mean(wide * wide, axis=-1, keepdims=True) + EPS)


def rms_scale_mx(wide):
    n = wide.shape[-1]
    ones = jnp.full((n, n), 1.0 / n, BF16)
    return lax.rsqrt(dot((wide * wide).astype(BF16), ones) + EPS)


def rms_round_mx(values_in):
    wide = values_in.astype(F32)
    return (wide * rms_scale_mx(wide)).astype(BF16)


def rms_round(values_in):
    wide = values_in.astype(F32)
    return (wide * rms_scale(wide)).astype(BF16)


def gelu(values_in):
    return jax.nn.gelu(values_in, approximate=True)


def feed_forward(hidden, w_up, w_down):
    gated = gelu(dot(rms_round_mx(hidden), w_up)).astype(BF16)
    return (hidden.astype(F32) + dot(gated, w_down)).astype(BF16)


def lane_ids(shape):
    return lax.broadcasted_iota(jnp.int32, shape, len(shape) - 1)


def shuffle_matrix(width, source_of):
    rows = lax.broadcasted_iota(jnp.int32, (width, width), 0)
    cols = lax.broadcasted_iota(jnp.int32, (width, width), 1)
    return jnp.where(rows == source_of(cols), 1.0, 0.0).astype(BF16)


def tile_halves(half, j):
    tile, lane = j // LANES, j % LANES
    side, rest = lane // (LANES // 2), lane % (LANES // 2)
    return tile * LANES + (rest // half) * 2 * half + side * half + rest % half


def full_halves(width, half, j):
    side, rest = j // (width // 2), j % (width // 2)
    return (rest // half) * 2 * half + side * half + rest % half


def rotary_angles(count, half, lanes):
    rates = np.exp(-math.log(10000.0) * np.arange(half) / half)
    return np.arange(count)[:, None] * rates[np.arange(lanes) % half][None, :]


def unpack_tokens(flat_ref, out_ref, cols, chan):
    count = flat_ref.shape[0]
    lane = lane_ids((count, LANES))
    for col in range(cols):
        tile, shift = divmod(col * chan, LANES)
        piece = flat_ref[:, tile * LANES : (tile + 1) * LANES]
        if shift + chan > LANES:
            after = flat_ref[:, (tile + 1) * LANES : (tile + 2) * LANES]
            piece = jnp.where(lane >= shift, piece, after)
        if shift:
            piece = pltpu.roll(piece, LANES - shift, 1)
        out_ref[pl.ds(col, count, stride=cols), :] = piece


def pack_tokens(tok_ref, out_ref, rows, cols, chan):
    lane = lane_ids((rows, LANES))
    moved = {}

    def shifted(col):
        if col not in moved:
            piece = tok_ref[pl.ds(col, rows, stride=cols), :]
            shift = (col * chan) % LANES
            moved[col] = pltpu.roll(piece, shift, 1) if shift else piece
        return moved[col]

    for tile in range(cols * chan // LANES):
        first, last = tile * LANES // chan, ((tile + 1) * LANES - 1) // chan
        whole = shifted(last)
        for col in range(last - 1, first - 1, -1):
            whole = jnp.where(lane < (col + 1) * chan - tile * LANES, shifted(col), whole)
        out_ref[0, :, tile * LANES : (tile + 1) * LANES] = whole.astype(BF16)


def level(moment):
    cosine = jnp.cos((moment / STEPS + 0.008) / 1.008 * math.pi / 2.0)
    return cosine * cosine


def time_vector(moment, w_time):
    half = w_time.shape[0] // 2
    rates = jnp.exp(lane_ids((1, half)).astype(F32) * (-math.log(10000.0) / half))
    angles = moment * rates
    embedded = jnp.concatenate([jnp.sin(angles), jnp.cos(angles)], axis=-1)
    first = embedded.astype(BF16)
    rest = embedded - first.astype(F32)
    second = rest.astype(BF16)
    third = (rest - second.astype(F32)).astype(BF16)
    return dot(first, w_time) + dot(second, w_time) + dot(third, w_time)


def row_kernel(
    rows, cols, chan,
    time_ref, anc_ref, state_ref, prev_ref, w_time_ref, w_in_ref, w_qkv_ref, cos_ref, sin_ref, w_ao_ref, w_up_ref, w_down_ref, w_out_ref,
    out_ref, state_scr, coef_ref, pick_ref, next_qkv_ref, next_ao_ref, next_up_ref, next_down_ref, next_out_ref,
    anc_scr, prev_scr, w_time_scr, w_in_scr, w_qkv_scr, cos_scr, sin_scr, w_ao_scr, w_up_scr, w_down_scr,
    flat_scr, tok_scr, sems,
):
    moves = (
        (anc_ref, anc_scr), (state_ref, state_scr), (prev_ref, prev_scr), (w_time_ref, w_time_scr), (w_in_ref, w_in_scr),
        (w_qkv_ref.at[0], w_qkv_scr), (cos_ref, cos_scr), (sin_ref, sin_scr),
        (w_ao_ref.at[0], w_ao_scr), (w_up_ref.at[0], w_up_scr), (w_down_ref.at[0], w_down_scr),
        (w_qkv_ref.at[1], next_qkv_ref), (w_ao_ref.at[1], next_ao_ref), (w_up_ref.at[1], next_up_ref),
        (w_down_ref.at[1], next_down_ref), (w_out_ref, next_out_ref),
    )
    copies = [pltpu.make_async_copy(s, t, sems.at[i]) for i, (s, t) in enumerate(moves)]
    for copy in copies:
        copy.start()
    width = out_ref.shape[-1]
    head = width // HEADS
    half = head // 2
    copies[3].wait()
    offset_vec = time_vector(time_ref[0].astype(F32), w_time_scr[...])
    for c in copies[1:3] + copies[4:11]:
        c.wait()
    flat_scr[:rows, :] = state_scr[0].astype(F32)
    flat_scr[rows:, :] = prev_scr[0].astype(F32)
    unpack_tokens(flat_scr, tok_scr, cols, chan)
    count = rows * cols
    w_in = w_in_scr[...].astype(F32)
    blank = jnp.zeros((LANES - chan, width), F32)
    w_state = jnp.concatenate([w_in[:chan], blank], axis=0).astype(BF16)
    w_prev = jnp.concatenate([w_in[chan:], blank], axis=0).astype(BF16)
    hidden = dot(jnp.concatenate([tok_scr[:count].astype(BF16), tok_scr[count:].astype(BF16)], axis=-1), jnp.concatenate([w_state, w_prev], axis=0))
    hidden = (hidden + offset_vec).astype(BF16)

    pick = shuffle_matrix(width, functools.partial(tile_halves, half))
    w_q = dot(w_qkv_scr[:, :width], pick).astype(BF16)
    w_k = dot(w_qkv_scr[:, width : 2 * width], pick).astype(BF16)
    w_v = w_qkv_scr[:, 2 * width :]
    normed = rms_round_mx(hidden)
    cos, sin = cos_scr[...], sin_scr[...]
    lane = lane_ids((cols, LANES))
    per_tile = LANES // head
    pair = per_tile // 2

    def swap_halves(weight):
        parts = []
        for t in range(width // LANES):
            mid = t * LANES + LANES // 2
            parts += [weight[:, mid : (t + 1) * LANES], weight[:, t * LANES : mid]]
        return jnp.concatenate(parts, axis=-1)

    def spin(part):
        plain = dot(normed, part)
        swapped = dot(normed, swap_halves(part))
        factor = rms_scale_mx(plain)
        tiles = []
        for t in range(width // LANES):
            piece, other, scale = (x[:, t * LANES : (t + 1) * LANES].reshape(rows, cols, LANES) for x in (plain, swapped, factor))
            tiles.append((piece * cos[None] + other * sin[None]) * scale)
        return tiles

    scale = 1.0 / math.sqrt(head)
    queries = [(x * scale).astype(BF16) for x in spin(w_q)]
    keys = [x.astype(BF16) for x in spin(w_k)]
    values = dot(normed, w_v).astype(BF16).reshape(rows, cols, width)

    mixtures = []
    for row in range(rows):
        outs = []
        for t in range(width // LANES):
            q_tile, k_tile = queries[t][row], keys[t][row]
            v_tile = values[row, :, t * LANES : (t + 1) * LANES]
            results = []
            for side in range(2):
                k_parts, v_parts = [], []
                for n in range(side * pair, (side + 1) * pair):
                    own = (lane % (LANES // 2)) // half == n
                    k_parts.append(jnp.where(own, k_tile, jnp.zeros_like(k_tile)))
                    ones = jnp.where((lane // head) == (n + pair) % per_tile, 1.0, 0.0).astype(BF16)
                    v_parts.append(jnp.where(lane // head == n, v_tile, ones))
                score = dot_nt(q_tile, jnp.concatenate(k_parts, axis=0))
                results.append(dot(jnp.exp(score).astype(BF16), jnp.concatenate(v_parts, axis=0)))
            low = lane < LANES // 2
            top = jnp.where(low, results[0], results[1])
            bottom = pltpu.roll(jnp.where(low, results[1], results[0]), LANES // 2, 1)
            outs.append(top / bottom)
        mixtures.append(jnp.concatenate(outs, axis=-1))
    mixture = jnp.concatenate(mixtures, axis=0).astype(BF16)
    hidden = (hidden.astype(F32) + dot(mixture, w_ao_scr[...])).astype(BF16)
    out_ref[...] = feed_forward(hidden, w_up_scr[...], w_down_scr[...])
    moment = jnp.full((1, LANES), time_ref[0].astype(F32))
    now, after = level(moment), level(moment - STRIDE)
    keep = jnp.sqrt(1.0 - after) / jnp.sqrt(1.0 - now)
    coef_ref[0:1, :] = jnp.sqrt(after) - keep * jnp.sqrt(now)
    coef_ref[1:2, :] = keep
    for copy in copies[11:] + copies[:1]:
        copy.wait()
    pick_ref[0] = anc_scr[lax.axis_index("dom")]


def project_keys(rows, cols, half, block, h_ref, w_k, w_v, cos_ref, sin_ref):
    wide = HEADS * half
    normed = rms_round(h_ref[...])
    left, right = turn_rows(rows, cols, wide, block, dot(normed, w_k), 1.0, cos_ref, sin_ref)
    values = dot(normed, w_v).astype(BF16).reshape(rows, cols, 2 * wide)
    return left, right, values


def turn_rows(rows, cols, wide, block, part, factor, cos_ref, sin_ref):
    scaled = part * (rms_scale(part) * factor)
    scaled = scaled.reshape(rows, cols, 2 * wide)
    first = lax.bitwise_xor(lax.axis_index("row"), block) * rows
    left, right = [], []
    for row in range(rows):
        cos, sin = cos_ref[pl.ds(first + row, 1), :], sin_ref[pl.ds(first + row, 1), :]
        a, c = scaled[row, :, :wide], scaled[row, :, wide:]
        left.append((a * cos - c * sin).astype(BF16))
        right.append((a * sin + c * cos).astype(BF16))
    return left, right


def mix_rows(rows, cols, half, q_left, q_right, keys, totals):
    wide = HEADS * half
    width = 2 * wide
    ids0 = lax.broadcasted_iota(jnp.int32, (width, width), 0)
    ids1 = lax.broadcasted_iota(jnp.int32, (width, width), 1)
    gather = jnp.where(ids0 // half == ids1 // half, 1.0, 0.0).astype(BF16)
    num_left, num_right, den = totals
    for two in range(0, len(keys), 2):
        prods = [q_left * k_l[None] + q_right * k_r[None] for k_l, k_r, _ in keys[two : two + 2]]
        score = dot(jnp.concatenate(prods, axis=-1).reshape(rows * cols, width), gather)
        weight = jnp.exp(score).reshape(rows, cols, width)
        for side, (_, _, value) in enumerate(keys[two : two + 2]):
            share = weight[..., side * wide : (side + 1) * wide]
            num_left += share * value[:, :wide].astype(F32)[None]
            num_right += share * value[:, wide:].astype(F32)[None]
            den += share
    return num_left, num_right, den


def all_keys(rows, cols, half, blocks, h_refs, w_k, w_v, cos_ref, sin_ref):
    keys = []
    for block, h_ref in zip(blocks, h_refs):
        left, right, values = project_keys(rows, cols, half, block, h_ref, w_k, w_v, cos_ref, sin_ref)
        keys += [(left[row], right[row], values[row]) for row in range(rows)]
    return keys


def early_kernel(blocks, rows, cols, *refs):
    h_refs = refs[: len(blocks)]
    w_qkv_ref, w_ao_ref, cos_ref, sin_ref = refs[len(blocks) : len(blocks) + 4]
    q_ref, left_ref, right_ref, den_ref, w_kv_ref, w_o_ref = refs[len(blocks) + 4 :]
    width = h_refs[0].shape[-1]
    head = width // HEADS
    half = head // 2
    wide = width // 2
    pick = shuffle_matrix(width, functools.partial(full_halves, width, half))
    w_q = dot(w_qkv_ref[:, :width], pick).astype(BF16)
    w_k = dot(w_qkv_ref[:, width : 2 * width], pick).astype(BF16)
    w_v = dot(w_qkv_ref[:, 2 * width :], pick).astype(BF16)
    w_kv_ref[:, :width] = w_k
    w_kv_ref[:, width:] = w_v
    w_o_ref[...] = lax.dot_general(
        pick, w_ao_ref[...], (((0,), (0,)), ((), ())), preferred_element_type=F32
    ).astype(BF16)
    part = dot(rms_round(h_refs[0][...]), w_q)
    left, right = turn_rows(rows, cols, wide, 0, part, 1.0 / math.sqrt(head), cos_ref, sin_ref)
    q_left, q_right = jnp.stack(left), jnp.stack(right)
    q_ref[:, :, :wide] = q_left
    q_ref[:, :, wide:] = q_right
    keys = all_keys(rows, cols, half, blocks, h_refs, w_k, w_v, cos_ref, sin_ref)
    totals = (jnp.zeros((rows, cols, wide), F32),) * 3
    left_ref[...], right_ref[...], den_ref[...] = mix_rows(rows, cols, half, q_left, q_right, keys, totals)


def late_kernel(blocks, rows, cols, chan, own_ref, *refs):
    h_refs = refs[: len(blocks)]
    (
        q_ref, left_ref, right_ref, den_ref, w_kv_ref, w_o_ref, w_up_ref, w_down_ref, w_out_ref, cos_ref, sin_ref,
        out_ref, tok_scr,
    ) = refs[len(blocks) :]
    width = own_ref.shape[-1]
    half = width // HEADS // 2
    wide = width // 2
    keys = all_keys(
        rows, cols, half, blocks, h_refs, w_kv_ref[:, :width], w_kv_ref[:, width:], cos_ref, sin_ref
    )
    left, right, den = mix_rows(
        rows, cols, half, q_ref[:, :, :wide], q_ref[:, :, wide:], keys,
        (left_ref[...], right_ref[...], den_ref[...]),
    )
    mixture = jnp.concatenate([left / den, right / den], axis=-1).astype(BF16)
    hidden = (own_ref[...].astype(F32) + dot(mixture.reshape(rows * cols, width), w_o_ref[...])).astype(BF16)
    hidden = feed_forward(hidden, w_up_ref[...], w_down_ref[...])
    tok_scr[:, :chan] = lax.dot_general(
        rms_round(hidden), w_out_ref[...], (((1,), (1,)), ((), ())), preferred_element_type=F32
    )
    pack_tokens(tok_scr, out_ref, rows, cols, chan)


def finish_kernel(turn, pick_ref, coef_ref, *refs):
    count = len(turn)
    states, preds = refs[:count], refs[count : 2 * count]
    new_state_ref, new_pred_ref, state_scr, sems = refs[2 * count :]
    pick = lax.bitwise_xor(pick_ref[0], lax.axis_index("dom"))
    for place, k in enumerate(turn):

        def write(k=place):
            copy_pred = pltpu.make_async_copy(preds[k], new_pred_ref, sems.at[0])
            copy_pred.start()
            state_scr[...] = (
                coef_ref[0:1, 0:1][None] * preds[k][...].astype(F32)
                + coef_ref[1:2, 0:1][None] * states[k][...].astype(F32)
            ).astype(BF16)
            copy_state = pltpu.make_async_copy(state_scr, new_state_ref, sems.at[1])
            copy_state.start()
            copy_pred.wait()
            copy_state.wait()

        if count > 1:
            pl.when(pick == k)(write)
        else:
            write()


VMEM_SPEC = pl.BlockSpec(memory_space=pltpu.VMEM)
SMEM_SPEC = pl.BlockSpec(memory_space=pltpu.SMEM)
HBM_SPEC = pl.BlockSpec(memory_space=pltpu.HBM)


def cube(value, axis, size, bits):
    blocks = [value]
    step = bits // 2
    order = [0]
    while step:
        pairs = [(i, i ^ step) for i in range(size)]
        blocks = blocks + [lax.ppermute(b, axis, pairs) for b in blocks]
        order = order + [o ^ step for o in order]
        step //= 2
    return [blocks[order.index(b)] for b in range(bits)]


def kernel_call(body, name, operands, specs, outs, work, scratch=(), out_specs=None, limit=VMEM_LIMIT):
    single = not isinstance(outs, (list, tuple))
    if out_specs is None:
        out_specs = VMEM_SPEC if single else [VMEM_SPEC] * len(outs)
    return pl.pallas_call(
        body,
        out_shape=outs,
        in_specs=specs,
        out_specs=out_specs,
        scratch_shapes=list(scratch),
        compiler_params=pltpu.CompilerParams(vmem_limit_bytes=limit),
        cost_estimate=pl.CostEstimate(flops=work, bytes_accessed=0, transcendentals=0),
        name=name,
    )(*operands)


def make(mesh):
    n_dom, n_row = mesh.shape["dom"], mesh.shape["row"]

    def per_device(
        state, prev_pred, ancestors, timestep, w_in, w_time, w_qkv, w_attn_out, w_up, w_down, w_out
    ):
        rows, flat = state.shape[1], state.shape[2]
        chan, width = w_out.shape[1], w_out.shape[0]
        cols = flat // chan
        head = width // HEADS
        half = head // 2
        like = jax.ShapeDtypeStruct

        along = rotary_angles(cols, half, LANES)
        sign = np.where(np.arange(LANES) < LANES // 2, -1.0, 1.0)
        tables = [jnp.asarray(np.cos(along), F32), jnp.asarray(np.sin(along) * sign, F32)]
        like_of = lambda arr: like(arr.shape, arr.dtype)
        block_of = lambda arr: like(arr.shape[1:], arr.dtype)
        vmem = lambda arr: pltpu.VMEM(arr.shape, arr.dtype)
        block_vmem = lambda arr: pltpu.VMEM(arr.shape[1:], arr.dtype)
        my_dom = lax.axis_index("dom").astype(jnp.int32)
        inputs = (
            timestep, ancestors, state, prev_pred, w_time, w_in, w_qkv, *tables, w_attn_out, w_up, w_down, w_out.T,
        )
        hidden, state_out, coefs, pick, *weights = kernel_call(
            functools.partial(row_kernel, rows, cols, chan), "row_block",
            (timestep, *[pltpu.with_memory_space_constraint(x, pltpu.HBM) for x in inputs[1:]]),
            [SMEM_SPEC] + [HBM_SPEC] * (len(inputs) - 1),
            [
                like((rows * cols, width), BF16), like_of(state), like((2, LANES), F32), like((1,), jnp.int32),
                block_of(w_qkv), block_of(w_attn_out), block_of(w_up), block_of(w_down), like_of(w_out.T),
            ],
            5 * WORK_UNIT,
            [
                pltpu.SMEM(ancestors.shape, jnp.int32),
                vmem(prev_pred), vmem(w_time), vmem(w_in), block_vmem(w_qkv), vmem(tables[0]), vmem(tables[1]),
                block_vmem(w_attn_out), block_vmem(w_up), block_vmem(w_down),
                pltpu.VMEM((2 * rows, flat), F32),
                pltpu.VMEM((2 * rows * cols, LANES), F32),
                pltpu.SemaphoreType.DMA((16,)),
            ],
            [VMEM_SPEC] * 3 + [SMEM_SPEC] + [VMEM_SPEC] * 5,
        )
        w_qkv1, w_ao1, w_up1, w_down1, w_out1 = weights

        top = n_row // 2
        early = cube(hidden, "row", n_row, top)
        across = lax.ppermute(hidden, "row", [(i, i ^ top) for i in range(n_row)])
        early_ids, late_ids = list(range(top)), list(range(top, n_row))
        down = rotary_angles(n_row * rows, half, width // 2)
        tables = [jnp.asarray(np.cos(down), F32), jnp.asarray(np.sin(down), F32)]
        piece = like((rows, cols, width // 2), F32)
        *sums, w_kv, w_o = kernel_call(
            functools.partial(early_kernel, early_ids, rows, cols), "column_early",
            (*early, w_qkv1, w_ao1, *tables),
            [VMEM_SPEC] * (top + 4),
            [
                like((rows, cols, width), BF16), piece, piece, piece,
                like((width, 2 * width), BF16), like((width, width), BF16),
            ],
            3 * WORK_UNIT,
        )
        late = cube(across, "row", n_row, top)
        own_pred = kernel_call(
            functools.partial(late_kernel, late_ids, rows, cols, chan), "column_late",
            (hidden, *late, *sums, w_kv, w_o, w_up1, w_down1, w_out1, *tables),
            [VMEM_SPEC] * (top + 12),
            like((1, rows, flat), BF16),
            5 * WORK_UNIT,
            [pltpu.VMEM((rows * cols, LANES), F32)],
        )

        if n_dom & (n_dom - 1) == 0 and n_dom <= 8:

            def spread(value):
                got = [lax.ppermute(value, "dom", [(i, i ^ k) for i in range(n_dom)]) for k in range(n_dom - 1, 0, -1)]
                return [value] + got[::-1]
        else:

            def spread(value):
                every = lax.all_gather(value, "dom")
                return [lax.dynamic_index_in_dim(every, ancestors[my_dom], 0, keepdims=False)]

        states, preds = spread(state_out), spread(own_pred)
        shape = like(state.shape, BF16)
        turn = list(range(0, len(preds), 2)) + list(range(len(preds) - 1, 0, -2))
        states, preds = [[x[i] for i in turn] for x in (states, preds)]
        return kernel_call(
            functools.partial(finish_kernel, turn), "finish",
            (pick, coefs, *states, *preds),
            [SMEM_SPEC] + [VMEM_SPEC] * (1 + 2 * len(preds)),
            (shape, shape),
            WORK_UNIT,
            [pltpu.VMEM(state.shape, BF16), pltpu.SemaphoreType.DMA((2,))],
            (HBM_SPEC, HBM_SPEC),
        )

    return per_device


def solution(mesh):
    spread = P(("group", "dom"), "row", None)
    return jax.shard_map(
        make(mesh),
        mesh=mesh,
        in_specs=(spread, spread, P("group"), P("group")) + (P(),) * 7,
        out_specs=(spread, spread),
        check_vma=False,
    )
```

```python
import functools
import math

import jax
import jax.numpy as jnp
import numpy as np
from jax import lax
from jax.experimental import pallas as pl
from jax.experimental.pallas import tpu as pltpu
from jax.sharding import PartitionSpec as P

HEADS = 8
STEPS = 1000
STRIDE = 20
EPS = 1e-06
LANES = 128
VMEM_LIMIT = 32 * 1024 * 1024
ROW_VMEM_LIMIT = 62 * 1024 * 1024
WORK_UNIT = 1 << 30
FIRST_WORK = 3
MORE_WORK = 3
F32 = jnp.float32
BF16 = jnp.bfloat16


def dot(lhs, rhs):
    return jnp.dot(lhs, rhs, preferred_element_type=F32)


def dot_nt(lhs, rhs):
    return lax.dot_general(lhs, rhs, (((1,), (1,)), ((), ())), preferred_element_type=F32)


def rms_scale(wide):
    return lax.rsqrt(jnp.mean(wide * wide, axis=-1, keepdims=True) + EPS)


def rms_scale_mx(wide):
    n = wide.shape[-1]
    ones = jnp.full((n, n), 1.0 / n, BF16)
    return lax.rsqrt(dot((wide * wide).astype(BF16), ones) + EPS)


def rms_round_mx(values_in):
    wide = values_in.astype(F32)
    return (wide * rms_scale_mx(wide)).astype(BF16)


def rms_round(values_in):
    wide = values_in.astype(F32)
    return (wide * rms_scale(wide)).astype(BF16)


def gelu(values_in):
    return jax.nn.gelu(values_in, approximate=True)


def feed_forward(hidden, w_up, w_down):
    gated = gelu(dot(rms_round_mx(hidden), w_up)).astype(BF16)
    return (hidden.astype(F32) + dot(gated, w_down)).astype(BF16)


def lane_ids(shape):
    return lax.broadcasted_iota(jnp.int32, shape, len(shape) - 1)


def shuffle_matrix(width, source_of):
    rows = lax.broadcasted_iota(jnp.int32, (width, width), 0)
    cols = lax.broadcasted_iota(jnp.int32, (width, width), 1)
    return jnp.where(rows == source_of(cols), 1.0, 0.0).astype(BF16)


def tile_halves(half, j):
    tile, lane = j // LANES, j % LANES
    side, rest = lane // (LANES // 2), lane % (LANES // 2)
    return tile * LANES + (rest // half) * 2 * half + side * half + rest % half


def full_halves(width, half, j):
    side, rest = j // (width // 2), j % (width // 2)
    return (rest // half) * 2 * half + side * half + rest % half


def rotary_angles(count, half, lanes):
    rates = np.exp(-math.log(10000.0) * np.arange(half) / half)
    return np.arange(count)[:, None] * rates[np.arange(lanes) % half][None, :]


def unpack_tokens(flat_ref, out_ref, cols, chan):
    count = flat_ref.shape[0]
    lane = lane_ids((count, LANES))
    for col in range(cols):
        tile, shift = divmod(col * chan, LANES)
        piece = flat_ref[:, tile * LANES : (tile + 1) * LANES]
        if shift + chan > LANES:
            after = flat_ref[:, (tile + 1) * LANES : (tile + 2) * LANES]
            piece = jnp.where(lane >= shift, piece, after)
        if shift:
            piece = pltpu.roll(piece, LANES - shift, 1)
        out_ref[pl.ds(col, count, stride=cols), :] = piece


def pack_tokens(tok_ref, out_ref, rows, cols, chan):
    lane = lane_ids((rows, LANES))
    moved = {}

    def shifted(col):
        if col not in moved:
            piece = tok_ref[pl.ds(col, rows, stride=cols), :]
            shift = (col * chan) % LANES
            moved[col] = pltpu.roll(piece, shift, 1) if shift else piece
        return moved[col]

    for tile in range(cols * chan // LANES):
        first, last = tile * LANES // chan, ((tile + 1) * LANES - 1) // chan
        whole = shifted(last)
        for col in range(last - 1, first - 1, -1):
            whole = jnp.where(lane < (col + 1) * chan - tile * LANES, shifted(col), whole)
        out_ref[0, :, tile * LANES : (tile + 1) * LANES] = whole.astype(BF16)


def level(moment):
    cosine = jnp.cos((moment / STEPS + 0.008) / 1.008 * math.pi / 2.0)
    return cosine * cosine


def time_vector(moment, w_time):
    half = w_time.shape[0] // 2
    rates = jnp.exp(lane_ids((1, half)).astype(F32) * (-math.log(10000.0) / half))
    angles = moment * rates
    embedded = jnp.concatenate([jnp.sin(angles), jnp.cos(angles)], axis=-1)
    first = embedded.astype(BF16)
    rest = embedded - first.astype(F32)
    second = rest.astype(BF16)
    third = (rest - second.astype(F32)).astype(BF16)
    return dot(first, w_time) + dot(second, w_time) + dot(third, w_time)


def row_kernel(
    rows, cols, chan,
    time_ref, anc_ref, state_ref, prev_ref, w_time_ref, w_in_ref, w_qkv_ref, cos_ref, sin_ref, w_ao_ref, w_up_ref, w_down_ref, w_out_ref,
    out_ref, state_scr, coef_ref, pick_ref, next_qkv_ref, next_ao_ref, next_up_ref, next_down_ref, next_out_ref,
    anc_scr, prev_scr, w_time_scr, w_in_scr, w_qkv_scr, cos_scr, sin_scr, w_ao_scr, w_up_scr, w_down_scr,
    flat_scr, tok_scr, sems,
):
    moves = (
        (anc_ref, anc_scr), (state_ref, state_scr), (prev_ref, prev_scr), (w_time_ref, w_time_scr), (w_in_ref, w_in_scr),
        (w_qkv_ref.at[0], w_qkv_scr), (cos_ref, cos_scr), (sin_ref, sin_scr),
        (w_ao_ref.at[0], w_ao_scr), (w_up_ref.at[0], w_up_scr), (w_down_ref.at[0], w_down_scr),
        (w_qkv_ref.at[1], next_qkv_ref), (w_ao_ref.at[1], next_ao_ref), (w_up_ref.at[1], next_up_ref),
        (w_down_ref.at[1], next_down_ref), (w_out_ref, next_out_ref),
    )
    copies = [pltpu.make_async_copy(s, t, sems.at[i]) for i, (s, t) in enumerate(moves)]
    for copy in copies:
        copy.start()
    width = out_ref.shape[-1]
    head = width // HEADS
    half = head // 2
    copies[3].wait()
    offset_vec = time_vector(time_ref[0].astype(F32), w_time_scr[...])
    for c in copies[1:3] + copies[4:11]:
        c.wait()
    flat_scr[:rows, :] = state_scr[0].astype(F32)
    flat_scr[rows:, :] = prev_scr[0].astype(F32)
    unpack_tokens(flat_scr, tok_scr, cols, chan)
    count = rows * cols
    w_in = w_in_scr[...].astype(F32)
    blank = jnp.zeros((LANES - chan, width), F32)
    w_state = jnp.concatenate([w_in[:chan], blank], axis=0).astype(BF16)
    w_prev = jnp.concatenate([w_in[chan:], blank], axis=0).astype(BF16)
    hidden = dot(jnp.concatenate([tok_scr[:count].astype(BF16), tok_scr[count:].astype(BF16)], axis=-1), jnp.concatenate([w_state, w_prev], axis=0))
    hidden = (hidden + offset_vec).astype(BF16)

    pick = shuffle_matrix(width, functools.partial(tile_halves, half))
    w_q = dot(w_qkv_scr[:, :width], pick).astype(BF16)
    w_k = dot(w_qkv_scr[:, width : 2 * width], pick).astype(BF16)
    w_v = w_qkv_scr[:, 2 * width :]
    normed = rms_round_mx(hidden)
    cos, sin = cos_scr[...], sin_scr[...]
    lane = lane_ids((cols, LANES))
    per_tile = LANES // head
    pair = per_tile // 2

    def swap_halves(weight):
        parts = []
        for t in range(width // LANES):
            mid = t * LANES + LANES // 2
            parts += [weight[:, mid : (t + 1) * LANES], weight[:, t * LANES : mid]]
        return jnp.concatenate(parts, axis=-1)

    def spin(part):
        plain = dot(normed, part)
        swapped = dot(normed, swap_halves(part))
        factor = rms_scale_mx(plain)
        tiles = []
        for t in range(width // LANES):
            piece, other, scale = (x[:, t * LANES : (t + 1) * LANES].reshape(rows, cols, LANES) for x in (plain, swapped, factor))
            tiles.append((piece * cos[None] + other * sin[None]) * scale)
        return tiles

    scale = 1.0 / math.sqrt(head)
    queries = [(x * scale).astype(BF16) for x in spin(w_q)]
    keys = [x.astype(BF16) for x in spin(w_k)]
    values = dot(normed, w_v).astype(BF16).reshape(rows, cols, width)

    mixtures = []
    for row in range(rows):
        outs = []
        for t in range(width // LANES):
            q_tile, k_tile = queries[t][row], keys[t][row]
            v_tile = values[row, :, t * LANES : (t + 1) * LANES]
            results = []
            for side in range(2):
                k_parts, v_parts = [], []
                for n in range(side * pair, (side + 1) * pair):
                    own = (lane % (LANES // 2)) // half == n
                    k_parts.append(jnp.where(own, k_tile, jnp.zeros_like(k_tile)))
                    ones = jnp.where((lane // head) == (n + pair) % per_tile, 1.0, 0.0).astype(BF16)
                    v_parts.append(jnp.where(lane // head == n, v_tile, ones))
                score = dot_nt(q_tile, jnp.concatenate(k_parts, axis=0))
                results.append(dot(jnp.exp(score).astype(BF16), jnp.concatenate(v_parts, axis=0)))
            low = lane < LANES // 2
            top = jnp.where(low, results[0], results[1])
            bottom = pltpu.roll(jnp.where(low, results[1], results[0]), LANES // 2, 1)
            outs.append(top / bottom)
        mixtures.append(jnp.concatenate(outs, axis=-1))
    mixture = jnp.concatenate(mixtures, axis=0).astype(BF16)
    hidden = (hidden.astype(F32) + dot(mixture, w_ao_scr[...])).astype(BF16)
    out_ref[...] = feed_forward(hidden, w_up_scr[...], w_down_scr[...])
    moment = jnp.full((1, LANES), time_ref[0].astype(F32))
    now, after = level(moment), level(moment - STRIDE)
    keep = jnp.sqrt(1.0 - after) / jnp.sqrt(1.0 - now)
    coef_ref[0:1, :] = jnp.sqrt(after) - keep * jnp.sqrt(now)
    coef_ref[1:2, :] = keep
    for copy in copies[11:] + copies[:1]:
        copy.wait()
    pick_ref[0] = anc_scr[lax.axis_index("dom")]


def project_keys(rows, cols, half, block, h_ref, w_k, w_v, cos_ref, sin_ref):
    wide = HEADS * half
    normed = rms_round(h_ref[...])
    left, right = turn_rows(rows, cols, wide, block, dot(normed, w_k), 1.0, cos_ref, sin_ref)
    values = dot(normed, w_v).astype(BF16).reshape(rows, cols, 2 * wide)
    return left, right, values


def turn_rows(rows, cols, wide, block, part, factor, cos_ref, sin_ref):
    scaled = part * (rms_scale(part) * factor)
    scaled = scaled.reshape(rows, cols, 2 * wide)
    first = lax.bitwise_xor(lax.axis_index("row"), block) * rows
    left, right = [], []
    for row in range(rows):
        cos, sin = cos_ref[pl.ds(first + row, 1), :], sin_ref[pl.ds(first + row, 1), :]
        a, c = scaled[row, :, :wide], scaled[row, :, wide:]
        left.append((a * cos - c * sin).astype(BF16))
        right.append((a * sin + c * cos).astype(BF16))
    return left, right


def mix_rows(rows, cols, half, q_left, q_right, keys, totals):
    wide = HEADS * half
    width = 2 * wide
    ids0 = lax.broadcasted_iota(jnp.int32, (width, width), 0)
    ids1 = lax.broadcasted_iota(jnp.int32, (width, width), 1)
    gather = jnp.where(ids0 // half == ids1 // half, 1.0, 0.0).astype(BF16)
    num_left, num_right, den = totals
    for two in range(0, len(keys), 2):
        prods = [q_left * k_l[None] + q_right * k_r[None] for k_l, k_r, _ in keys[two : two + 2]]
        score = dot(jnp.concatenate(prods, axis=-1).reshape(rows * cols, width), gather)
        weight = jnp.exp(score).reshape(rows, cols, width)
        for side, (_, _, value) in enumerate(keys[two : two + 2]):
            share = weight[..., side * wide : (side + 1) * wide]
            num_left += share * value[:, :wide].astype(F32)[None]
            num_right += share * value[:, wide:].astype(F32)[None]
            den += share
    return num_left, num_right, den


def all_keys(rows, cols, half, blocks, h_refs, w_k, w_v, cos_ref, sin_ref):
    keys = []
    for block, h_ref in zip(blocks, h_refs):
        left, right, values = project_keys(rows, cols, half, block, h_ref, w_k, w_v, cos_ref, sin_ref)
        keys += [(left[row], right[row], values[row]) for row in range(rows)]
    return keys


def first_kernel(rows, cols, own_ref, *refs):
    w_qkv_ref, w_ao_ref, cos_ref, sin_ref, q_ref, left_ref, right_ref, den_ref, w_kv_ref, w_o_ref = refs
    width = own_ref.shape[-1]
    head = width // HEADS
    half = head // 2
    wide = width // 2
    pick = shuffle_matrix(width, functools.partial(full_halves, width, half))
    w_q = dot(w_qkv_ref[:, :width], pick).astype(BF16)
    w_k = dot(w_qkv_ref[:, width : 2 * width], pick).astype(BF16)
    w_v = dot(w_qkv_ref[:, 2 * width :], pick).astype(BF16)
    w_kv_ref[:, :width] = w_k
    w_kv_ref[:, width:] = w_v
    w_o_ref[...] = lax.dot_general(
        pick, w_ao_ref[...], (((0,), (0,)), ((), ())), preferred_element_type=F32
    ).astype(BF16)
    part = dot(rms_round(own_ref[...]), w_q)
    left, right = turn_rows(rows, cols, wide, 0, part, 1.0 / math.sqrt(head), cos_ref, sin_ref)
    q_left, q_right = jnp.stack(left), jnp.stack(right)
    q_ref[:, :, :wide] = q_left
    q_ref[:, :, wide:] = q_right
    keys = all_keys(rows, cols, half, [0], [own_ref], w_k, w_v, cos_ref, sin_ref)
    totals = (jnp.zeros((rows, cols, wide), F32),) * 3
    left_ref[...], right_ref[...], den_ref[...] = mix_rows(rows, cols, half, q_left, q_right, keys, totals)


def more_kernel(blocks, rows, cols, *refs):
    h_refs = refs[: len(blocks)]
    q_ref, left_in, right_in, den_in, w_kv_ref, cos_ref, sin_ref, left_ref, right_ref, den_ref = refs[len(blocks) :]
    width = q_ref.shape[-1]
    half = width // HEADS // 2
    wide = width // 2
    keys = all_keys(rows, cols, half, blocks, h_refs, w_kv_ref[:, :width], w_kv_ref[:, width:], cos_ref, sin_ref)
    totals = (left_in[...], right_in[...], den_in[...])
    left_ref[...], right_ref[...], den_ref[...] = mix_rows(
        rows, cols, half, q_ref[:, :, :wide], q_ref[:, :, wide:], keys, totals
    )


def late_kernel(blocks, rows, cols, chan, own_ref, *refs):
    h_refs = refs[: len(blocks)]
    (
        q_ref, left_ref, right_ref, den_ref, w_kv_ref, w_o_ref, w_up_ref, w_down_ref, w_out_ref, cos_ref, sin_ref,
        out_ref, tok_scr,
    ) = refs[len(blocks) :]
    width = own_ref.shape[-1]
    half = width // HEADS // 2
    wide = width // 2
    keys = all_keys(
        rows, cols, half, blocks, h_refs, w_kv_ref[:, :width], w_kv_ref[:, width:], cos_ref, sin_ref
    )
    left, right, den = mix_rows(
        rows, cols, half, q_ref[:, :, :wide], q_ref[:, :, wide:], keys,
        (left_ref[...], right_ref[...], den_ref[...]),
    )
    mixture = jnp.concatenate([left / den, right / den], axis=-1).astype(BF16)
    hidden = (own_ref[...].astype(F32) + dot(mixture.reshape(rows * cols, width), w_o_ref[...])).astype(BF16)
    hidden = feed_forward(hidden, w_up_ref[...], w_down_ref[...])
    tok_scr[:, :chan] = lax.dot_general(
        rms_round(hidden), w_out_ref[...], (((1,), (1,)), ((), ())), preferred_element_type=F32
    )
    pack_tokens(tok_scr, out_ref, rows, cols, chan)


def finish_kernel(turn, pick_ref, coef_ref, *refs):
    count = len(turn)
    states, preds = refs[:count], refs[count : 2 * count]
    new_state_ref, new_pred_ref, state_scr, sems = refs[2 * count :]
    pick = lax.bitwise_xor(pick_ref[0], lax.axis_index("dom"))
    for place, k in enumerate(turn):

        def write(k=place):
            copy_pred = pltpu.make_async_copy(preds[k], new_pred_ref, sems.at[0])
            copy_pred.start()
            state_scr[...] = (
                coef_ref[0:1, 0:1][None] * preds[k][...].astype(F32)
                + coef_ref[1:2, 0:1][None] * states[k][...].astype(F32)
            ).astype(BF16)
            copy_state = pltpu.make_async_copy(state_scr, new_state_ref, sems.at[1])
            copy_state.start()
            copy_pred.wait()
            copy_state.wait()

        if count > 1:
            pl.when(pick == k)(write)
        else:
            write()


VMEM_SPEC = pl.BlockSpec(memory_space=pltpu.VMEM)
SMEM_SPEC = pl.BlockSpec(memory_space=pltpu.SMEM)
HBM_SPEC = pl.BlockSpec(memory_space=pltpu.HBM)


def cube(value, axis, size, bits):
    blocks = [value]
    step = bits // 2
    order = [0]
    while step:
        pairs = [(i, i ^ step) for i in range(size)]
        blocks = blocks + [lax.ppermute(b, axis, pairs) for b in blocks]
        order = order + [o ^ step for o in order]
        step //= 2
    return [blocks[order.index(b)] for b in range(bits)]


def kernel_call(body, name, operands, specs, outs, work, scratch=(), out_specs=None, limit=VMEM_LIMIT):
    single = not isinstance(outs, (list, tuple))
    if out_specs is None:
        out_specs = VMEM_SPEC if single else [VMEM_SPEC] * len(outs)
    return pl.pallas_call(
        body,
        out_shape=outs,
        in_specs=specs,
        out_specs=out_specs,
        scratch_shapes=list(scratch),
        compiler_params=pltpu.CompilerParams(vmem_limit_bytes=limit),
        cost_estimate=pl.CostEstimate(flops=work, bytes_accessed=0, transcendentals=0),
        name=name,
    )(*operands)


def make(mesh):
    n_dom, n_row = mesh.shape["dom"], mesh.shape["row"]

    def per_device(
        state, prev_pred, ancestors, timestep, w_in, w_time, w_qkv, w_attn_out, w_up, w_down, w_out
    ):
        rows, flat = state.shape[1], state.shape[2]
        chan, width = w_out.shape[1], w_out.shape[0]
        cols = flat // chan
        head = width // HEADS
        half = head // 2
        like = jax.ShapeDtypeStruct

        along = rotary_angles(cols, half, LANES)
        sign = np.where(np.arange(LANES) < LANES // 2, -1.0, 1.0)
        tables = [jnp.asarray(np.cos(along), F32), jnp.asarray(np.sin(along) * sign, F32)]
        like_of = lambda arr: like(arr.shape, arr.dtype)
        block_of = lambda arr: like(arr.shape[1:], arr.dtype)
        vmem = lambda arr: pltpu.VMEM(arr.shape, arr.dtype)
        block_vmem = lambda arr: pltpu.VMEM(arr.shape[1:], arr.dtype)
        my_dom = lax.axis_index("dom").astype(jnp.int32)
        inputs = (
            timestep, ancestors, state, prev_pred, w_time, w_in, w_qkv, *tables, w_attn_out, w_up, w_down, w_out.T,
        )
        hidden, state_out, coefs, pick, *weights = kernel_call(
            functools.partial(row_kernel, rows, cols, chan), "row_block",
            (timestep, *[pltpu.with_memory_space_constraint(x, pltpu.HBM) for x in inputs[1:]]),
            [SMEM_SPEC] + [HBM_SPEC] * (len(inputs) - 1),
            [
                like((rows * cols, width), BF16), like_of(state), like((2, LANES), F32), like((1,), jnp.int32),
                block_of(w_qkv), block_of(w_attn_out), block_of(w_up), block_of(w_down), like_of(w_out.T),
            ],
            5 * WORK_UNIT,
            [
                pltpu.SMEM(ancestors.shape, jnp.int32),
                vmem(prev_pred), vmem(w_time), vmem(w_in), block_vmem(w_qkv), vmem(tables[0]), vmem(tables[1]),
                block_vmem(w_attn_out), block_vmem(w_up), block_vmem(w_down),
                pltpu.VMEM((2 * rows, flat), F32),
                pltpu.VMEM((2 * rows * cols, LANES), F32),
                pltpu.SemaphoreType.DMA((16,)),
            ],
            [VMEM_SPEC] * 3 + [SMEM_SPEC] + [VMEM_SPEC] * 5,
        )
        w_qkv1, w_ao1, w_up1, w_down1, w_out1 = weights

        top = n_row // 2
        early = cube(hidden, "row", n_row, top)
        across = lax.ppermute(hidden, "row", [(i, i ^ top) for i in range(n_row)])
        down = rotary_angles(n_row * rows, half, width // 2)
        tables = [jnp.asarray(np.cos(down), F32), jnp.asarray(np.sin(down), F32)]
        piece = like((rows, cols, width // 2), F32)
        query, *sums, w_kv, w_o = kernel_call(
            functools.partial(first_kernel, rows, cols), "column_first",
            (hidden, w_qkv1, w_ao1, *tables),
            [VMEM_SPEC] * 5,
            [
                like((rows, cols, width), BF16), piece, piece, piece,
                like((width, 2 * width), BF16), like((width, width), BF16),
            ],
            FIRST_WORK * WORK_UNIT,
        )
        middle = [*early[1:], across]
        sums = kernel_call(
            functools.partial(more_kernel, list(range(1, top + 1)), rows, cols), "column_early",
            (*middle, query, *sums, w_kv, *tables),
            [VMEM_SPEC] * (len(middle) + 7),
            [piece, piece, piece],
            MORE_WORK * WORK_UNIT,
        )
        late = cube(across, "row", n_row, top)[1:]
        late_ids = list(range(top + 1, n_row))
        own_pred = kernel_call(
            functools.partial(late_kernel, late_ids, rows, cols, chan), "column_late",
            (hidden, *late, query, *sums, w_kv, w_o, w_up1, w_down1, w_out1, *tables),
            [VMEM_SPEC] * (len(late) + 12),
            like((1, rows, flat), BF16),
            5 * WORK_UNIT,
            [pltpu.VMEM((rows * cols, LANES), F32)],
        )

        if n_dom & (n_dom - 1) == 0 and n_dom <= 8:

            def spread(value):
                got = [lax.ppermute(value, "dom", [(i, i ^ k) for i in range(n_dom)]) for k in range(n_dom - 1, 0, -1)]
                return [value] + got[::-1]
        else:

            def spread(value):
                every = lax.all_gather(value, "dom")
                return [lax.dynamic_index_in_dim(every, ancestors[my_dom], 0, keepdims=False)]

        states, preds = spread(state_out), spread(own_pred)
        shape = like(state.shape, BF16)
        turn = list(range(0, len(preds), 2)) + list(range(len(preds) - 1, 0, -2))
        states, preds = [[x[i] for i in turn] for x in (states, preds)]
        return kernel_call(
            functools.partial(finish_kernel, turn), "finish",
            (pick, coefs, *states, *preds),
            [SMEM_SPEC] + [VMEM_SPEC] * (1 + 2 * len(preds)),
            (shape, shape),
            WORK_UNIT,
            [pltpu.VMEM(state.shape, BF16), pltpu.SemaphoreType.DMA((2,))],
            (HBM_SPEC, HBM_SPEC),
        )

    return per_device


def solution(mesh):
    spread = P(("group", "dom"), "row", None)
    return jax.shard_map(
        make(mesh),
        mesh=mesh,
        in_specs=(spread, spread, P("group"), P("group")) + (P(),) * 7,
        out_specs=(spread, spread),
        check_vma=False,
    )
```

```python
import functools
import math

import jax
import jax.numpy as jnp
import numpy as np
from jax import lax
from jax.experimental import pallas as pl
from jax.experimental.pallas import tpu as pltpu
from jax.sharding import PartitionSpec as P

HEADS = 8
STEPS = 1000
STRIDE = 20
EPS = 1e-06
LANES = 128
VMEM_LIMIT = 32 * 1024 * 1024
ROW_VMEM_LIMIT = 62 * 1024 * 1024
WORK_UNIT = 1 << 30
FIRST_WORK = 3
MORE_WORK = 3
F32 = jnp.float32
BF16 = jnp.bfloat16


def dot(lhs, rhs):
    return jnp.dot(lhs, rhs, preferred_element_type=F32)


def dot_nt(lhs, rhs):
    return lax.dot_general(lhs, rhs, (((1,), (1,)), ((), ())), preferred_element_type=F32)


def rms_scale(wide):
    return lax.rsqrt(jnp.mean(wide * wide, axis=-1, keepdims=True) + EPS)


def rms_scale_mx(wide):
    n = wide.shape[-1]
    ones = jnp.full((n, n), 1.0 / n, BF16)
    return lax.rsqrt(dot((wide * wide).astype(BF16), ones) + EPS)


def rms_round_mx(values_in):
    wide = values_in.astype(F32)
    return (wide * rms_scale_mx(wide)).astype(BF16)


def rms_round(values_in):
    wide = values_in.astype(F32)
    return (wide * rms_scale(wide)).astype(BF16)


def gelu(values_in):
    return jax.nn.gelu(values_in, approximate=True)


def feed_forward(hidden, w_up, w_down):
    gated = gelu(dot(rms_round_mx(hidden), w_up)).astype(BF16)
    return (hidden.astype(F32) + dot(gated, w_down)).astype(BF16)


def lane_ids(shape):
    return lax.broadcasted_iota(jnp.int32, shape, len(shape) - 1)


def shuffle_matrix(width, source_of):
    rows = lax.broadcasted_iota(jnp.int32, (width, width), 0)
    cols = lax.broadcasted_iota(jnp.int32, (width, width), 1)
    return jnp.where(rows == source_of(cols), 1.0, 0.0).astype(BF16)


def tile_halves(half, j):
    tile, lane = j // LANES, j % LANES
    side, rest = lane // (LANES // 2), lane % (LANES // 2)
    return tile * LANES + (rest // half) * 2 * half + side * half + rest % half


def full_halves(width, half, j):
    side, rest = j // (width // 2), j % (width // 2)
    return (rest // half) * 2 * half + side * half + rest % half


def rotary_angles(count, half, lanes):
    rates = np.exp(-math.log(10000.0) * np.arange(half) / half)
    return np.arange(count)[:, None] * rates[np.arange(lanes) % half][None, :]


def unpack_tokens(flat_ref, out_ref, cols, chan):
    count = flat_ref.shape[0]
    lane = lane_ids((count, LANES))
    for col in range(cols):
        tile, shift = divmod(col * chan, LANES)
        piece = flat_ref[:, tile * LANES : (tile + 1) * LANES]
        if shift + chan > LANES:
            after = flat_ref[:, (tile + 1) * LANES : (tile + 2) * LANES]
            piece = jnp.where(lane >= shift, piece, after)
        if shift:
            piece = pltpu.roll(piece, LANES - shift, 1)
        out_ref[pl.ds(col, count, stride=cols), :] = piece


def pack_tokens(tok_ref, out_ref, rows, cols, chan):
    lane = lane_ids((rows, LANES))
    moved = {}

    def shifted(col):
        if col not in moved:
            piece = tok_ref[pl.ds(col, rows, stride=cols), :]
            shift = (col * chan) % LANES
            moved[col] = pltpu.roll(piece, shift, 1) if shift else piece
        return moved[col]

    for tile in range(cols * chan // LANES):
        first, last = tile * LANES // chan, ((tile + 1) * LANES - 1) // chan
        whole = shifted(last)
        for col in range(last - 1, first - 1, -1):
            whole = jnp.where(lane < (col + 1) * chan - tile * LANES, shifted(col), whole)
        out_ref[0, :, tile * LANES : (tile + 1) * LANES] = whole.astype(BF16)


def level(moment):
    cosine = jnp.cos((moment / STEPS + 0.008) / 1.008 * math.pi / 2.0)
    return cosine * cosine


def time_vector(moment, w_time):
    half = w_time.shape[0] // 2
    rates = jnp.exp(lane_ids((1, half)).astype(F32) * (-math.log(10000.0) / half))
    angles = moment * rates
    embedded = jnp.concatenate([jnp.sin(angles), jnp.cos(angles)], axis=-1)
    first = embedded.astype(BF16)
    rest = embedded - first.astype(F32)
    second = rest.astype(BF16)
    third = (rest - second.astype(F32)).astype(BF16)
    return dot(first, w_time) + dot(second, w_time) + dot(third, w_time)


def row_kernel(
    rows, cols, chan, small,
    time_ref, anc_ref, state_ref, prev_ref, w_time_ref, w_in_ref, w_qkv_ref, cos_ref, sin_ref, w_ao_ref, w_up_ref, w_down_ref, w_out_ref,
    out_ref, state_scr, coef_ref, pick_ref, need_ref, next_qkv_ref, next_ao_ref, next_up_ref, next_down_ref, next_out_ref,
    anc_scr, prev_scr, w_time_scr, w_in_scr, w_qkv_scr, cos_scr, sin_scr, w_ao_scr, w_up_scr, w_down_scr,
    flat_scr, tok_scr, sems,
):
    moves = (
        (anc_ref, anc_scr), (state_ref, state_scr), (prev_ref, prev_scr), (w_time_ref, w_time_scr), (w_in_ref, w_in_scr),
        (w_qkv_ref.at[0], w_qkv_scr), (cos_ref, cos_scr), (sin_ref, sin_scr),
        (w_ao_ref.at[0], w_ao_scr), (w_up_ref.at[0], w_up_scr), (w_down_ref.at[0], w_down_scr),
        (w_qkv_ref.at[1], next_qkv_ref), (w_ao_ref.at[1], next_ao_ref), (w_up_ref.at[1], next_up_ref),
        (w_down_ref.at[1], next_down_ref), (w_out_ref, next_out_ref),
    )
    copies = [pltpu.make_async_copy(s, t, sems.at[i]) for i, (s, t) in enumerate(moves)]
    for copy in copies:
        copy.start()
    width = out_ref.shape[-1]
    head = width // HEADS
    half = head // 2
    copies[3].wait()
    offset_vec = time_vector(time_ref[0].astype(F32), w_time_scr[...])
    for c in copies[1:3] + copies[4:11]:
        c.wait()
    flat_scr[:rows, :] = state_scr[0].astype(F32)
    flat_scr[rows:, :] = prev_scr[0].astype(F32)
    unpack_tokens(flat_scr, tok_scr, cols, chan)
    count = rows * cols
    w_in = w_in_scr[...].astype(F32)
    blank = jnp.zeros((LANES - chan, width), F32)
    w_state = jnp.concatenate([w_in[:chan], blank], axis=0).astype(BF16)
    w_prev = jnp.concatenate([w_in[chan:], blank], axis=0).astype(BF16)
    hidden = dot(jnp.concatenate([tok_scr[:count].astype(BF16), tok_scr[count:].astype(BF16)], axis=-1), jnp.concatenate([w_state, w_prev], axis=0))
    hidden = (hidden + offset_vec).astype(BF16)

    pick = shuffle_matrix(width, functools.partial(tile_halves, half))
    w_q = dot(w_qkv_scr[:, :width], pick).astype(BF16)
    w_k = dot(w_qkv_scr[:, width : 2 * width], pick).astype(BF16)
    w_v = w_qkv_scr[:, 2 * width :]
    normed = rms_round_mx(hidden)
    cos, sin = cos_scr[...], sin_scr[...]
    lane = lane_ids((cols, LANES))
    per_tile = LANES // head
    pair = per_tile // 2

    def swap_halves(weight):
        parts = []
        for t in range(width // LANES):
            mid = t * LANES + LANES // 2
            parts += [weight[:, mid : (t + 1) * LANES], weight[:, t * LANES : mid]]
        return jnp.concatenate(parts, axis=-1)

    def spin(part):
        plain = dot(normed, part)
        swapped = dot(normed, swap_halves(part))
        factor = rms_scale_mx(plain)
        tiles = []
        for t in range(width // LANES):
            piece, other, scale = (x[:, t * LANES : (t + 1) * LANES].reshape(rows, cols, LANES) for x in (plain, swapped, factor))
            tiles.append((piece * cos[None] + other * sin[None]) * scale)
        return tiles

    scale = 1.0 / math.sqrt(head)
    queries = [(x * scale).astype(BF16) for x in spin(w_q)]
    keys = [x.astype(BF16) for x in spin(w_k)]
    values = dot(normed, w_v).astype(BF16).reshape(rows, cols, width)

    mixtures = []
    for row in range(rows):
        outs = []
        for t in range(width // LANES):
            q_tile, k_tile = queries[t][row], keys[t][row]
            v_tile = values[row, :, t * LANES : (t + 1) * LANES]
            results = []
            for side in range(2):
                k_parts, v_parts = [], []
                for n in range(side * pair, (side + 1) * pair):
                    own = (lane % (LANES // 2)) // half == n
                    k_parts.append(jnp.where(own, k_tile, jnp.zeros_like(k_tile)))
                    ones = jnp.where((lane // head) == (n + pair) % per_tile, 1.0, 0.0).astype(BF16)
                    v_parts.append(jnp.where(lane // head == n, v_tile, ones))
                score = dot_nt(q_tile, jnp.concatenate(k_parts, axis=0))
                results.append(dot(jnp.exp(score).astype(BF16), jnp.concatenate(v_parts, axis=0)))
            low = lane < LANES // 2
            top = jnp.where(low, results[0], results[1])
            bottom = pltpu.roll(jnp.where(low, results[1], results[0]), LANES // 2, 1)
            outs.append(top / bottom)
        mixtures.append(jnp.concatenate(outs, axis=-1))
    mixture = jnp.concatenate(mixtures, axis=0).astype(BF16)
    hidden = (hidden.astype(F32) + dot(mixture, w_ao_scr[...])).astype(BF16)
    out_ref[...] = feed_forward(hidden, w_up_scr[...], w_down_scr[...])
    moment = jnp.full((1, LANES), time_ref[0].astype(F32))
    now, after = level(moment), level(moment - STRIDE)
    keep = jnp.sqrt(1.0 - after) / jnp.sqrt(1.0 - now)
    coef_ref[0:1, :] = jnp.sqrt(after) - keep * jnp.sqrt(now)
    coef_ref[1:2, :] = keep
    for copy in copies[11:] + copies[:1]:
        copy.wait()
    pick_ref[0] = anc_scr[lax.axis_index("dom")]
    need = jnp.int32(0)
    if small:
        for j in range(anc_scr.shape[0]):
            need = lax.bitwise_or(need, lax.shift_left(jnp.int32(1), lax.bitwise_xor(anc_scr[j], jnp.int32(j))))
    need_ref[0] = lax.shift_right_logical(need, jnp.int32(1))


def project_keys(rows, cols, half, block, h_ref, w_k, w_v, cos_ref, sin_ref):
    wide = HEADS * half
    normed = rms_round(h_ref[...])
    left, right = turn_rows(rows, cols, wide, block, dot(normed, w_k), 1.0, cos_ref, sin_ref)
    values = dot(normed, w_v).astype(BF16).reshape(rows, cols, 2 * wide)
    return left, right, values


def turn_rows(rows, cols, wide, block, part, factor, cos_ref, sin_ref):
    scaled = part * (rms_scale(part) * factor)
    scaled = scaled.reshape(rows, cols, 2 * wide)
    first = lax.bitwise_xor(lax.axis_index("row"), block) * rows
    left, right = [], []
    for row in range(rows):
        cos, sin = cos_ref[pl.ds(first + row, 1), :], sin_ref[pl.ds(first + row, 1), :]
        a, c = scaled[row, :, :wide], scaled[row, :, wide:]
        left.append((a * cos - c * sin).astype(BF16))
        right.append((a * sin + c * cos).astype(BF16))
    return left, right


def mix_rows(rows, cols, half, q_left, q_right, keys, totals):
    wide = HEADS * half
    width = 2 * wide
    ids0 = lax.broadcasted_iota(jnp.int32, (width, width), 0)
    ids1 = lax.broadcasted_iota(jnp.int32, (width, width), 1)
    gather = jnp.where(ids0 // half == ids1 // half, 1.0, 0.0).astype(BF16)
    num_left, num_right, den = totals
    for two in range(0, len(keys), 2):
        prods = [q_left * k_l[None] + q_right * k_r[None] for k_l, k_r, _ in keys[two : two + 2]]
        score = dot(jnp.concatenate(prods, axis=-1).reshape(rows * cols, width), gather)
        weight = jnp.exp(score).reshape(rows, cols, width)
        for side, (_, _, value) in enumerate(keys[two : two + 2]):
            share = weight[..., side * wide : (side + 1) * wide]
            num_left += share * value[:, :wide].astype(F32)[None]
            num_right += share * value[:, wide:].astype(F32)[None]
            den += share
    return num_left, num_right, den


def all_keys(rows, cols, half, blocks, h_refs, w_k, w_v, cos_ref, sin_ref):
    keys = []
    for block, h_ref in zip(blocks, h_refs):
        left, right, values = project_keys(rows, cols, half, block, h_ref, w_k, w_v, cos_ref, sin_ref)
        keys += [(left[row], right[row], values[row]) for row in range(rows)]
    return keys


def first_kernel(rows, cols, own_ref, *refs):
    w_qkv_ref, w_ao_ref, cos_ref, sin_ref, q_ref, left_ref, right_ref, den_ref, w_kv_ref, w_o_ref = refs
    width = own_ref.shape[-1]
    head = width // HEADS
    half = head // 2
    wide = width // 2
    pick = shuffle_matrix(width, functools.partial(full_halves, width, half))
    w_q = dot(w_qkv_ref[:, :width], pick).astype(BF16)
    w_k = dot(w_qkv_ref[:, width : 2 * width], pick).astype(BF16)
    w_v = dot(w_qkv_ref[:, 2 * width :], pick).astype(BF16)
    w_kv_ref[:, :width] = w_k
    w_kv_ref[:, width:] = w_v
    w_o_ref[...] = lax.dot_general(
        pick, w_ao_ref[...], (((0,), (0,)), ((), ())), preferred_element_type=F32
    ).astype(BF16)
    part = dot(rms_round(own_ref[...]), w_q)
    left, right = turn_rows(rows, cols, wide, 0, part, 1.0 / math.sqrt(head), cos_ref, sin_ref)
    q_left, q_right = jnp.stack(left), jnp.stack(right)
    q_ref[:, :, :wide] = q_left
    q_ref[:, :, wide:] = q_right
    keys = all_keys(rows, cols, half, [0], [own_ref], w_k, w_v, cos_ref, sin_ref)
    totals = (jnp.zeros((rows, cols, wide), F32),) * 3
    left_ref[...], right_ref[...], den_ref[...] = mix_rows(rows, cols, half, q_left, q_right, keys, totals)


def more_kernel(blocks, rows, cols, *refs):
    h_refs = refs[: len(blocks)]
    q_ref, left_in, right_in, den_in, w_kv_ref, cos_ref, sin_ref, left_ref, right_ref, den_ref = refs[len(blocks) :]
    width = q_ref.shape[-1]
    half = width // HEADS // 2
    wide = width // 2
    keys = all_keys(rows, cols, half, blocks, h_refs, w_kv_ref[:, :width], w_kv_ref[:, width:], cos_ref, sin_ref)
    totals = (left_in[...], right_in[...], den_in[...])
    left_ref[...], right_ref[...], den_ref[...] = mix_rows(
        rows, cols, half, q_ref[:, :, :wide], q_ref[:, :, wide:], keys, totals
    )


def late_kernel(blocks, rows, cols, chan, own_ref, *refs):
    h_refs = refs[: len(blocks)]
    (
        q_ref, left_ref, right_ref, den_ref, w_kv_ref, w_o_ref, w_up_ref, w_down_ref, w_out_ref, cos_ref, sin_ref,
        out_ref, tok_scr,
    ) = refs[len(blocks) :]
    width = own_ref.shape[-1]
    half = width // HEADS // 2
    wide = width // 2
    keys = all_keys(
        rows, cols, half, blocks, h_refs, w_kv_ref[:, :width], w_kv_ref[:, width:], cos_ref, sin_ref
    )
    left, right, den = mix_rows(
        rows, cols, half, q_ref[:, :, :wide], q_ref[:, :, wide:], keys,
        (left_ref[...], right_ref[...], den_ref[...]),
    )
    mixture = jnp.concatenate([left / den, right / den], axis=-1).astype(BF16)
    hidden = (own_ref[...].astype(F32) + dot(mixture.reshape(rows * cols, width), w_o_ref[...])).astype(BF16)
    hidden = feed_forward(hidden, w_up_ref[...], w_down_ref[...])
    tok_scr[:, :chan] = lax.dot_general(
        rms_round(hidden), w_out_ref[...], (((1,), (1,)), ((), ())), preferred_element_type=F32
    )
    pack_tokens(tok_scr, out_ref, rows, cols, chan)


def finish_kernel(turn, pick_ref, coef_ref, *refs):
    count = len(turn)
    states, preds = refs[:count], refs[count : 2 * count]
    new_state_ref, new_pred_ref, state_scr, sems = refs[2 * count :]
    pick = lax.bitwise_xor(pick_ref[0], lax.axis_index("dom"))
    for place, k in enumerate(turn):

        def write(k=place):
            copy_pred = pltpu.make_async_copy(preds[k], new_pred_ref, sems.at[0])
            copy_pred.start()
            state_scr[...] = (
                coef_ref[0:1, 0:1][None] * preds[k][...].astype(F32)
                + coef_ref[1:2, 0:1][None] * states[k][...].astype(F32)
            ).astype(BF16)
            copy_state = pltpu.make_async_copy(state_scr, new_state_ref, sems.at[1])
            copy_state.start()
            copy_pred.wait()
            copy_state.wait()

        if count > 1:
            pl.when(pick == k)(write)
        else:
            write()


VMEM_SPEC = pl.BlockSpec(memory_space=pltpu.VMEM)
SMEM_SPEC = pl.BlockSpec(memory_space=pltpu.SMEM)
HBM_SPEC = pl.BlockSpec(memory_space=pltpu.HBM)


def cube(value, axis, size, bits):
    blocks = [value]
    step = bits // 2
    order = [0]
    while step:
        pairs = [(i, i ^ step) for i in range(size)]
        blocks = blocks + [lax.ppermute(b, axis, pairs) for b in blocks]
        order = order + [o ^ step for o in order]
        step //= 2
    return [blocks[order.index(b)] for b in range(bits)]


def kernel_call(body, name, operands, specs, outs, work, scratch=(), out_specs=None, limit=VMEM_LIMIT):
    single = not isinstance(outs, (list, tuple))
    if out_specs is None:
        out_specs = VMEM_SPEC if single else [VMEM_SPEC] * len(outs)
    return pl.pallas_call(
        body,
        out_shape=outs,
        in_specs=specs,
        out_specs=out_specs,
        scratch_shapes=list(scratch),
        compiler_params=pltpu.CompilerParams(vmem_limit_bytes=limit),
        cost_estimate=pl.CostEstimate(flops=work, bytes_accessed=0, transcendentals=0),
        name=name,
    )(*operands)


def make(mesh):
    n_dom, n_row = mesh.shape["dom"], mesh.shape["row"]

    def per_device(
        state, prev_pred, ancestors, timestep, w_in, w_time, w_qkv, w_attn_out, w_up, w_down, w_out
    ):
        rows, flat = state.shape[1], state.shape[2]
        chan, width = w_out.shape[1], w_out.shape[0]
        cols = flat // chan
        head = width // HEADS
        half = head // 2
        like = jax.ShapeDtypeStruct

        along = rotary_angles(cols, half, LANES)
        sign = np.where(np.arange(LANES) < LANES // 2, -1.0, 1.0)
        tables = [jnp.asarray(np.cos(along), F32), jnp.asarray(np.sin(along) * sign, F32)]
        like_of = lambda arr: like(arr.shape, arr.dtype)
        block_of = lambda arr: like(arr.shape[1:], arr.dtype)
        vmem = lambda arr: pltpu.VMEM(arr.shape, arr.dtype)
        block_vmem = lambda arr: pltpu.VMEM(arr.shape[1:], arr.dtype)
        my_dom = lax.axis_index("dom").astype(jnp.int32)
        small = n_dom in (2, 4)
        inputs = (
            timestep, ancestors, state, prev_pred, w_time, w_in, w_qkv, *tables, w_attn_out, w_up, w_down, w_out.T,
        )
        hidden, state_out, coefs, pick, need, *weights = kernel_call(
            functools.partial(row_kernel, rows, cols, chan, small), "row_block",
            (timestep, *[pltpu.with_memory_space_constraint(x, pltpu.HBM) for x in inputs[1:]]),
            [SMEM_SPEC] + [HBM_SPEC] * (len(inputs) - 1),
            [
                like((rows * cols, width), BF16), like_of(state), like((2, LANES), F32), like((1,), jnp.int32), like((1,), jnp.int32),
                block_of(w_qkv), block_of(w_attn_out), block_of(w_up), block_of(w_down), like_of(w_out.T),
            ],
            5 * WORK_UNIT,
            [
                pltpu.SMEM(ancestors.shape, jnp.int32),
                vmem(prev_pred), vmem(w_time), vmem(w_in), block_vmem(w_qkv), vmem(tables[0]), vmem(tables[1]),
                block_vmem(w_attn_out), block_vmem(w_up), block_vmem(w_down),
                pltpu.VMEM((2 * rows, flat), F32),
                pltpu.VMEM((2 * rows * cols, LANES), F32),
                pltpu.SemaphoreType.DMA((16,)),
            ],
            [VMEM_SPEC] * 3 + [SMEM_SPEC] * 2 + [VMEM_SPEC] * 5,
        )
        w_qkv1, w_ao1, w_up1, w_down1, w_out1 = weights

        top = n_row // 2
        early = cube(hidden, "row", n_row, top)
        across = lax.ppermute(hidden, "row", [(i, i ^ top) for i in range(n_row)])
        down = rotary_angles(n_row * rows, half, width // 2)
        tables = [jnp.asarray(np.cos(down), F32), jnp.asarray(np.sin(down), F32)]
        piece = like((rows, cols, width // 2), F32)
        query, *sums, w_kv, w_o = kernel_call(
            functools.partial(first_kernel, rows, cols), "column_first",
            (hidden, w_qkv1, w_ao1, *tables),
            [VMEM_SPEC] * 5,
            [
                like((rows, cols, width), BF16), piece, piece, piece,
                like((width, 2 * width), BF16), like((width, width), BF16),
            ],
            FIRST_WORK * WORK_UNIT,
        )
        middle = [*early[1:], across]
        sums = kernel_call(
            functools.partial(more_kernel, list(range(1, top + 1)), rows, cols), "column_early",
            (*middle, query, *sums, w_kv, *tables),
            [VMEM_SPEC] * (len(middle) + 7),
            [piece, piece, piece],
            MORE_WORK * WORK_UNIT,
        )
        late = cube(across, "row", n_row, top)[1:]
        late_ids = list(range(top + 1, n_row))
        own_pred = kernel_call(
            functools.partial(late_kernel, late_ids, rows, cols, chan), "column_late",
            (hidden, *late, query, *sums, w_kv, w_o, w_up1, w_down1, w_out1, *tables),
            [VMEM_SPEC] * (len(late) + 12),
            like((1, rows, flat), BF16),
            5 * WORK_UNIT,
            [pltpu.VMEM((rows * cols, LANES), F32)],
        )

        shape = like(state.shape, BF16)

        def finish(turn, states, preds, coefs, pick):
            return kernel_call(
                functools.partial(finish_kernel, turn), "finish",
                (pick, coefs, *states, *preds),
                [SMEM_SPEC] + [VMEM_SPEC] * (1 + 2 * len(preds)),
                (shape, shape),
                WORK_UNIT,
                [pltpu.VMEM(state.shape, BF16), pltpu.SemaphoreType.DMA((2,))],
                (HBM_SPEC, HBM_SPEC),
            )

        if not small:
            every = [
                lax.dynamic_index_in_dim(lax.all_gather(x, "dom"), ancestors[my_dom], 0, keepdims=False)
                for x in (state_out, own_pred)
            ]
            return finish([0], every[:1], every[1:], coefs, pick)

        def swap(value, k):
            return lax.ppermute(value, "dom", [(i, i ^ k) for i in range(n_dom)])

        def gather(turn, states, own_pred, coefs, pick):
            preds = [own_pred] + [swap(own_pred, k) for k in turn]
            return finish([0, *turn], [states[0]] + [states[k] for k in turn], preds, coefs, pick)

        turn = list(range(2, n_dom)) + [1]
        states = [state_out] + [swap(state_out, k) for k in turn]
        states = {0: states[0], **dict(zip(turn, states[1:]))}
        branches = [
            functools.partial(gather, [k for k in turn if (code >> k) & 1]) for code in range(0, 1 << n_dom, 2)
        ]
        return lax.switch(need[0], branches, states, own_pred, coefs, pick)

    return per_device


def solution(mesh):
    spread = P(("group", "dom"), "row", None)
    return jax.shard_map(
        make(mesh),
        mesh=mesh,
        in_specs=(spread, spread, P("group"), P("group")) + (P(),) * 7,
        out_specs=(spread, spread),
        check_vma=False,
    )
```

```python
import functools
import math

import jax
import jax.numpy as jnp
import numpy as np
from jax import lax
from jax.experimental import pallas as pl
from jax.experimental.pallas import tpu as pltpu
from jax.sharding import PartitionSpec as P

HEADS = 8
STEPS = 1000
STRIDE = 20
EPS = 1e-06
LANES = 128
VMEM_LIMIT = 32 * 1024 * 1024
ROW_VMEM_LIMIT = 62 * 1024 * 1024
WORK_UNIT = 1 << 30
FIRST_WORK = 3
MORE_WORK = 3
F32 = jnp.float32
BF16 = jnp.bfloat16


def dot(lhs, rhs):
    return jnp.dot(lhs, rhs, preferred_element_type=F32)


def dot_nt(lhs, rhs):
    return lax.dot_general(lhs, rhs, (((1,), (1,)), ((), ())), preferred_element_type=F32)


def rms_scale(wide):
    return lax.rsqrt(jnp.mean(wide * wide, axis=-1, keepdims=True) + EPS)


def rms_scale_mx(wide):
    n = wide.shape[-1]
    ones = jnp.full((n, n), 1.0 / n, BF16)
    return lax.rsqrt(dot((wide * wide).astype(BF16), ones) + EPS)


def rms_round_mx(values_in):
    wide = values_in.astype(F32)
    return (wide * rms_scale_mx(wide)).astype(BF16)


def rms_round(values_in):
    wide = values_in.astype(F32)
    return (wide * rms_scale(wide)).astype(BF16)


def gelu(values_in):
    return jax.nn.gelu(values_in, approximate=True)


def feed_forward(hidden, w_up, w_down):
    gated = gelu(dot(rms_round_mx(hidden), w_up)).astype(BF16)
    return (hidden.astype(F32) + dot(gated, w_down)).astype(BF16)


def lane_ids(shape):
    return lax.broadcasted_iota(jnp.int32, shape, len(shape) - 1)


def shuffle_matrix(width, source_of):
    rows = lax.broadcasted_iota(jnp.int32, (width, width), 0)
    cols = lax.broadcasted_iota(jnp.int32, (width, width), 1)
    return jnp.where(rows == source_of(cols), 1.0, 0.0).astype(BF16)


def tile_halves(half, j):
    tile, lane = j // LANES, j % LANES
    side, rest = lane // (LANES // 2), lane % (LANES // 2)
    return tile * LANES + (rest // half) * 2 * half + side * half + rest % half


def full_halves(width, half, j):
    side, rest = j // (width // 2), j % (width // 2)
    return (rest // half) * 2 * half + side * half + rest % half


def rotary_angles(count, half, lanes):
    rates = np.exp(-math.log(10000.0) * np.arange(half) / half)
    return np.arange(count)[:, None] * rates[np.arange(lanes) % half][None, :]


def unpack_tokens(flat_ref, out_ref, cols, chan):
    count = flat_ref.shape[0]
    lane = lane_ids((count, LANES))
    for col in range(cols):
        tile, shift = divmod(col * chan, LANES)
        piece = flat_ref[:, tile * LANES : (tile + 1) * LANES]
        if shift + chan > LANES:
            after = flat_ref[:, (tile + 1) * LANES : (tile + 2) * LANES]
            piece = jnp.where(lane >= shift, piece, after)
        if shift:
            piece = pltpu.roll(piece, LANES - shift, 1)
        out_ref[pl.ds(col, count, stride=cols), :] = piece


def pack_tokens(tok_ref, out_ref, rows, cols, chan):
    lane = lane_ids((rows, LANES))
    moved = {}

    def shifted(col):
        if col not in moved:
            piece = tok_ref[pl.ds(col, rows, stride=cols), :]
            shift = (col * chan) % LANES
            moved[col] = pltpu.roll(piece, shift, 1) if shift else piece
        return moved[col]

    for tile in range(cols * chan // LANES):
        first, last = tile * LANES // chan, ((tile + 1) * LANES - 1) // chan
        whole = shifted(last)
        for col in range(last - 1, first - 1, -1):
            whole = jnp.where(lane < (col + 1) * chan - tile * LANES, shifted(col), whole)
        out_ref[0, :, tile * LANES : (tile + 1) * LANES] = whole.astype(BF16)


def level(moment):
    cosine = jnp.cos((moment / STEPS + 0.008) / 1.008 * math.pi / 2.0)
    return cosine * cosine


def time_embedding(moment, width):
    half = width // 2
    rates = jnp.exp(lane_ids((1, half)).astype(F32) * (-math.log(10000.0) / half))
    angles = moment * rates
    return jnp.concatenate([jnp.sin(angles), jnp.cos(angles)], axis=-1)


def time_vector(embedded, w_time):
    first = embedded.astype(BF16)
    rest = embedded - first.astype(F32)
    second = rest.astype(BF16)
    third = (rest - second.astype(F32)).astype(BF16)
    return dot(first, w_time) + dot(second, w_time) + dot(third, w_time)


def row_kernel(
    rows, cols, chan, small,
    time_ref, anc_ref, state_ref, prev_ref, w_time_ref, w_in_ref, w_qkv_ref, cos_ref, sin_ref, w_ao_ref, w_up_ref, w_down_ref, w_out_ref,
    out_ref, state_scr, coef_ref, pick_ref, need_ref, next_qkv_ref, next_ao_ref, next_up_ref, next_down_ref, next_out_ref,
    anc_scr, prev_scr, w_time_scr, w_in_scr, w_qkv_scr, cos_scr, sin_scr, w_ao_scr, w_up_scr, w_down_scr,
    flat_scr, tok_scr, sems,
):
    moves = (
        (anc_ref, anc_scr), (state_ref, state_scr), (prev_ref, prev_scr), (w_time_ref, w_time_scr), (w_in_ref, w_in_scr),
        (w_qkv_ref.at[0], w_qkv_scr), (cos_ref, cos_scr), (sin_ref, sin_scr),
        (w_ao_ref.at[0], w_ao_scr), (w_up_ref.at[0], w_up_scr), (w_down_ref.at[0], w_down_scr),
        (w_qkv_ref.at[1], next_qkv_ref), (w_ao_ref.at[1], next_ao_ref), (w_up_ref.at[1], next_up_ref),
        (w_down_ref.at[1], next_down_ref), (w_out_ref, next_out_ref),
    )
    copies = [pltpu.make_async_copy(s, t, sems.at[i]) for i, (s, t) in enumerate(moves)]
    for copy in copies[:11]:
        copy.start()
    moment = jnp.full((1, LANES), time_ref[0].astype(F32))
    now, after = level(moment), level(moment - STRIDE)
    keep = jnp.sqrt(1.0 - after) / jnp.sqrt(1.0 - now)
    coef_ref[0:1, :] = jnp.sqrt(after) - keep * jnp.sqrt(now)
    coef_ref[1:2, :] = keep
    embedded = time_embedding(time_ref[0].astype(F32), w_time_scr.shape[0])
    width = out_ref.shape[-1]
    head = width // HEADS
    half = head // 2
    for c in copies[1:3]:
        c.wait()
    for copy in copies[11:]:
        copy.start()
    flat_scr[:rows, :] = state_scr[0].astype(F32)
    flat_scr[rows:, :] = prev_scr[0].astype(F32)
    unpack_tokens(flat_scr, tok_scr, cols, chan)
    for c in copies[3:11]:
        c.wait()
    offset_vec = time_vector(embedded, w_time_scr[...])
    count = rows * cols
    w_in = w_in_scr[...].astype(F32)
    blank = jnp.zeros((LANES - chan, width), F32)
    w_state = jnp.concatenate([w_in[:chan], blank], axis=0).astype(BF16)
    w_prev = jnp.concatenate([w_in[chan:], blank], axis=0).astype(BF16)
    hidden = dot(jnp.concatenate([tok_scr[:count].astype(BF16), tok_scr[count:].astype(BF16)], axis=-1), jnp.concatenate([w_state, w_prev], axis=0))
    hidden = (hidden + offset_vec).astype(BF16)

    pick = shuffle_matrix(width, functools.partial(tile_halves, half))
    w_q = dot(w_qkv_scr[:, :width], pick).astype(BF16)
    w_k = dot(w_qkv_scr[:, width : 2 * width], pick).astype(BF16)
    w_v = w_qkv_scr[:, 2 * width :]
    normed = rms_round_mx(hidden)
    cos, sin = cos_scr[...], sin_scr[...]
    lane = lane_ids((cols, LANES))
    per_tile = LANES // head
    pair = per_tile // 2

    def swap_halves(weight):
        parts = []
        for t in range(width // LANES):
            mid = t * LANES + LANES // 2
            parts += [weight[:, mid : (t + 1) * LANES], weight[:, t * LANES : mid]]
        return jnp.concatenate(parts, axis=-1)

    def spin(part):
        plain = dot(normed, part)
        swapped = dot(normed, swap_halves(part))
        factor = rms_scale_mx(plain)
        tiles = []
        for t in range(width // LANES):
            piece, other, scale = (x[:, t * LANES : (t + 1) * LANES].reshape(rows, cols, LANES) for x in (plain, swapped, factor))
            tiles.append((piece * cos[None] + other * sin[None]) * scale)
        return tiles

    scale = 1.0 / math.sqrt(head)
    queries = [(x * scale).astype(BF16) for x in spin(w_q)]
    keys = [x.astype(BF16) for x in spin(w_k)]
    values = dot(normed, w_v).astype(BF16).reshape(rows, cols, width)

    mixtures = []
    for row in range(rows):
        outs = []
        for t in range(width // LANES):
            q_tile, k_tile = queries[t][row], keys[t][row]
            v_tile = values[row, :, t * LANES : (t + 1) * LANES]
            results = []
            for side in range(2):
                k_parts, v_parts = [], []
                for n in range(side * pair, (side + 1) * pair):
                    own = (lane % (LANES // 2)) // half == n
                    k_parts.append(jnp.where(own, k_tile, jnp.zeros_like(k_tile)))
                    ones = jnp.where((lane // head) == (n + pair) % per_tile, 1.0, 0.0).astype(BF16)
                    v_parts.append(jnp.where(lane // head == n, v_tile, ones))
                score = dot_nt(q_tile, jnp.concatenate(k_parts, axis=0))
                results.append(dot(jnp.exp(score).astype(BF16), jnp.concatenate(v_parts, axis=0)))
            low = lane < LANES // 2
            top = jnp.where(low, results[0], results[1])
            bottom = pltpu.roll(jnp.where(low, results[1], results[0]), LANES // 2, 1)
            outs.append(top / bottom)
        mixtures.append(jnp.concatenate(outs, axis=-1))
    mixture = jnp.concatenate(mixtures, axis=0).astype(BF16)
    hidden = (hidden.astype(F32) + dot(mixture, w_ao_scr[...])).astype(BF16)
    out_ref[...] = feed_forward(hidden, w_up_scr[...], w_down_scr[...])
    for copy in copies[11:] + copies[:1]:
        copy.wait()
    pick_ref[0] = anc_scr[lax.axis_index("dom")]
    need = jnp.int32(0)
    if small:
        for j in range(anc_scr.shape[0]):
            need = lax.bitwise_or(need, lax.shift_left(jnp.int32(1), lax.bitwise_xor(anc_scr[j], jnp.int32(j))))
    need_ref[0] = (1 << (anc_scr.shape[0] - 1)) - 1 - lax.shift_right_logical(need, jnp.int32(1))


def project_keys(rows, cols, half, block, h_ref, w_k, w_v, cos_ref, sin_ref):
    wide = HEADS * half
    normed = rms_round(h_ref[...])
    left, right = turn_rows(rows, cols, wide, block, dot(normed, w_k), 1.0, cos_ref, sin_ref)
    values = dot(normed, w_v).astype(BF16).reshape(rows, cols, 2 * wide)
    return left, right, values


def turn_rows(rows, cols, wide, block, part, factor, cos_ref, sin_ref):
    scaled = part * (rms_scale(part) * factor)
    scaled = scaled.reshape(rows, cols, 2 * wide)
    first = lax.bitwise_xor(lax.axis_index("row"), block) * rows
    left, right = [], []
    for row in range(rows):
        cos, sin = cos_ref[pl.ds(first + row, 1), :], sin_ref[pl.ds(first + row, 1), :]
        a, c = scaled[row, :, :wide], scaled[row, :, wide:]
        left.append((a * cos - c * sin).astype(BF16))
        right.append((a * sin + c * cos).astype(BF16))
    return left, right


def mix_rows(rows, cols, half, q_left, q_right, keys, totals):
    wide = HEADS * half
    width = 2 * wide
    ids0 = lax.broadcasted_iota(jnp.int32, (width, width), 0)
    ids1 = lax.broadcasted_iota(jnp.int32, (width, width), 1)
    gather = jnp.where(ids0 // half == ids1 // half, 1.0, 0.0).astype(BF16)
    num_left, num_right, den = totals
    for two in range(0, len(keys), 2):
        prods = [q_left * k_l[None] + q_right * k_r[None] for k_l, k_r, _ in keys[two : two + 2]]
        score = dot(jnp.concatenate(prods, axis=-1).reshape(rows * cols, width), gather)
        weight = jnp.exp(score).reshape(rows, cols, width)
        for side, (_, _, value) in enumerate(keys[two : two + 2]):
            share = weight[..., side * wide : (side + 1) * wide]
            num_left += share * value[:, :wide].astype(F32)[None]
            num_right += share * value[:, wide:].astype(F32)[None]
            den += share
    return num_left, num_right, den


def all_keys(rows, cols, half, blocks, h_refs, w_k, w_v, cos_ref, sin_ref):
    keys = []
    for block, h_ref in zip(blocks, h_refs):
        left, right, values = project_keys(rows, cols, half, block, h_ref, w_k, w_v, cos_ref, sin_ref)
        keys += [(left[row], right[row], values[row]) for row in range(rows)]
    return keys


def first_kernel(rows, cols, own_ref, *refs):
    w_qkv_ref, w_ao_ref, cos_ref, sin_ref, q_ref, left_ref, right_ref, den_ref, w_kv_ref, w_o_ref = refs
    width = own_ref.shape[-1]
    head = width // HEADS
    half = head // 2
    wide = width // 2
    pick = shuffle_matrix(width, functools.partial(full_halves, width, half))
    w_q = dot(w_qkv_ref[:, :width], pick).astype(BF16)
    w_k = dot(w_qkv_ref[:, width : 2 * width], pick).astype(BF16)
    w_v = dot(w_qkv_ref[:, 2 * width :], pick).astype(BF16)
    w_kv_ref[:, :width] = w_k
    w_kv_ref[:, width:] = w_v
    w_o_ref[...] = lax.dot_general(
        pick, w_ao_ref[...], (((0,), (0,)), ((), ())), preferred_element_type=F32
    ).astype(BF16)
    part = dot(rms_round(own_ref[...]), w_q)
    left, right = turn_rows(rows, cols, wide, 0, part, 1.0 / math.sqrt(head), cos_ref, sin_ref)
    q_left, q_right = jnp.stack(left), jnp.stack(right)
    q_ref[:, :, :wide] = q_left
    q_ref[:, :, wide:] = q_right
    keys = all_keys(rows, cols, half, [0], [own_ref], w_k, w_v, cos_ref, sin_ref)
    totals = (jnp.zeros((rows, cols, wide), F32),) * 3
    left_ref[...], right_ref[...], den_ref[...] = mix_rows(rows, cols, half, q_left, q_right, keys, totals)


def more_kernel(blocks, rows, cols, *refs):
    h_refs = refs[: len(blocks)]
    q_ref, left_in, right_in, den_in, w_kv_ref, cos_ref, sin_ref, left_ref, right_ref, den_ref = refs[len(blocks) :]
    width = q_ref.shape[-1]
    half = width // HEADS // 2
    wide = width // 2
    keys = all_keys(rows, cols, half, blocks, h_refs, w_kv_ref[:, :width], w_kv_ref[:, width:], cos_ref, sin_ref)
    totals = (left_in[...], right_in[...], den_in[...])
    left_ref[...], right_ref[...], den_ref[...] = mix_rows(
        rows, cols, half, q_ref[:, :, :wide], q_ref[:, :, wide:], keys, totals
    )


def late_kernel(blocks, rows, cols, chan, own_ref, *refs):
    h_refs = refs[: len(blocks)]
    (
        q_ref, left_ref, right_ref, den_ref, w_kv_ref, w_o_ref, w_up_ref, w_down_ref, w_out_ref, cos_ref, sin_ref,
        out_ref, tok_scr,
    ) = refs[len(blocks) :]
    width = own_ref.shape[-1]
    half = width // HEADS // 2
    wide = width // 2
    keys = all_keys(
        rows, cols, half, blocks, h_refs, w_kv_ref[:, :width], w_kv_ref[:, width:], cos_ref, sin_ref
    )
    left, right, den = mix_rows(
        rows, cols, half, q_ref[:, :, :wide], q_ref[:, :, wide:], keys,
        (left_ref[...], right_ref[...], den_ref[...]),
    )
    mixture = jnp.concatenate([left / den, right / den], axis=-1).astype(BF16)
    hidden = (own_ref[...].astype(F32) + dot(mixture.reshape(rows * cols, width), w_o_ref[...])).astype(BF16)
    hidden = feed_forward(hidden, w_up_ref[...], w_down_ref[...])
    tok_scr[:, :chan] = lax.dot_general(
        rms_round(hidden), w_out_ref[...], (((1,), (1,)), ((), ())), preferred_element_type=F32
    )
    pack_tokens(tok_scr, out_ref, rows, cols, chan)


def finish_kernel(turn, pick_ref, coef_ref, *refs):
    count = len(turn)
    states, preds = refs[:count], refs[count : 2 * count]
    new_state_ref, new_pred_ref, state_scr, sems = refs[2 * count :]
    pick = lax.bitwise_xor(pick_ref[0], lax.axis_index("dom"))
    for place, k in enumerate(turn):

        def write(k=place):
            copy_pred = pltpu.make_async_copy(preds[k], new_pred_ref, sems.at[0])
            copy_pred.start()
            state_scr[...] = (
                coef_ref[0:1, 0:1][None] * preds[k][...].astype(F32)
                + coef_ref[1:2, 0:1][None] * states[k][...].astype(F32)
            ).astype(BF16)
            copy_state = pltpu.make_async_copy(state_scr, new_state_ref, sems.at[1])
            copy_state.start()
            copy_pred.wait()
            copy_state.wait()

        if count > 1:
            pl.when(pick == k)(write)
        else:
            write()


VMEM_SPEC = pl.BlockSpec(memory_space=pltpu.VMEM)
SMEM_SPEC = pl.BlockSpec(memory_space=pltpu.SMEM)
HBM_SPEC = pl.BlockSpec(memory_space=pltpu.HBM)


def cube(value, axis, size, bits):
    blocks = [value]
    step = bits // 2
    order = [0]
    while step:
        pairs = [(i, i ^ step) for i in range(size)]
        blocks = blocks + [lax.ppermute(b, axis, pairs) for b in blocks]
        order = order + [o ^ step for o in order]
        step //= 2
    return [blocks[order.index(b)] for b in range(bits)]


def kernel_call(body, name, operands, specs, outs, work, scratch=(), out_specs=None, limit=VMEM_LIMIT):
    single = not isinstance(outs, (list, tuple))
    if out_specs is None:
        out_specs = VMEM_SPEC if single else [VMEM_SPEC] * len(outs)
    return pl.pallas_call(
        body,
        out_shape=outs,
        in_specs=specs,
        out_specs=out_specs,
        scratch_shapes=list(scratch),
        compiler_params=pltpu.CompilerParams(vmem_limit_bytes=limit),
        cost_estimate=pl.CostEstimate(flops=work, bytes_accessed=0, transcendentals=0),
        name=name,
    )(*operands)


def make(mesh):
    n_dom, n_row = mesh.shape["dom"], mesh.shape["row"]

    def per_device(
        state, prev_pred, ancestors, timestep, w_in, w_time, w_qkv, w_attn_out, w_up, w_down, w_out
    ):
        rows, flat = state.shape[1], state.shape[2]
        chan, width = w_out.shape[1], w_out.shape[0]
        cols = flat // chan
        head = width // HEADS
        half = head // 2
        like = jax.ShapeDtypeStruct

        along = rotary_angles(cols, half, LANES)
        sign = np.where(np.arange(LANES) < LANES // 2, -1.0, 1.0)
        tables = [jnp.asarray(np.cos(along), F32), jnp.asarray(np.sin(along) * sign, F32)]
        like_of = lambda arr: like(arr.shape, arr.dtype)
        block_of = lambda arr: like(arr.shape[1:], arr.dtype)
        vmem = lambda arr: pltpu.VMEM(arr.shape, arr.dtype)
        block_vmem = lambda arr: pltpu.VMEM(arr.shape[1:], arr.dtype)
        my_dom = lax.axis_index("dom").astype(jnp.int32)
        small = n_dom in (2, 4)
        inputs = (
            timestep, ancestors, state, prev_pred, w_time, w_in, w_qkv, *tables, w_attn_out, w_up, w_down, w_out.T,
        )
        hidden, state_out, coefs, pick, need, *weights = kernel_call(
            functools.partial(row_kernel, rows, cols, chan, small), "row_block",
            (timestep, *[pltpu.with_memory_space_constraint(x, pltpu.HBM) for x in inputs[1:]]),
            [SMEM_SPEC] + [HBM_SPEC] * (len(inputs) - 1),
            [
                like((rows * cols, width), BF16), like_of(state), like((2, LANES), F32), like((1,), jnp.int32), like((1,), jnp.int32),
                block_of(w_qkv), block_of(w_attn_out), block_of(w_up), block_of(w_down), like_of(w_out.T),
            ],
            5 * WORK_UNIT,
            [
                pltpu.SMEM(ancestors.shape, jnp.int32),
                vmem(prev_pred), vmem(w_time), vmem(w_in), block_vmem(w_qkv), vmem(tables[0]), vmem(tables[1]),
                block_vmem(w_attn_out), block_vmem(w_up), block_vmem(w_down),
                pltpu.VMEM((2 * rows, flat), F32),
                pltpu.VMEM((2 * rows * cols, LANES), F32),
                pltpu.SemaphoreType.DMA((16,)),
            ],
            [VMEM_SPEC] * 3 + [SMEM_SPEC] * 2 + [VMEM_SPEC] * 5,
        )
        w_qkv1, w_ao1, w_up1, w_down1, w_out1 = weights

        top = n_row // 2
        early = cube(hidden, "row", n_row, top)
        across = lax.ppermute(hidden, "row", [(i, i ^ top) for i in range(n_row)])
        down = rotary_angles(n_row * rows, half, width // 2)
        tables = [jnp.asarray(np.cos(down), F32), jnp.asarray(np.sin(down), F32)]
        piece = like((rows, cols, width // 2), F32)
        query, *sums, w_kv, w_o = kernel_call(
            functools.partial(first_kernel, rows, cols), "column_first",
            (hidden, w_qkv1, w_ao1, *tables),
            [VMEM_SPEC] * 5,
            [
                like((rows, cols, width), BF16), piece, piece, piece,
                like((width, 2 * width), BF16), like((width, width), BF16),
            ],
            FIRST_WORK * WORK_UNIT,
        )
        middle = [*early[1:], across]
        sums = kernel_call(
            functools.partial(more_kernel, list(range(1, top + 1)), rows, cols), "column_early",
            (*middle, query, *sums, w_kv, *tables),
            [VMEM_SPEC] * (len(middle) + 7),
            [piece, piece, piece],
            MORE_WORK * WORK_UNIT,
        )
        late = cube(across, "row", n_row, top)[1:]
        late_ids = list(range(top + 1, n_row))
        own_pred = kernel_call(
            functools.partial(late_kernel, late_ids, rows, cols, chan), "column_late",
            (hidden, *late, query, *sums, w_kv, w_o, w_up1, w_down1, w_out1, *tables),
            [VMEM_SPEC] * (len(late) + 12),
            like((1, rows, flat), BF16),
            5 * WORK_UNIT,
            [pltpu.VMEM((rows * cols, LANES), F32)],
        )

        shape = like(state.shape, BF16)

        def finish(turn, states, preds, coefs, pick):
            return kernel_call(
                functools.partial(finish_kernel, turn), "finish",
                (pick, coefs, *states, *preds),
                [SMEM_SPEC] + [VMEM_SPEC] * (1 + 2 * len(preds)),
                (shape, shape),
                WORK_UNIT,
                [pltpu.VMEM(state.shape, BF16), pltpu.SemaphoreType.DMA((2,))],
                (HBM_SPEC, HBM_SPEC),
            )

        if not small:
            every = [
                lax.dynamic_index_in_dim(lax.all_gather(x, "dom"), ancestors[my_dom], 0, keepdims=False)
                for x in (state_out, own_pred)
            ]
            return finish([0], every[:1], every[1:], coefs, pick)

        def swap(value, k):
            return lax.ppermute(value, "dom", [(i, i ^ k) for i in range(n_dom)])

        def gather(turn, states, own_pred, coefs, pick):
            preds = [own_pred] + [swap(own_pred, k) for k in turn]
            return finish([0, *turn], [states[0]] + [states[1 + order.index(k)] for k in turn], preds, coefs, pick)

        order = list(range(2, n_dom)) + [1]
        states = [state_out] + [swap(state_out, k) for k in order]
        branches = [
            functools.partial(gather, [k for k in order if (code >> k) & 1]) for code in range((1 << n_dom) - 2, -1, -2)
        ]
        return lax.switch(need[0], branches, states, own_pred, coefs, pick)

    return per_device


def solution(mesh):
    spread = P(("group", "dom"), "row", None)
    return jax.shard_map(
        make(mesh),
        mesh=mesh,
        in_specs=(spread, spread, P("group"), P("group")) + (P(),) * 7,
        out_specs=(spread, spread),
        check_vma=False,
    )
```

```python
import functools
import math

import jax
import jax.numpy as jnp
import numpy as np
from jax import lax
from jax.experimental import pallas as pl
from jax.experimental.pallas import tpu as pltpu
from jax.sharding import PartitionSpec as P

HEADS = 8
STEPS = 1000
STRIDE = 20
EPS = 1e-06
LANES = 128
VMEM_LIMIT = 32 * 1024 * 1024
ROW_VMEM_LIMIT = 62 * 1024 * 1024
WORK_UNIT = 1 << 30
FIRST_WORK = 3
MORE_WORK = 3
F32 = jnp.float32
BF16 = jnp.bfloat16


def dot(lhs, rhs):
    return jnp.dot(lhs, rhs, preferred_element_type=F32)


def dot_nt(lhs, rhs):
    return lax.dot_general(lhs, rhs, (((1,), (1,)), ((), ())), preferred_element_type=F32)


def rms_scale(wide):
    return lax.rsqrt(jnp.mean(wide * wide, axis=-1, keepdims=True) + EPS)


def rms_scale_mx(wide):
    n = wide.shape[-1]
    ones = jnp.full((n, n), 1.0 / n, BF16)
    return lax.rsqrt(dot((wide * wide).astype(BF16), ones) + EPS)


def rms_round_mx(values_in):
    wide = values_in.astype(F32)
    return (wide * rms_scale_mx(wide)).astype(BF16)


def rms_round(values_in):
    wide = values_in.astype(F32)
    return (wide * rms_scale(wide)).astype(BF16)


def gelu(values_in):
    half = 0.5 * values_in
    slope = math.sqrt(2.0 / math.pi)
    inner = values_in * (slope + (slope * 0.044715) * (values_in * values_in))
    return half + half * jnp.tanh(inner)


def feed_forward(hidden, w_up, w_down):
    gated = gelu(dot(rms_round_mx(hidden), w_up)).astype(BF16)
    return (hidden.astype(F32) + dot(gated, w_down)).astype(BF16)


def lane_ids(shape):
    return lax.broadcasted_iota(jnp.int32, shape, len(shape) - 1)


def shuffle_matrix(width, source_of):
    rows = lax.broadcasted_iota(jnp.int32, (width, width), 0)
    cols = lax.broadcasted_iota(jnp.int32, (width, width), 1)
    return jnp.where(rows == source_of(cols), 1.0, 0.0).astype(BF16)


def tile_halves(half, j):
    tile, lane = j // LANES, j % LANES
    side, rest = lane // (LANES // 2), lane % (LANES // 2)
    return tile * LANES + (rest // half) * 2 * half + side * half + rest % half


def full_halves(width, half, j):
    side, rest = j // (width // 2), j % (width // 2)
    return (rest // half) * 2 * half + side * half + rest % half


def rotary_angles(count, half, lanes):
    rates = np.exp(-math.log(10000.0) * np.arange(half) / half)
    return np.arange(count)[:, None] * rates[np.arange(lanes) % half][None, :]


def unpack_tokens(flat_ref, out_ref, cols, chan):
    count = flat_ref.shape[0]
    lane = lane_ids((count, LANES))
    for col in range(cols):
        tile, shift = divmod(col * chan, LANES)
        piece = flat_ref[:, tile * LANES : (tile + 1) * LANES]
        if shift + chan > LANES:
            after = flat_ref[:, (tile + 1) * LANES : (tile + 2) * LANES]
            piece = jnp.where(lane >= shift, piece, after)
        if shift:
            piece = pltpu.roll(piece, LANES - shift, 1)
        out_ref[pl.ds(col, count, stride=cols), :] = piece


def pack_tokens(tok_ref, out_ref, rows, cols, chan):
    lane = lane_ids((rows, LANES))
    moved = {}

    def shifted(col):
        if col not in moved:
            piece = tok_ref[pl.ds(col, rows, stride=cols), :]
            shift = (col * chan) % LANES
            moved[col] = pltpu.roll(piece, shift, 1) if shift else piece
        return moved[col]

    for tile in range(cols * chan // LANES):
        first, last = tile * LANES // chan, ((tile + 1) * LANES - 1) // chan
        whole = shifted(last)
        for col in range(last - 1, first - 1, -1):
            whole = jnp.where(lane < (col + 1) * chan - tile * LANES, shifted(col), whole)
        out_ref[0, :, tile * LANES : (tile + 1) * LANES] = whole.astype(BF16)


def level(moment):
    cosine = jnp.cos((moment / STEPS + 0.008) / 1.008 * math.pi / 2.0)
    return cosine * cosine


def time_embedding(moment, width):
    half = width // 2
    rates = jnp.exp(lane_ids((1, half)).astype(F32) * (-math.log(10000.0) / half))
    angles = moment * rates
    return jnp.concatenate([jnp.sin(angles), jnp.cos(angles)], axis=-1)


def time_vector(embedded, w_time):
    first = embedded.astype(BF16)
    rest = embedded - first.astype(F32)
    second = rest.astype(BF16)
    third = (rest - second.astype(F32)).astype(BF16)
    return dot(first, w_time) + dot(second, w_time) + dot(third, w_time)


def row_kernel(
    rows, cols, chan, small,
    time_ref, anc_ref, state_ref, prev_ref, w_time_ref, w_in_ref, w_qkv_ref, cos_ref, sin_ref, w_ao_ref, w_up_ref, w_down_ref, w_out_ref,
    out_ref, state_scr, coef_ref, pick_ref, need_ref, next_qkv_ref, next_ao_ref, next_up_ref, next_down_ref, next_out_ref,
    anc_scr, prev_scr, w_time_scr, w_in_scr, w_qkv_scr, cos_scr, sin_scr, w_ao_scr, w_up_scr, w_down_scr,
    flat_scr, tok_scr, sems,
):
    moves = (
        (anc_ref, anc_scr), (state_ref, state_scr), (prev_ref, prev_scr), (w_time_ref, w_time_scr), (w_in_ref, w_in_scr),
        (w_qkv_ref.at[0], w_qkv_scr), (cos_ref, cos_scr), (sin_ref, sin_scr),
        (w_ao_ref.at[0], w_ao_scr), (w_up_ref.at[0], w_up_scr), (w_down_ref.at[0], w_down_scr),
        (w_qkv_ref.at[1], next_qkv_ref), (w_ao_ref.at[1], next_ao_ref), (w_up_ref.at[1], next_up_ref),
        (w_down_ref.at[1], next_down_ref), (w_out_ref, next_out_ref),
    )
    copies = [pltpu.make_async_copy(s, t, sems.at[i]) for i, (s, t) in enumerate(moves)]
    for copy in copies[:11]:
        copy.start()
    moment = jnp.full((1, LANES), time_ref[0].astype(F32))
    now, after = level(moment), level(moment - STRIDE)
    keep = jnp.sqrt(1.0 - after) / jnp.sqrt(1.0 - now)
    coef_ref[0:1, :] = jnp.sqrt(after) - keep * jnp.sqrt(now)
    coef_ref[1:2, :] = keep
    embedded = time_embedding(time_ref[0].astype(F32), w_time_scr.shape[0])
    width = out_ref.shape[-1]
    head = width // HEADS
    half = head // 2
    for c in copies[1:3]:
        c.wait()
    for copy in copies[11:]:
        copy.start()
    flat_scr[:rows, :] = state_scr[0].astype(F32)
    flat_scr[rows:, :] = prev_scr[0].astype(F32)
    unpack_tokens(flat_scr, tok_scr, cols, chan)
    for c in copies[3:11]:
        c.wait()
    offset_vec = time_vector(embedded, w_time_scr[...])
    count = rows * cols
    w_in = w_in_scr[...].astype(F32)
    blank = jnp.zeros((LANES - chan, width), F32)
    w_state = jnp.concatenate([w_in[:chan], blank], axis=0).astype(BF16)
    w_prev = jnp.concatenate([w_in[chan:], blank], axis=0).astype(BF16)
    hidden = dot(jnp.concatenate([tok_scr[:count].astype(BF16), tok_scr[count:].astype(BF16)], axis=-1), jnp.concatenate([w_state, w_prev], axis=0))
    hidden = (hidden + offset_vec).astype(BF16)

    pick = shuffle_matrix(width, functools.partial(tile_halves, half))
    w_q = dot(w_qkv_scr[:, :width], pick).astype(BF16)
    w_k = dot(w_qkv_scr[:, width : 2 * width], pick).astype(BF16)
    w_v = w_qkv_scr[:, 2 * width :]
    normed = rms_round_mx(hidden)
    cos, sin = cos_scr[...], sin_scr[...]
    lane = lane_ids((cols, LANES))
    per_tile = LANES // head
    pair = per_tile // 2

    def swap_halves(weight):
        parts = []
        for t in range(width // LANES):
            mid = t * LANES + LANES // 2
            parts += [weight[:, mid : (t + 1) * LANES], weight[:, t * LANES : mid]]
        return jnp.concatenate(parts, axis=-1)

    def spin(part):
        plain = dot(normed, part)
        swapped = dot(normed, swap_halves(part))
        factor = rms_scale_mx(plain)
        tiles = []
        for t in range(width // LANES):
            piece, other, scale = (x[:, t * LANES : (t + 1) * LANES].reshape(rows, cols, LANES) for x in (plain, swapped, factor))
            tiles.append((piece * cos[None] + other * sin[None]) * scale)
        return tiles

    scale = 1.0 / math.sqrt(head)
    queries = [(x * scale).astype(BF16) for x in spin(w_q)]
    keys = [x.astype(BF16) for x in spin(w_k)]
    values = dot(normed, w_v).astype(BF16).reshape(rows, cols, width)

    mixtures = []
    for row in range(rows):
        outs = []
        for t in range(width // LANES):
            q_tile, k_tile = queries[t][row], keys[t][row]
            v_tile = values[row, :, t * LANES : (t + 1) * LANES]
            results = []
            for side in range(2):
                k_parts, v_parts = [], []
                for n in range(side * pair, (side + 1) * pair):
                    own = (lane % (LANES // 2)) // half == n
                    k_parts.append(jnp.where(own, k_tile, jnp.zeros_like(k_tile)))
                    ones = jnp.where((lane // head) == (n + pair) % per_tile, 1.0, 0.0).astype(BF16)
                    v_parts.append(jnp.where(lane // head == n, v_tile, ones))
                score = dot_nt(q_tile, jnp.concatenate(k_parts, axis=0))
                results.append(dot(jnp.exp(score).astype(BF16), jnp.concatenate(v_parts, axis=0)))
            low = lane < LANES // 2
            top = jnp.where(low, results[0], results[1])
            bottom = pltpu.roll(jnp.where(low, results[1], results[0]), LANES // 2, 1)
            outs.append(top / bottom)
        mixtures.append(jnp.concatenate(outs, axis=-1))
    mixture = jnp.concatenate(mixtures, axis=0).astype(BF16)
    hidden = (hidden.astype(F32) + dot(mixture, w_ao_scr[...])).astype(BF16)
    out_ref[...] = feed_forward(hidden, w_up_scr[...], w_down_scr[...])
    for copy in copies[11:] + copies[:1]:
        copy.wait()
    pick_ref[0] = anc_scr[lax.axis_index("dom")]
    need = jnp.int32(0)
    if small:
        for j in range(anc_scr.shape[0]):
            need = lax.bitwise_or(need, lax.shift_left(jnp.int32(1), lax.bitwise_xor(anc_scr[j], jnp.int32(j))))
    need_ref[0] = (1 << (anc_scr.shape[0] - 1)) - 1 - lax.shift_right_logical(need, jnp.int32(1))


def project_keys(rows, cols, half, block, h_ref, w_k, w_v, cos_ref, sin_ref):
    wide = HEADS * half
    normed = rms_round(h_ref[...])
    left, right = turn_rows(rows, cols, wide, block, dot(normed, w_k), 1.0, cos_ref, sin_ref)
    values = dot(normed, w_v).astype(BF16).reshape(rows, cols, 2 * wide)
    return left, right, values


def turn_rows(rows, cols, wide, block, part, factor, cos_ref, sin_ref):
    scaled = part * (rms_scale(part) * factor)
    scaled = scaled.reshape(rows, cols, 2 * wide)
    first = lax.bitwise_xor(lax.axis_index("row"), block) * rows
    left, right = [], []
    for row in range(rows):
        cos, sin = cos_ref[pl.ds(first + row, 1), :], sin_ref[pl.ds(first + row, 1), :]
        a, c = scaled[row, :, :wide], scaled[row, :, wide:]
        left.append((a * cos - c * sin).astype(BF16))
        right.append((a * sin + c * cos).astype(BF16))
    return left, right


def mix_rows(rows, cols, half, q_left, q_right, keys, totals):
    wide = HEADS * half
    width = 2 * wide
    ids0 = lax.broadcasted_iota(jnp.int32, (width, width), 0)
    ids1 = lax.broadcasted_iota(jnp.int32, (width, width), 1)
    gather = jnp.where(ids0 // half == ids1 // half, 1.0, 0.0).astype(BF16)
    num_left, num_right, den = totals
    for two in range(0, len(keys), 2):
        prods = [q_left * k_l[None] + q_right * k_r[None] for k_l, k_r, _ in keys[two : two + 2]]
        score = dot(jnp.concatenate(prods, axis=-1).reshape(rows * cols, width), gather)
        weight = jnp.exp(score).reshape(rows, cols, width)
        for side, (_, _, value) in enumerate(keys[two : two + 2]):
            share = weight[..., side * wide : (side + 1) * wide]
            num_left += share * value[:, :wide].astype(F32)[None]
            num_right += share * value[:, wide:].astype(F32)[None]
            den += share
    return num_left, num_right, den


def all_keys(rows, cols, half, blocks, h_refs, w_k, w_v, cos_ref, sin_ref):
    keys = []
    for block, h_ref in zip(blocks, h_refs):
        left, right, values = project_keys(rows, cols, half, block, h_ref, w_k, w_v, cos_ref, sin_ref)
        keys += [(left[row], right[row], values[row]) for row in range(rows)]
    return keys


def first_kernel(rows, cols, own_ref, *refs):
    w_qkv_ref, w_ao_ref, cos_ref, sin_ref, q_ref, left_ref, right_ref, den_ref, w_kv_ref, w_o_ref = refs
    width = own_ref.shape[-1]
    head = width // HEADS
    half = head // 2
    wide = width // 2
    pick = shuffle_matrix(width, functools.partial(full_halves, width, half))
    w_q = dot(w_qkv_ref[:, :width], pick).astype(BF16)
    w_k = dot(w_qkv_ref[:, width : 2 * width], pick).astype(BF16)
    w_v = dot(w_qkv_ref[:, 2 * width :], pick).astype(BF16)
    w_kv_ref[:, :width] = w_k
    w_kv_ref[:, width:] = w_v
    w_o_ref[...] = lax.dot_general(
        pick, w_ao_ref[...], (((0,), (0,)), ((), ())), preferred_element_type=F32
    ).astype(BF16)
    part = dot(rms_round(own_ref[...]), w_q)
    left, right = turn_rows(rows, cols, wide, 0, part, 1.0 / math.sqrt(head), cos_ref, sin_ref)
    q_left, q_right = jnp.stack(left), jnp.stack(right)
    q_ref[:, :, :wide] = q_left
    q_ref[:, :, wide:] = q_right
    keys = all_keys(rows, cols, half, [0], [own_ref], w_k, w_v, cos_ref, sin_ref)
    totals = (jnp.zeros((rows, cols, wide), F32),) * 3
    left_ref[...], right_ref[...], den_ref[...] = mix_rows(rows, cols, half, q_left, q_right, keys, totals)


def more_kernel(blocks, rows, cols, *refs):
    h_refs = refs[: len(blocks)]
    q_ref, left_in, right_in, den_in, w_kv_ref, cos_ref, sin_ref, left_ref, right_ref, den_ref = refs[len(blocks) :]
    width = q_ref.shape[-1]
    half = width // HEADS // 2
    wide = width // 2
    keys = all_keys(rows, cols, half, blocks, h_refs, w_kv_ref[:, :width], w_kv_ref[:, width:], cos_ref, sin_ref)
    totals = (left_in[...], right_in[...], den_in[...])
    left_ref[...], right_ref[...], den_ref[...] = mix_rows(
        rows, cols, half, q_ref[:, :, :wide], q_ref[:, :, wide:], keys, totals
    )


def late_kernel(blocks, rows, cols, chan, own_ref, *refs):
    h_refs = refs[: len(blocks)]
    (
        q_ref, left_ref, right_ref, den_ref, w_kv_ref, w_o_ref, w_up_ref, w_down_ref, w_out_ref, cos_ref, sin_ref,
        out_ref, tok_scr,
    ) = refs[len(blocks) :]
    width = own_ref.shape[-1]
    half = width // HEADS // 2
    wide = width // 2
    keys = all_keys(
        rows, cols, half, blocks, h_refs, w_kv_ref[:, :width], w_kv_ref[:, width:], cos_ref, sin_ref
    )
    left, right, den = mix_rows(
        rows, cols, half, q_ref[:, :, :wide], q_ref[:, :, wide:], keys,
        (left_ref[...], right_ref[...], den_ref[...]),
    )
    mixture = jnp.concatenate([left / den, right / den], axis=-1).astype(BF16)
    hidden = (own_ref[...].astype(F32) + dot(mixture.reshape(rows * cols, width), w_o_ref[...])).astype(BF16)
    hidden = feed_forward(hidden, w_up_ref[...], w_down_ref[...])
    tok_scr[:, :chan] = lax.dot_general(
        rms_round(hidden), w_out_ref[...], (((1,), (1,)), ((), ())), preferred_element_type=F32
    )
    pack_tokens(tok_scr, out_ref, rows, cols, chan)


def finish_kernel(turn, pick_ref, coef_ref, *refs):
    count = len(turn)
    states, preds = refs[:count], refs[count : 2 * count]
    new_state_ref, new_pred_ref, state_scr, sems = refs[2 * count :]
    pick = lax.bitwise_xor(pick_ref[0], lax.axis_index("dom"))
    for place, k in enumerate(turn):

        def write(k=place):
            copy_pred = pltpu.make_async_copy(preds[k], new_pred_ref, sems.at[0])
            copy_pred.start()
            state_scr[...] = (
                coef_ref[0:1, 0:1][None] * preds[k][...].astype(F32)
                + coef_ref[1:2, 0:1][None] * states[k][...].astype(F32)
            ).astype(BF16)
            copy_state = pltpu.make_async_copy(state_scr, new_state_ref, sems.at[1])
            copy_state.start()
            copy_pred.wait()
            copy_state.wait()

        if count > 1:
            pl.when(pick == k)(write)
        else:
            write()


VMEM_SPEC = pl.BlockSpec(memory_space=pltpu.VMEM)
SMEM_SPEC = pl.BlockSpec(memory_space=pltpu.SMEM)
HBM_SPEC = pl.BlockSpec(memory_space=pltpu.HBM)


def cube(value, axis, size, bits):
    blocks = [value]
    step = bits // 2
    order = [0]
    while step:
        pairs = [(i, i ^ step) for i in range(size)]
        blocks = blocks + [lax.ppermute(b, axis, pairs) for b in blocks]
        order = order + [o ^ step for o in order]
        step //= 2
    return [blocks[order.index(b)] for b in range(bits)]


def kernel_call(body, name, operands, specs, outs, work, scratch=(), out_specs=None, limit=VMEM_LIMIT):
    single = not isinstance(outs, (list, tuple))
    if out_specs is None:
        out_specs = VMEM_SPEC if single else [VMEM_SPEC] * len(outs)
    return pl.pallas_call(
        body,
        out_shape=outs,
        in_specs=specs,
        out_specs=out_specs,
        scratch_shapes=list(scratch),
        compiler_params=pltpu.CompilerParams(vmem_limit_bytes=limit),
        cost_estimate=pl.CostEstimate(flops=work, bytes_accessed=0, transcendentals=0),
        name=name,
    )(*operands)


def make(mesh):
    n_dom, n_row = mesh.shape["dom"], mesh.shape["row"]

    def per_device(
        state, prev_pred, ancestors, timestep, w_in, w_time, w_qkv, w_attn_out, w_up, w_down, w_out
    ):
        rows, flat = state.shape[1], state.shape[2]
        chan, width = w_out.shape[1], w_out.shape[0]
        cols = flat // chan
        head = width // HEADS
        half = head // 2
        like = jax.ShapeDtypeStruct

        along = rotary_angles(cols, half, LANES)
        sign = np.where(np.arange(LANES) < LANES // 2, -1.0, 1.0)
        tables = [jnp.asarray(np.cos(along), F32), jnp.asarray(np.sin(along) * sign, F32)]
        like_of = lambda arr: like(arr.shape, arr.dtype)
        block_of = lambda arr: like(arr.shape[1:], arr.dtype)
        vmem = lambda arr: pltpu.VMEM(arr.shape, arr.dtype)
        block_vmem = lambda arr: pltpu.VMEM(arr.shape[1:], arr.dtype)
        my_dom = lax.axis_index("dom").astype(jnp.int32)
        small = n_dom in (2, 4)
        inputs = (
            timestep, ancestors, state, prev_pred, w_time, w_in, w_qkv, *tables, w_attn_out, w_up, w_down, w_out.T,
        )
        hidden, state_out, coefs, pick, need, *weights = kernel_call(
            functools.partial(row_kernel, rows, cols, chan, small), "row_block",
            (timestep, *[pltpu.with_memory_space_constraint(x, pltpu.HBM) for x in inputs[1:]]),
            [SMEM_SPEC] + [HBM_SPEC] * (len(inputs) - 1),
            [
                like((rows * cols, width), BF16), like_of(state), like((2, LANES), F32), like((1,), jnp.int32), like((1,), jnp.int32),
                block_of(w_qkv), block_of(w_attn_out), block_of(w_up), block_of(w_down), like_of(w_out.T),
            ],
            5 * WORK_UNIT,
            [
                pltpu.SMEM(ancestors.shape, jnp.int32),
                vmem(prev_pred), vmem(w_time), vmem(w_in), block_vmem(w_qkv), vmem(tables[0]), vmem(tables[1]),
                block_vmem(w_attn_out), block_vmem(w_up), block_vmem(w_down),
                pltpu.VMEM((2 * rows, flat), F32),
                pltpu.VMEM((2 * rows * cols, LANES), F32),
                pltpu.SemaphoreType.DMA((16,)),
            ],
            [VMEM_SPEC] * 3 + [SMEM_SPEC] * 2 + [VMEM_SPEC] * 5,
        )
        w_qkv1, w_ao1, w_up1, w_down1, w_out1 = weights

        top = n_row // 2
        early = cube(hidden, "row", n_row, top)
        across = lax.ppermute(hidden, "row", [(i, i ^ top) for i in range(n_row)])
        down = rotary_angles(n_row * rows, half, width // 2)
        tables = [jnp.asarray(np.cos(down), F32), jnp.asarray(np.sin(down), F32)]
        piece = like((rows, cols, width // 2), F32)
        query, *sums, w_kv, w_o = kernel_call(
            functools.partial(first_kernel, rows, cols), "column_first",
            (hidden, w_qkv1, w_ao1, *tables),
            [VMEM_SPEC] * 5,
            [
                like((rows, cols, width), BF16), piece, piece, piece,
                like((width, 2 * width), BF16), like((width, width), BF16),
            ],
            FIRST_WORK * WORK_UNIT,
        )
        middle = [*early[1:], across]
        sums = kernel_call(
            functools.partial(more_kernel, list(range(1, top + 1)), rows, cols), "column_early",
            (*middle, query, *sums, w_kv, *tables),
            [VMEM_SPEC] * (len(middle) + 7),
            [piece, piece, piece],
            MORE_WORK * WORK_UNIT,
        )
        late = cube(across, "row", n_row, top)[1:]
        late_ids = list(range(top + 1, n_row))
        own_pred = kernel_call(
            functools.partial(late_kernel, late_ids, rows, cols, chan), "column_late",
            (hidden, *late, query, *sums, w_kv, w_o, w_up1, w_down1, w_out1, *tables),
            [VMEM_SPEC] * (len(late) + 12),
            like((1, rows, flat), BF16),
            5 * WORK_UNIT,
            [pltpu.VMEM((rows * cols, LANES), F32)],
        )

        shape = like(state.shape, BF16)

        def finish(turn, states, preds, coefs, pick):
            return kernel_call(
                functools.partial(finish_kernel, turn), "finish",
                (pick, coefs, *states, *preds),
                [SMEM_SPEC] + [VMEM_SPEC] * (1 + 2 * len(preds)),
                (shape, shape),
                WORK_UNIT,
                [pltpu.VMEM(state.shape, BF16), pltpu.SemaphoreType.DMA((2,))],
                (HBM_SPEC, HBM_SPEC),
            )

        if not small:
            every = [
                lax.dynamic_index_in_dim(lax.all_gather(x, "dom"), ancestors[my_dom], 0, keepdims=False)
                for x in (state_out, own_pred)
            ]
            return finish([0], every[:1], every[1:], coefs, pick)

        def swap(value, k):
            return lax.ppermute(value, "dom", [(i, i ^ k) for i in range(n_dom)])

        def gather(turn, states, own_pred, coefs, pick):
            preds = [own_pred] + [swap(own_pred, k) for k in turn]
            return finish([0, *turn], [states[0]] + [states[1 + order.index(k)] for k in turn], preds, coefs, pick)

        order = list(range(2, n_dom)) + [1]
        states = [state_out] + [swap(state_out, k) for k in order]
        branches = [
            functools.partial(gather, [k for k in order if (code >> k) & 1]) for code in range((1 << n_dom) - 2, -1, -2)
        ]
        return lax.switch(need[0], branches, states, own_pred, coefs, pick)

    return per_device


def solution(mesh):
    spread = P(("group", "dom"), "row", None)
    return jax.shard_map(
        make(mesh),
        mesh=mesh,
        in_specs=(spread, spread, P("group"), P("group")) + (P(),) * 7,
        out_specs=(spread, spread),
        check_vma=False,
    )
```

```python
import functools
import math

import jax
import jax.numpy as jnp
import numpy as np
from jax import lax
from jax.experimental import pallas as pl
from jax.experimental.pallas import tpu as pltpu
from jax.sharding import PartitionSpec as P

HEADS = 8
STEPS = 1000
STRIDE = 20
EPS = 1e-06
LANES = 128
VMEM_LIMIT = 32 * 1024 * 1024
ROW_VMEM_LIMIT = 62 * 1024 * 1024
WORK_UNIT = 1 << 30
FIRST_WORK = 3
MORE_WORK = 3
F32 = jnp.float32
BF16 = jnp.bfloat16


def dot(lhs, rhs):
    return jnp.dot(lhs, rhs, preferred_element_type=F32)


def dot_nt(lhs, rhs):
    return lax.dot_general(lhs, rhs, (((1,), (1,)), ((), ())), preferred_element_type=F32)


def rms_scale(wide):
    return lax.rsqrt(jnp.mean(wide * wide, axis=-1, keepdims=True) + EPS)


def rms_scale_mx(wide):
    n = wide.shape[-1]
    ones = jnp.full((n, n), 1.0 / n, BF16)
    return lax.rsqrt(dot((wide * wide).astype(BF16), ones) + EPS)


def rms_round_mx(values_in):
    wide = values_in.astype(F32)
    return (wide * rms_scale_mx(wide)).astype(BF16)


def rms_round(values_in):
    wide = values_in.astype(F32)
    return (wide * rms_scale(wide)).astype(BF16)


def gelu(values_in):
    half = 0.5 * values_in
    slope = math.sqrt(2.0 / math.pi)
    inner = values_in * (slope + (slope * 0.044715) * (values_in * values_in))
    return half + half * jnp.tanh(inner)


def feed_forward(hidden, w_up, w_down):
    gated = gelu(dot(rms_round_mx(hidden), w_up)).astype(BF16)
    return (hidden.astype(F32) + dot(gated, w_down)).astype(BF16)


def lane_ids(shape):
    return lax.broadcasted_iota(jnp.int32, shape, len(shape) - 1)


def shuffle_matrix(width, source_of):
    rows = lax.broadcasted_iota(jnp.int32, (width, width), 0)
    cols = lax.broadcasted_iota(jnp.int32, (width, width), 1)
    return jnp.where(rows == source_of(cols), 1.0, 0.0).astype(BF16)


def tile_halves(half, j):
    tile, lane = j // LANES, j % LANES
    side, rest = lane // (LANES // 2), lane % (LANES // 2)
    return tile * LANES + (rest // half) * 2 * half + side * half + rest % half


def full_halves(width, half, j):
    side, rest = j // (width // 2), j % (width // 2)
    return (rest // half) * 2 * half + side * half + rest % half


def rotary_angles(count, half, lanes):
    rates = np.exp(-math.log(10000.0) * np.arange(half) / half)
    return np.arange(count)[:, None] * rates[np.arange(lanes) % half][None, :]


def unpack_tokens(flat_ref, out_ref, cols, chan):
    count = flat_ref.shape[0]
    lane = lane_ids((count, LANES))
    for col in range(cols):
        tile, shift = divmod(col * chan, LANES)
        piece = flat_ref[:, tile * LANES : (tile + 1) * LANES]
        if shift + chan > LANES:
            after = flat_ref[:, (tile + 1) * LANES : (tile + 2) * LANES]
            piece = jnp.where(lane >= shift, piece, after)
        if shift:
            piece = pltpu.roll(piece, LANES - shift, 1)
        out_ref[pl.ds(col, count, stride=cols), :] = piece


def pack_tokens(tok_ref, out_ref, rows, cols, chan):
    lane = lane_ids((rows, LANES))
    moved = {}

    def shifted(col):
        if col not in moved:
            piece = tok_ref[pl.ds(col, rows, stride=cols), :]
            shift = (col * chan) % LANES
            moved[col] = pltpu.roll(piece, shift, 1) if shift else piece
        return moved[col]

    for tile in range(cols * chan // LANES):
        first, last = tile * LANES // chan, ((tile + 1) * LANES - 1) // chan
        whole = shifted(last)
        for col in range(last - 1, first - 1, -1):
            whole = jnp.where(lane < (col + 1) * chan - tile * LANES, shifted(col), whole)
        out_ref[0, :, tile * LANES : (tile + 1) * LANES] = whole.astype(BF16)


def level(moment):
    cosine = jnp.cos((moment / STEPS + 0.008) / 1.008 * math.pi / 2.0)
    return cosine * cosine


def time_embedding(moment, width):
    half = width // 2
    rates = jnp.exp(lane_ids((1, half)).astype(F32) * (-math.log(10000.0) / half))
    angles = moment * rates
    return jnp.concatenate([jnp.sin(angles), jnp.cos(angles)], axis=-1)


def time_vector(embedded, w_time):
    first = embedded.astype(BF16)
    rest = embedded - first.astype(F32)
    second = rest.astype(BF16)
    third = (rest - second.astype(F32)).astype(BF16)
    return dot(first, w_time) + dot(second, w_time) + dot(third, w_time)


def row_kernel(
    rows, cols, chan, small,
    time_ref, anc_ref, state_ref, prev_ref, w_time_ref, w_in_ref, w_qkv_ref, cos_ref, sin_ref, w_ao_ref, w_up_ref, w_down_ref, w_out_ref,
    out_ref, state_scr, coef_ref, pick_ref, need_ref, next_qkv_ref, next_ao_ref, next_up_ref, next_down_ref, next_out_ref,
    anc_scr, prev_scr, w_time_scr, w_in_scr, w_qkv_scr, cos_scr, sin_scr, w_ao_scr, w_up_scr, w_down_scr,
    flat_scr, tok_scr, sems,
):
    moves = (
        (anc_ref, anc_scr), (state_ref, state_scr), (prev_ref, prev_scr), (w_time_ref, w_time_scr), (w_in_ref, w_in_scr),
        (w_qkv_ref.at[0], w_qkv_scr), (cos_ref, cos_scr), (sin_ref, sin_scr),
        (w_ao_ref.at[0], w_ao_scr), (w_up_ref.at[0], w_up_scr), (w_down_ref.at[0], w_down_scr),
        (w_qkv_ref.at[1], next_qkv_ref), (w_ao_ref.at[1], next_ao_ref), (w_up_ref.at[1], next_up_ref),
        (w_down_ref.at[1], next_down_ref), (w_out_ref, next_out_ref),
    )
    copies = [pltpu.make_async_copy(s, t, sems.at[i]) for i, (s, t) in enumerate(moves)]
    for copy in copies[:11]:
        copy.start()
    moment = jnp.full((1, LANES), time_ref[0].astype(F32))
    now, after = level(moment), level(moment - STRIDE)
    keep = jnp.sqrt(1.0 - after) / jnp.sqrt(1.0 - now)
    coef_ref[0:1, :] = jnp.sqrt(after) - keep * jnp.sqrt(now)
    coef_ref[1:2, :] = keep
    embedded = time_embedding(time_ref[0].astype(F32), w_time_scr.shape[0])
    width = out_ref.shape[-1]
    head = width // HEADS
    half = head // 2
    for c in copies[1:3]:
        c.wait()
    for copy in copies[11:]:
        copy.start()
    flat_scr[:rows, :] = state_scr[0].astype(F32)
    flat_scr[rows:, :] = prev_scr[0].astype(F32)
    unpack_tokens(flat_scr, tok_scr, cols, chan)
    for c in copies[3:11]:
        c.wait()
    offset_vec = time_vector(embedded, w_time_scr[...])
    count = rows * cols
    w_in = w_in_scr[...].astype(F32)
    blank = jnp.zeros((LANES - chan, width), F32)
    w_state = jnp.concatenate([w_in[:chan], blank], axis=0).astype(BF16)
    w_prev = jnp.concatenate([w_in[chan:], blank], axis=0).astype(BF16)
    hidden = dot(jnp.concatenate([tok_scr[:count].astype(BF16), tok_scr[count:].astype(BF16)], axis=-1), jnp.concatenate([w_state, w_prev], axis=0))
    hidden = (hidden + offset_vec).astype(BF16)

    pick = shuffle_matrix(width, functools.partial(tile_halves, half))
    w_q = dot(w_qkv_scr[:, :width], pick).astype(BF16)
    w_k = dot(w_qkv_scr[:, width : 2 * width], pick).astype(BF16)
    w_v = w_qkv_scr[:, 2 * width :]
    normed = rms_round_mx(hidden)
    cos, sin = cos_scr[...], sin_scr[...]
    lane = lane_ids((cols, LANES))
    per_tile = LANES // head
    pair = per_tile // 2

    def swap_halves(weight):
        parts = []
        for t in range(width // LANES):
            mid = t * LANES + LANES // 2
            parts += [weight[:, mid : (t + 1) * LANES], weight[:, t * LANES : mid]]
        return jnp.concatenate(parts, axis=-1)

    def spin(part):
        plain = dot(normed, part)
        swapped = dot(normed, swap_halves(part))
        factor = rms_scale_mx(plain)
        tiles = []
        for t in range(width // LANES):
            piece, other, scale = (x[:, t * LANES : (t + 1) * LANES].reshape(rows, cols, LANES) for x in (plain, swapped, factor))
            tiles.append((piece * cos[None] + other * sin[None]) * scale)
        return tiles

    scale = math.log2(math.e) / math.sqrt(head)
    queries = [(x * scale).astype(BF16) for x in spin(w_q)]
    keys = [x.astype(BF16) for x in spin(w_k)]
    values = dot(normed, w_v).astype(BF16).reshape(rows, cols, width)

    mixtures = []
    for row in range(rows):
        outs = []
        for t in range(width // LANES):
            q_tile, k_tile = queries[t][row], keys[t][row]
            v_tile = values[row, :, t * LANES : (t + 1) * LANES]
            results = []
            for side in range(2):
                k_parts, v_parts = [], []
                for n in range(side * pair, (side + 1) * pair):
                    own = (lane % (LANES // 2)) // half == n
                    k_parts.append(jnp.where(own, k_tile, jnp.zeros_like(k_tile)))
                    ones = jnp.where((lane // head) == (n + pair) % per_tile, 1.0, 0.0).astype(BF16)
                    v_parts.append(jnp.where(lane // head == n, v_tile, ones))
                score = dot_nt(q_tile, jnp.concatenate(k_parts, axis=0))
                results.append(dot(jnp.exp2(score).astype(BF16), jnp.concatenate(v_parts, axis=0)))
            low = lane < LANES // 2
            top = jnp.where(low, results[0], results[1])
            bottom = pltpu.roll(jnp.where(low, results[1], results[0]), LANES // 2, 1)
            outs.append(top / bottom)
        mixtures.append(jnp.concatenate(outs, axis=-1))
    mixture = jnp.concatenate(mixtures, axis=0).astype(BF16)
    hidden = (hidden.astype(F32) + dot(mixture, w_ao_scr[...])).astype(BF16)
    out_ref[...] = feed_forward(hidden, w_up_scr[...], w_down_scr[...])
    for copy in copies[11:] + copies[:1]:
        copy.wait()
    pick_ref[0] = anc_scr[lax.axis_index("dom")]
    need = jnp.int32(0)
    if small:
        for j in range(anc_scr.shape[0]):
            need = lax.bitwise_or(need, lax.shift_left(jnp.int32(1), lax.bitwise_xor(anc_scr[j], jnp.int32(j))))
    need_ref[0] = (1 << (anc_scr.shape[0] - 1)) - 1 - lax.shift_right_logical(need, jnp.int32(1))


def project_keys(rows, cols, half, block, h_ref, w_k, w_v, cos_ref, sin_ref):
    wide = HEADS * half
    normed = rms_round(h_ref[...])
    left, right = turn_rows(rows, cols, wide, block, dot(normed, w_k), 1.0, cos_ref, sin_ref)
    values = dot(normed, w_v).astype(BF16).reshape(rows, cols, 2 * wide)
    return left, right, values


def turn_rows(rows, cols, wide, block, part, factor, cos_ref, sin_ref):
    scaled = part * (rms_scale(part) * factor)
    scaled = scaled.reshape(rows, cols, 2 * wide)
    first = lax.bitwise_xor(lax.axis_index("row"), block) * rows
    left, right = [], []
    for row in range(rows):
        cos, sin = cos_ref[pl.ds(first + row, 1), :], sin_ref[pl.ds(first + row, 1), :]
        a, c = scaled[row, :, :wide], scaled[row, :, wide:]
        left.append((a * cos - c * sin).astype(BF16))
        right.append((a * sin + c * cos).astype(BF16))
    return left, right


def mix_rows(rows, cols, half, q_left, q_right, keys, totals):
    wide = HEADS * half
    width = 2 * wide
    ids0 = lax.broadcasted_iota(jnp.int32, (width, width), 0)
    ids1 = lax.broadcasted_iota(jnp.int32, (width, width), 1)
    gather = jnp.where(ids0 // half == ids1 // half, 1.0, 0.0).astype(BF16)
    num_left, num_right, den = totals
    for two in range(0, len(keys), 2):
        prods = [q_left * k_l[None] + q_right * k_r[None] for k_l, k_r, _ in keys[two : two + 2]]
        score = dot(jnp.concatenate(prods, axis=-1).reshape(rows * cols, width), gather)
        weight = jnp.exp2(score).reshape(rows, cols, width)
        for side, (_, _, value) in enumerate(keys[two : two + 2]):
            share = weight[..., side * wide : (side + 1) * wide]
            num_left += share * value[:, :wide].astype(F32)[None]
            num_right += share * value[:, wide:].astype(F32)[None]
            den += share
    return num_left, num_right, den


def all_keys(rows, cols, half, blocks, h_refs, w_k, w_v, cos_ref, sin_ref):
    keys = []
    for block, h_ref in zip(blocks, h_refs):
        left, right, values = project_keys(rows, cols, half, block, h_ref, w_k, w_v, cos_ref, sin_ref)
        keys += [(left[row], right[row], values[row]) for row in range(rows)]
    return keys


def first_kernel(rows, cols, own_ref, *refs):
    w_qkv_ref, w_ao_ref, cos_ref, sin_ref, q_ref, left_ref, right_ref, den_ref, w_kv_ref, w_o_ref = refs
    width = own_ref.shape[-1]
    head = width // HEADS
    half = head // 2
    wide = width // 2
    pick = shuffle_matrix(width, functools.partial(full_halves, width, half))
    w_q = dot(w_qkv_ref[:, :width], pick).astype(BF16)
    w_k = dot(w_qkv_ref[:, width : 2 * width], pick).astype(BF16)
    w_v = dot(w_qkv_ref[:, 2 * width :], pick).astype(BF16)
    w_kv_ref[:, :width] = w_k
    w_kv_ref[:, width:] = w_v
    w_o_ref[...] = lax.dot_general(
        pick, w_ao_ref[...], (((0,), (0,)), ((), ())), preferred_element_type=F32
    ).astype(BF16)
    part = dot(rms_round(own_ref[...]), w_q)
    left, right = turn_rows(rows, cols, wide, 0, part, math.log2(math.e) / math.sqrt(head), cos_ref, sin_ref)
    q_left, q_right = jnp.stack(left), jnp.stack(right)
    q_ref[:, :, :wide] = q_left
    q_ref[:, :, wide:] = q_right
    keys = all_keys(rows, cols, half, [0], [own_ref], w_k, w_v, cos_ref, sin_ref)
    totals = (jnp.zeros((rows, cols, wide), F32),) * 3
    left_ref[...], right_ref[...], den_ref[...] = mix_rows(rows, cols, half, q_left, q_right, keys, totals)


def more_kernel(blocks, rows, cols, *refs):
    h_refs = refs[: len(blocks)]
    q_ref, left_in, right_in, den_in, w_kv_ref, cos_ref, sin_ref, left_ref, right_ref, den_ref = refs[len(blocks) :]
    width = q_ref.shape[-1]
    half = width // HEADS // 2
    wide = width // 2
    keys = all_keys(rows, cols, half, blocks, h_refs, w_kv_ref[:, :width], w_kv_ref[:, width:], cos_ref, sin_ref)
    totals = (left_in[...], right_in[...], den_in[...])
    left_ref[...], right_ref[...], den_ref[...] = mix_rows(
        rows, cols, half, q_ref[:, :, :wide], q_ref[:, :, wide:], keys, totals
    )


def late_kernel(blocks, rows, cols, chan, own_ref, *refs):
    h_refs = refs[: len(blocks)]
    (
        q_ref, left_ref, right_ref, den_ref, w_kv_ref, w_o_ref, w_up_ref, w_down_ref, w_out_ref, cos_ref, sin_ref,
        out_ref, tok_scr,
    ) = refs[len(blocks) :]
    width = own_ref.shape[-1]
    half = width // HEADS // 2
    wide = width // 2
    keys = all_keys(
        rows, cols, half, blocks, h_refs, w_kv_ref[:, :width], w_kv_ref[:, width:], cos_ref, sin_ref
    )
    left, right, den = mix_rows(
        rows, cols, half, q_ref[:, :, :wide], q_ref[:, :, wide:], keys,
        (left_ref[...], right_ref[...], den_ref[...]),
    )
    mixture = jnp.concatenate([left / den, right / den], axis=-1).astype(BF16)
    hidden = (own_ref[...].astype(F32) + dot(mixture.reshape(rows * cols, width), w_o_ref[...])).astype(BF16)
    hidden = feed_forward(hidden, w_up_ref[...], w_down_ref[...])
    tok_scr[:, :chan] = lax.dot_general(
        rms_round_mx(hidden), w_out_ref[...], (((1,), (1,)), ((), ())), preferred_element_type=F32
    )
    pack_tokens(tok_scr, out_ref, rows, cols, chan)


def finish_kernel(turn, pick_ref, coef_ref, *refs):
    count = len(turn)
    states, preds = refs[:count], refs[count : 2 * count]
    new_state_ref, new_pred_ref, state_scr, sems = refs[2 * count :]
    pick = lax.bitwise_xor(pick_ref[0], lax.axis_index("dom"))
    for place, k in enumerate(turn):

        def write(k=place):
            copy_pred = pltpu.make_async_copy(preds[k], new_pred_ref, sems.at[0])
            copy_pred.start()
            state_scr[...] = (
                coef_ref[0:1, 0:1][None] * preds[k][...].astype(F32)
                + coef_ref[1:2, 0:1][None] * states[k][...].astype(F32)
            ).astype(BF16)
            copy_state = pltpu.make_async_copy(state_scr, new_state_ref, sems.at[1])
            copy_state.start()
            copy_pred.wait()
            copy_state.wait()

        if count > 1:
            pl.when(pick == k)(write)
        else:
            write()


VMEM_SPEC = pl.BlockSpec(memory_space=pltpu.VMEM)
SMEM_SPEC = pl.BlockSpec(memory_space=pltpu.SMEM)
HBM_SPEC = pl.BlockSpec(memory_space=pltpu.HBM)


def cube(value, axis, size, bits):
    blocks = [value]
    step = bits // 2
    order = [0]
    while step:
        pairs = [(i, i ^ step) for i in range(size)]
        blocks = blocks + [lax.ppermute(b, axis, pairs) for b in blocks]
        order = order + [o ^ step for o in order]
        step //= 2
    return [blocks[order.index(b)] for b in range(bits)]


def kernel_call(body, name, operands, specs, outs, work, scratch=(), out_specs=None, limit=VMEM_LIMIT):
    single = not isinstance(outs, (list, tuple))
    if out_specs is None:
        out_specs = VMEM_SPEC if single else [VMEM_SPEC] * len(outs)
    return pl.pallas_call(
        body,
        out_shape=outs,
        in_specs=specs,
        out_specs=out_specs,
        scratch_shapes=list(scratch),
        compiler_params=pltpu.CompilerParams(vmem_limit_bytes=limit),
        cost_estimate=pl.CostEstimate(flops=work, bytes_accessed=0, transcendentals=0),
        name=name,
    )(*operands)


def make(mesh):
    n_dom, n_row = mesh.shape["dom"], mesh.shape["row"]

    def per_device(
        state, prev_pred, ancestors, timestep, w_in, w_time, w_qkv, w_attn_out, w_up, w_down, w_out
    ):
        rows, flat = state.shape[1], state.shape[2]
        chan, width = w_out.shape[1], w_out.shape[0]
        cols = flat // chan
        head = width // HEADS
        half = head // 2
        like = jax.ShapeDtypeStruct

        along = rotary_angles(cols, half, LANES)
        sign = np.where(np.arange(LANES) < LANES // 2, -1.0, 1.0)
        tables = [jnp.asarray(np.cos(along), F32), jnp.asarray(np.sin(along) * sign, F32)]
        like_of = lambda arr: like(arr.shape, arr.dtype)
        block_of = lambda arr: like(arr.shape[1:], arr.dtype)
        vmem = lambda arr: pltpu.VMEM(arr.shape, arr.dtype)
        block_vmem = lambda arr: pltpu.VMEM(arr.shape[1:], arr.dtype)
        my_dom = lax.axis_index("dom").astype(jnp.int32)
        small = n_dom in (2, 4)
        inputs = (
            timestep, ancestors, state, prev_pred, w_time, w_in, w_qkv, *tables, w_attn_out, w_up, w_down, w_out.T,
        )
        hidden, state_out, coefs, pick, need, *weights = kernel_call(
            functools.partial(row_kernel, rows, cols, chan, small), "row_block",
            (timestep, *[pltpu.with_memory_space_constraint(x, pltpu.HBM) for x in inputs[1:]]),
            [SMEM_SPEC] + [HBM_SPEC] * (len(inputs) - 1),
            [
                like((rows * cols, width), BF16), like_of(state), like((2, LANES), F32), like((1,), jnp.int32), like((1,), jnp.int32),
                block_of(w_qkv), block_of(w_attn_out), block_of(w_up), block_of(w_down), like_of(w_out.T),
            ],
            5 * WORK_UNIT,
            [
                pltpu.SMEM(ancestors.shape, jnp.int32),
                vmem(prev_pred), vmem(w_time), vmem(w_in), block_vmem(w_qkv), vmem(tables[0]), vmem(tables[1]),
                block_vmem(w_attn_out), block_vmem(w_up), block_vmem(w_down),
                pltpu.VMEM((2 * rows, flat), F32),
                pltpu.VMEM((2 * rows * cols, LANES), F32),
                pltpu.SemaphoreType.DMA((16,)),
            ],
            [VMEM_SPEC] * 3 + [SMEM_SPEC] * 2 + [VMEM_SPEC] * 5,
        )
        w_qkv1, w_ao1, w_up1, w_down1, w_out1 = weights

        top = n_row // 2
        early = cube(hidden, "row", n_row, top)
        across = lax.ppermute(hidden, "row", [(i, i ^ top) for i in range(n_row)])
        down = rotary_angles(n_row * rows, half, width // 2)
        tables = [jnp.asarray(np.cos(down), F32), jnp.asarray(np.sin(down), F32)]
        piece = like((rows, cols, width // 2), F32)
        query, *sums, w_kv, w_o = kernel_call(
            functools.partial(first_kernel, rows, cols), "column_first",
            (hidden, w_qkv1, w_ao1, *tables),
            [VMEM_SPEC] * 5,
            [
                like((rows, cols, width), BF16), piece, piece, piece,
                like((width, 2 * width), BF16), like((width, width), BF16),
            ],
            FIRST_WORK * WORK_UNIT,
        )
        middle = [*early[1:], across]
        sums = kernel_call(
            functools.partial(more_kernel, list(range(1, top + 1)), rows, cols), "column_early",
            (*middle, query, *sums, w_kv, *tables),
            [VMEM_SPEC] * (len(middle) + 7),
            [piece, piece, piece],
            MORE_WORK * WORK_UNIT,
        )
        late = cube(across, "row", n_row, top)[1:]
        late_ids = list(range(top + 1, n_row))
        own_pred = kernel_call(
            functools.partial(late_kernel, late_ids, rows, cols, chan), "column_late",
            (hidden, *late, query, *sums, w_kv, w_o, w_up1, w_down1, w_out1, *tables),
            [VMEM_SPEC] * (len(late) + 12),
            like((1, rows, flat), BF16),
            5 * WORK_UNIT,
            [pltpu.VMEM((rows * cols, LANES), F32)],
        )

        shape = like(state.shape, BF16)

        def finish(turn, states, preds, coefs, pick):
            return kernel_call(
                functools.partial(finish_kernel, turn), "finish",
                (pick, coefs, *states, *preds),
                [SMEM_SPEC] + [VMEM_SPEC] * (1 + 2 * len(preds)),
                (shape, shape),
                WORK_UNIT,
                [pltpu.VMEM(state.shape, BF16), pltpu.SemaphoreType.DMA((2,))],
                (HBM_SPEC, HBM_SPEC),
            )

        if not small:
            every = [
                lax.dynamic_index_in_dim(lax.all_gather(x, "dom"), ancestors[my_dom], 0, keepdims=False)
                for x in (state_out, own_pred)
            ]
            return finish([0], every[:1], every[1:], coefs, pick)

        def swap(value, k):
            return lax.ppermute(value, "dom", [(i, i ^ k) for i in range(n_dom)])

        def gather(turn, states, own_pred, coefs, pick):
            preds = [own_pred] + [swap(own_pred, k) for k in turn]
            return finish([0, *turn], [states[0]] + [states[1 + order.index(k)] for k in turn], preds, coefs, pick)

        order = list(range(2, n_dom)) + [1]
        states = [state_out] + [swap(state_out, k) for k in order]
        branches = [
            functools.partial(gather, [k for k in order if (code >> k) & 1]) for code in range((1 << n_dom) - 2, -1, -2)
        ]
        return lax.switch(need[0], branches, states, own_pred, coefs, pick)

    return per_device


def solution(mesh):
    spread = P(("group", "dom"), "row", None)
    return jax.shard_map(
        make(mesh),
        mesh=mesh,
        in_specs=(spread, spread, P("group"), P("group")) + (P(),) * 7,
        out_specs=(spread, spread),
        check_vma=False,
    )
```

```python
import functools
import math

import jax
import jax.numpy as jnp
import numpy as np
from jax import lax
from jax.experimental import pallas as pl
from jax.experimental.pallas import tpu as pltpu
from jax.sharding import PartitionSpec as P

HEADS = 8
STEPS = 1000
STRIDE = 20
EPS = 1e-06
LANES = 128
VMEM_LIMIT = 32 * 1024 * 1024
ROW_VMEM_LIMIT = 62 * 1024 * 1024
WORK_UNIT = 1 << 30
FIRST_WORK = 3
MORE_WORK = 3
F32 = jnp.float32
BF16 = jnp.bfloat16


def dot(lhs, rhs):
    return jnp.dot(lhs, rhs, preferred_element_type=F32)


def dot_nt(lhs, rhs):
    return lax.dot_general(lhs, rhs, (((1,), (1,)), ((), ())), preferred_element_type=F32)


def rms_scale(wide):
    return lax.rsqrt(jnp.mean(wide * wide, axis=-1, keepdims=True) + EPS)


def rms_scale_mx(wide):
    n = wide.shape[-1]
    ones = jnp.full((n, n), 1.0 / n, BF16)
    return lax.rsqrt(dot((wide * wide).astype(BF16), ones) + EPS)


def rms_round_mx(values_in):
    wide = values_in.astype(F32)
    return (wide * rms_scale_mx(wide)).astype(BF16)


def rms_round(values_in):
    wide = values_in.astype(F32)
    return (wide * rms_scale(wide)).astype(BF16)


def gelu(values_in):
    half = 0.5 * values_in
    slope = math.sqrt(2.0 / math.pi)
    inner = values_in * (slope + (slope * 0.044715) * (values_in * values_in))
    return half + half * jnp.tanh(inner)


def feed_forward(hidden, w_up, w_down):
    gated = gelu(dot(rms_round_mx(hidden), w_up)).astype(BF16)
    return (hidden.astype(F32) + dot(gated, w_down)).astype(BF16)


def lane_ids(shape):
    return lax.broadcasted_iota(jnp.int32, shape, len(shape) - 1)


def shuffle_matrix(width, source_of):
    rows = lax.broadcasted_iota(jnp.int32, (width, width), 0)
    cols = lax.broadcasted_iota(jnp.int32, (width, width), 1)
    return jnp.where(rows == source_of(cols), 1.0, 0.0).astype(BF16)


def tile_halves(half, j):
    tile, lane = j // LANES, j % LANES
    side, rest = lane // (LANES // 2), lane % (LANES // 2)
    return tile * LANES + (rest // half) * 2 * half + side * half + rest % half


def full_halves(width, half, j):
    side, rest = j // (width // 2), j % (width // 2)
    return (rest // half) * 2 * half + side * half + rest % half


def rotary_angles(count, half, lanes):
    rates = np.exp(-math.log(10000.0) * np.arange(half) / half)
    return np.arange(count)[:, None] * rates[np.arange(lanes) % half][None, :]


def unpack_tokens(flat_ref, out_ref, cols, chan):
    count = flat_ref.shape[0]
    lane = lane_ids((count, LANES))
    for col in range(cols):
        tile, shift = divmod(col * chan, LANES)
        piece = flat_ref[:, tile * LANES : (tile + 1) * LANES]
        if shift + chan > LANES:
            after = flat_ref[:, (tile + 1) * LANES : (tile + 2) * LANES]
            piece = jnp.where(lane >= shift, piece, after)
        if shift:
            piece = pltpu.roll(piece, LANES - shift, 1)
        out_ref[pl.ds(col, count, stride=cols), :] = piece


def pack_tokens(tok_ref, out_ref, rows, cols, chan):
    lane = lane_ids((rows, LANES))
    moved = {}

    def shifted(col):
        if col not in moved:
            piece = tok_ref[pl.ds(col, rows, stride=cols), :]
            shift = (col * chan) % LANES
            moved[col] = pltpu.roll(piece, shift, 1) if shift else piece
        return moved[col]

    for tile in range(cols * chan // LANES):
        first, last = tile * LANES // chan, ((tile + 1) * LANES - 1) // chan
        whole = shifted(last)
        for col in range(last - 1, first - 1, -1):
            whole = jnp.where(lane < (col + 1) * chan - tile * LANES, shifted(col), whole)
        out_ref[0, :, tile * LANES : (tile + 1) * LANES] = whole.astype(BF16)


def level(moment):
    cosine = jnp.cos((moment / STEPS + 0.008) / 1.008 * math.pi / 2.0)
    return cosine * cosine


def time_embedding(moment, width):
    half = width // 2
    rates = jnp.exp(lane_ids((1, half)).astype(F32) * (-math.log(10000.0) / half))
    angles = moment * rates
    return jnp.concatenate([jnp.sin(angles), jnp.cos(angles)], axis=-1)


def time_vector(embedded, w_time):
    first = embedded.astype(BF16)
    rest = embedded - first.astype(F32)
    second = rest.astype(BF16)
    third = (rest - second.astype(F32)).astype(BF16)
    return dot(first, w_time) + dot(second, w_time) + dot(third, w_time)


def row_kernel(
    rows, cols, chan, small,
    time_ref, anc_ref, state_ref, prev_ref, w_time_ref, w_in_ref, w_qkv_ref, cos_ref, sin_ref, w_ao_ref, w_up_ref, w_down_ref, w_out_ref,
    out_ref, state_scr, coef_ref, pick_ref, need_ref, next_qkv_ref, next_ao_ref, next_up_ref, next_down_ref, next_out_ref,
    anc_scr, prev_scr, w_time_scr, w_in_scr, w_qkv_scr, cos_scr, sin_scr, w_ao_scr, w_up_scr, w_down_scr,
    flat_scr, tok_scr, sems,
):
    moves = (
        (anc_ref, anc_scr), (state_ref, state_scr), (prev_ref, prev_scr), (w_time_ref, w_time_scr), (w_in_ref, w_in_scr),
        (w_qkv_ref.at[0], w_qkv_scr), (cos_ref, cos_scr), (sin_ref, sin_scr),
        (w_ao_ref.at[0], w_ao_scr), (w_up_ref.at[0], w_up_scr), (w_down_ref.at[0], w_down_scr),
        (w_qkv_ref.at[1], next_qkv_ref), (w_ao_ref.at[1], next_ao_ref), (w_up_ref.at[1], next_up_ref),
        (w_down_ref.at[1], next_down_ref), (w_out_ref, next_out_ref),
    )
    copies = [pltpu.make_async_copy(s, t, sems.at[i]) for i, (s, t) in enumerate(moves)]
    for copy in copies[:11]:
        copy.start()
    moment = jnp.full((1, LANES), time_ref[0].astype(F32))
    now, after = level(moment), level(moment - STRIDE)
    keep = jnp.sqrt(1.0 - after) / jnp.sqrt(1.0 - now)
    coef_ref[0:1, :] = jnp.sqrt(after) - keep * jnp.sqrt(now)
    coef_ref[1:2, :] = keep
    embedded = time_embedding(time_ref[0].astype(F32), w_time_scr.shape[0])
    width = out_ref.shape[-1]
    head = width // HEADS
    half = head // 2
    for c in copies[1:3]:
        c.wait()
    for copy in copies[11:]:
        copy.start()
    flat_scr[:rows, :] = state_scr[0].astype(F32)
    flat_scr[rows:, :] = prev_scr[0].astype(F32)
    unpack_tokens(flat_scr, tok_scr, cols, chan)
    for c in copies[3:11]:
        c.wait()
    offset_vec = time_vector(embedded, w_time_scr[...])
    count = rows * cols
    w_in = w_in_scr[...].astype(F32)
    blank = jnp.zeros((LANES - chan, width), F32)
    w_state = jnp.concatenate([w_in[:chan], blank], axis=0).astype(BF16)
    w_prev = jnp.concatenate([w_in[chan:], blank], axis=0).astype(BF16)
    hidden = dot(jnp.concatenate([tok_scr[:count].astype(BF16), tok_scr[count:].astype(BF16)], axis=-1), jnp.concatenate([w_state, w_prev], axis=0))
    hidden = (hidden + offset_vec).astype(BF16)

    pick = shuffle_matrix(width, functools.partial(tile_halves, half))
    w_q = dot(w_qkv_scr[:, :width], pick).astype(BF16)
    w_k = dot(w_qkv_scr[:, width : 2 * width], pick).astype(BF16)
    w_v = w_qkv_scr[:, 2 * width :]
    normed = rms_round_mx(hidden)
    cos, sin = cos_scr[...], sin_scr[...]
    lane = lane_ids((cols, LANES))
    per_tile = LANES // head
    pair = per_tile // 2

    def swap_halves(weight):
        parts = []
        for t in range(width // LANES):
            mid = t * LANES + LANES // 2
            parts += [weight[:, mid : (t + 1) * LANES], weight[:, t * LANES : mid]]
        return jnp.concatenate(parts, axis=-1)

    def spin(part, rolled=False):
        plain = dot(normed, part)
        swapped = None if rolled else dot(normed, swap_halves(part))
        factor = rms_scale_mx(plain)
        tiles = []
        for t in range(width // LANES):
            piece, scale = (x[:, t * LANES : (t + 1) * LANES].reshape(rows, cols, LANES) for x in (plain, factor))
            other = pltpu.roll(piece, LANES // 2, 2) if rolled else swapped[:, t * LANES : (t + 1) * LANES].reshape(rows, cols, LANES)
            tiles.append((piece * cos[None] + other * sin[None]) * scale)
        return tiles

    scale = math.log2(math.e) / math.sqrt(head)
    queries = [(x * scale).astype(BF16) for x in spin(w_q, True)]
    keys = [x.astype(BF16) for x in spin(w_k)]
    values = dot(normed, w_v).astype(BF16).reshape(rows, cols, width)

    mixtures = []
    for row in range(rows):
        outs = []
        for t in range(width // LANES):
            q_tile, k_tile = queries[t][row], keys[t][row]
            v_tile = values[row, :, t * LANES : (t + 1) * LANES]
            results = []
            for side in range(2):
                k_parts, v_parts = [], []
                for n in range(side * pair, (side + 1) * pair):
                    own = (lane % (LANES // 2)) // half == n
                    k_parts.append(jnp.where(own, k_tile, jnp.zeros_like(k_tile)))
                    ones = jnp.where((lane // head) == (n + pair) % per_tile, 1.0, 0.0).astype(BF16)
                    v_parts.append(jnp.where(lane // head == n, v_tile, ones))
                score = dot_nt(q_tile, jnp.concatenate(k_parts, axis=0))
                results.append(dot(jnp.exp2(score).astype(BF16), jnp.concatenate(v_parts, axis=0)))
            low = lane < LANES // 2
            top = jnp.where(low, results[0], results[1])
            bottom = pltpu.roll(jnp.where(low, results[1], results[0]), LANES // 2, 1)
            outs.append(top / bottom)
        mixtures.append(jnp.concatenate(outs, axis=-1))
    mixture = jnp.concatenate(mixtures, axis=0).astype(BF16)
    hidden = (hidden.astype(F32) + dot(mixture, w_ao_scr[...])).astype(BF16)
    out_ref[...] = feed_forward(hidden, w_up_scr[...], w_down_scr[...])
    for copy in copies[11:] + copies[:1]:
        copy.wait()
    pick_ref[0] = anc_scr[lax.axis_index("dom")]
    need = jnp.int32(0)
    if small:
        for j in range(anc_scr.shape[0]):
            need = lax.bitwise_or(need, lax.shift_left(jnp.int32(1), lax.bitwise_xor(anc_scr[j], jnp.int32(j))))
    need_ref[0] = (1 << (anc_scr.shape[0] - 1)) - 1 - lax.shift_right_logical(need, jnp.int32(1))


def project_keys(rows, cols, half, block, h_ref, w_k, w_v, cos_ref, sin_ref):
    wide = HEADS * half
    normed = rms_round(h_ref[...])
    left, right = turn_rows(rows, cols, wide, block, dot(normed, w_k), 1.0, cos_ref, sin_ref)
    values = dot(normed, w_v).astype(BF16).reshape(rows, cols, 2 * wide)
    return left, right, values


def turn_rows(rows, cols, wide, block, part, factor, cos_ref, sin_ref):
    scaled = part * (rms_scale(part) * factor)
    scaled = scaled.reshape(rows, cols, 2 * wide)
    first = lax.bitwise_xor(lax.axis_index("row"), block) * rows
    left, right = [], []
    for row in range(rows):
        cos, sin = cos_ref[pl.ds(first + row, 1), :], sin_ref[pl.ds(first + row, 1), :]
        a, c = scaled[row, :, :wide], scaled[row, :, wide:]
        left.append((a * cos - c * sin).astype(BF16))
        right.append((a * sin + c * cos).astype(BF16))
    return left, right


def mix_rows(rows, cols, half, q_left, q_right, keys, totals):
    wide = HEADS * half
    width = 2 * wide
    ids0 = lax.broadcasted_iota(jnp.int32, (width, width), 0)
    ids1 = lax.broadcasted_iota(jnp.int32, (width, width), 1)
    gather = jnp.where(ids0 // half == ids1 // half, 1.0, 0.0).astype(BF16)
    num_left, num_right, den = totals
    for two in range(0, len(keys), 2):
        prods = [q_left * k_l[None] + q_right * k_r[None] for k_l, k_r, _ in keys[two : two + 2]]
        score = dot(jnp.concatenate(prods, axis=-1).reshape(rows * cols, width), gather)
        weight = jnp.exp2(score).reshape(rows, cols, width)
        for side, (_, _, value) in enumerate(keys[two : two + 2]):
            share = weight[..., side * wide : (side + 1) * wide]
            num_left += share * value[:, :wide].astype(F32)[None]
            num_right += share * value[:, wide:].astype(F32)[None]
            den += share
    return num_left, num_right, den


def all_keys(rows, cols, half, blocks, h_refs, w_k, w_v, cos_ref, sin_ref):
    keys = []
    for block, h_ref in zip(blocks, h_refs):
        left, right, values = project_keys(rows, cols, half, block, h_ref, w_k, w_v, cos_ref, sin_ref)
        keys += [(left[row], right[row], values[row]) for row in range(rows)]
    return keys


def first_kernel(rows, cols, own_ref, *refs):
    w_qkv_ref, w_ao_ref, cos_ref, sin_ref, q_ref, left_ref, right_ref, den_ref, w_kv_ref, w_o_ref = refs
    width = own_ref.shape[-1]
    head = width // HEADS
    half = head // 2
    wide = width // 2
    pick = shuffle_matrix(width, functools.partial(full_halves, width, half))
    w_q = dot(w_qkv_ref[:, :width], pick).astype(BF16)
    w_k = dot(w_qkv_ref[:, width : 2 * width], pick).astype(BF16)
    w_v = dot(w_qkv_ref[:, 2 * width :], pick).astype(BF16)
    w_kv_ref[:, :width] = w_k
    w_kv_ref[:, width:] = w_v
    w_o_ref[...] = lax.dot_general(
        pick, w_ao_ref[...], (((0,), (0,)), ((), ())), preferred_element_type=F32
    ).astype(BF16)
    part = dot(rms_round(own_ref[...]), w_q)
    left, right = turn_rows(rows, cols, wide, 0, part, math.log2(math.e) / math.sqrt(head), cos_ref, sin_ref)
    q_left, q_right = jnp.stack(left), jnp.stack(right)
    q_ref[:, :, :wide] = q_left
    q_ref[:, :, wide:] = q_right
    keys = all_keys(rows, cols, half, [0], [own_ref], w_k, w_v, cos_ref, sin_ref)
    totals = (jnp.zeros((rows, cols, wide), F32),) * 3
    left_ref[...], right_ref[...], den_ref[...] = mix_rows(rows, cols, half, q_left, q_right, keys, totals)


def more_kernel(blocks, rows, cols, *refs):
    h_refs = refs[: len(blocks)]
    q_ref, left_in, right_in, den_in, w_kv_ref, cos_ref, sin_ref, left_ref, right_ref, den_ref = refs[len(blocks) :]
    width = q_ref.shape[-1]
    half = width // HEADS // 2
    wide = width // 2
    keys = all_keys(rows, cols, half, blocks, h_refs, w_kv_ref[:, :width], w_kv_ref[:, width:], cos_ref, sin_ref)
    totals = (left_in[...], right_in[...], den_in[...])
    left_ref[...], right_ref[...], den_ref[...] = mix_rows(
        rows, cols, half, q_ref[:, :, :wide], q_ref[:, :, wide:], keys, totals
    )


def late_kernel(blocks, rows, cols, chan, own_ref, *refs):
    h_refs = refs[: len(blocks)]
    (
        q_ref, left_ref, right_ref, den_ref, w_kv_ref, w_o_ref, w_up_ref, w_down_ref, w_out_ref, cos_ref, sin_ref,
        out_ref, tok_scr,
    ) = refs[len(blocks) :]
    width = own_ref.shape[-1]
    half = width // HEADS // 2
    wide = width // 2
    keys = all_keys(
        rows, cols, half, blocks, h_refs, w_kv_ref[:, :width], w_kv_ref[:, width:], cos_ref, sin_ref
    )
    left, right, den = mix_rows(
        rows, cols, half, q_ref[:, :, :wide], q_ref[:, :, wide:], keys,
        (left_ref[...], right_ref[...], den_ref[...]),
    )
    mixture = jnp.concatenate([left / den, right / den], axis=-1).astype(BF16)
    hidden = (own_ref[...].astype(F32) + dot(mixture.reshape(rows * cols, width), w_o_ref[...])).astype(BF16)
    hidden = feed_forward(hidden, w_up_ref[...], w_down_ref[...])
    tok_scr[:, :chan] = lax.dot_general(
        rms_round_mx(hidden), w_out_ref[...], (((1,), (1,)), ((), ())), preferred_element_type=F32
    )
    pack_tokens(tok_scr, out_ref, rows, cols, chan)


def finish_kernel(turn, pick_ref, coef_ref, *refs):
    count = len(turn)
    states, preds = refs[:count], refs[count : 2 * count]
    new_state_ref, new_pred_ref, state_scr, sems = refs[2 * count :]
    pick = lax.bitwise_xor(pick_ref[0], lax.axis_index("dom"))
    for place, k in enumerate(turn):

        def write(k=place):
            copy_pred = pltpu.make_async_copy(preds[k], new_pred_ref, sems.at[0])
            copy_pred.start()
            state_scr[...] = (
                coef_ref[0:1, 0:1][None] * preds[k][...].astype(F32)
                + coef_ref[1:2, 0:1][None] * states[k][...].astype(F32)
            ).astype(BF16)
            copy_state = pltpu.make_async_copy(state_scr, new_state_ref, sems.at[1])
            copy_state.start()
            copy_pred.wait()
            copy_state.wait()

        if count > 1:
            pl.when(pick == k)(write)
        else:
            write()


VMEM_SPEC = pl.BlockSpec(memory_space=pltpu.VMEM)
SMEM_SPEC = pl.BlockSpec(memory_space=pltpu.SMEM)
HBM_SPEC = pl.BlockSpec(memory_space=pltpu.HBM)


def cube(value, axis, size, bits):
    blocks = [value]
    step = bits // 2
    order = [0]
    while step:
        pairs = [(i, i ^ step) for i in range(size)]
        blocks = blocks + [lax.ppermute(b, axis, pairs) for b in blocks]
        order = order + [o ^ step for o in order]
        step //= 2
    return [blocks[order.index(b)] for b in range(bits)]


def kernel_call(body, name, operands, specs, outs, work, scratch=(), out_specs=None, limit=VMEM_LIMIT):
    single = not isinstance(outs, (list, tuple))
    if out_specs is None:
        out_specs = VMEM_SPEC if single else [VMEM_SPEC] * len(outs)
    return pl.pallas_call(
        body,
        out_shape=outs,
        in_specs=specs,
        out_specs=out_specs,
        scratch_shapes=list(scratch),
        compiler_params=pltpu.CompilerParams(vmem_limit_bytes=limit),
        cost_estimate=pl.CostEstimate(flops=work, bytes_accessed=0, transcendentals=0),
        name=name,
    )(*operands)


def make(mesh):
    n_dom, n_row = mesh.shape["dom"], mesh.shape["row"]

    def per_device(
        state, prev_pred, ancestors, timestep, w_in, w_time, w_qkv, w_attn_out, w_up, w_down, w_out
    ):
        rows, flat = state.shape[1], state.shape[2]
        chan, width = w_out.shape[1], w_out.shape[0]
        cols = flat // chan
        head = width // HEADS
        half = head // 2
        like = jax.ShapeDtypeStruct

        along = rotary_angles(cols, half, LANES)
        sign = np.where(np.arange(LANES) < LANES // 2, -1.0, 1.0)
        tables = [jnp.asarray(np.cos(along), F32), jnp.asarray(np.sin(along) * sign, F32)]
        like_of = lambda arr: like(arr.shape, arr.dtype)
        block_of = lambda arr: like(arr.shape[1:], arr.dtype)
        vmem = lambda arr: pltpu.VMEM(arr.shape, arr.dtype)
        block_vmem = lambda arr: pltpu.VMEM(arr.shape[1:], arr.dtype)
        my_dom = lax.axis_index("dom").astype(jnp.int32)
        small = n_dom in (2, 4)
        inputs = (
            timestep, ancestors, state, prev_pred, w_time, w_in, w_qkv, *tables, w_attn_out, w_up, w_down, w_out.T,
        )
        hidden, state_out, coefs, pick, need, *weights = kernel_call(
            functools.partial(row_kernel, rows, cols, chan, small), "row_block",
            (timestep, *[pltpu.with_memory_space_constraint(x, pltpu.HBM) for x in inputs[1:]]),
            [SMEM_SPEC] + [HBM_SPEC] * (len(inputs) - 1),
            [
                like((rows * cols, width), BF16), like_of(state), like((2, LANES), F32), like((1,), jnp.int32), like((1,), jnp.int32),
                block_of(w_qkv), block_of(w_attn_out), block_of(w_up), block_of(w_down), like_of(w_out.T),
            ],
            5 * WORK_UNIT,
            [
                pltpu.SMEM(ancestors.shape, jnp.int32),
                vmem(prev_pred), vmem(w_time), vmem(w_in), block_vmem(w_qkv), vmem(tables[0]), vmem(tables[1]),
                block_vmem(w_attn_out), block_vmem(w_up), block_vmem(w_down),
                pltpu.VMEM((2 * rows, flat), F32),
                pltpu.VMEM((2 * rows * cols, LANES), F32),
                pltpu.SemaphoreType.DMA((16,)),
            ],
            [VMEM_SPEC] * 3 + [SMEM_SPEC] * 2 + [VMEM_SPEC] * 5,
        )
        w_qkv1, w_ao1, w_up1, w_down1, w_out1 = weights

        top = n_row // 2
        early = cube(hidden, "row", n_row, top)
        across = lax.ppermute(hidden, "row", [(i, i ^ top) for i in range(n_row)])
        down = rotary_angles(n_row * rows, half, width // 2)
        tables = [jnp.asarray(np.cos(down), F32), jnp.asarray(np.sin(down), F32)]
        piece = like((rows, cols, width // 2), F32)
        query, *sums, w_kv, w_o = kernel_call(
            functools.partial(first_kernel, rows, cols), "column_first",
            (hidden, w_qkv1, w_ao1, *tables),
            [VMEM_SPEC] * 5,
            [
                like((rows, cols, width), BF16), piece, piece, piece,
                like((width, 2 * width), BF16), like((width, width), BF16),
            ],
            FIRST_WORK * WORK_UNIT,
        )
        middle = [*early[1:], across]
        sums = kernel_call(
            functools.partial(more_kernel, list(range(1, top + 1)), rows, cols), "column_early",
            (*middle, query, *sums, w_kv, *tables),
            [VMEM_SPEC] * (len(middle) + 7),
            [piece, piece, piece],
            MORE_WORK * WORK_UNIT,
        )
        late = cube(across, "row", n_row, top)[1:]
        late_ids = list(range(top + 1, n_row))
        own_pred = kernel_call(
            functools.partial(late_kernel, late_ids, rows, cols, chan), "column_late",
            (hidden, *late, query, *sums, w_kv, w_o, w_up1, w_down1, w_out1, *tables),
            [VMEM_SPEC] * (len(late) + 12),
            like((1, rows, flat), BF16),
            5 * WORK_UNIT,
            [pltpu.VMEM((rows * cols, LANES), F32)],
        )

        shape = like(state.shape, BF16)

        def finish(turn, states, preds, coefs, pick):
            return kernel_call(
                functools.partial(finish_kernel, turn), "finish",
                (pick, coefs, *states, *preds),
                [SMEM_SPEC] + [VMEM_SPEC] * (1 + 2 * len(preds)),
                (shape, shape),
                WORK_UNIT,
                [pltpu.VMEM(state.shape, BF16), pltpu.SemaphoreType.DMA((2,))],
                (HBM_SPEC, HBM_SPEC),
            )

        if not small:
            every = [
                lax.dynamic_index_in_dim(lax.all_gather(x, "dom"), ancestors[my_dom], 0, keepdims=False)
                for x in (state_out, own_pred)
            ]
            return finish([0], every[:1], every[1:], coefs, pick)

        def swap(value, k):
            return lax.ppermute(value, "dom", [(i, i ^ k) for i in range(n_dom)])

        def gather(turn, states, own_pred, coefs, pick):
            preds = [own_pred] + [swap(own_pred, k) for k in turn]
            return finish([0, *turn], [states[0]] + [states[1 + order.index(k)] for k in turn], preds, coefs, pick)

        order = list(range(2, n_dom)) + [1]
        states = [state_out] + [swap(state_out, k) for k in order]
        branches = [
            functools.partial(gather, [k for k in order if (code >> k) & 1]) for code in range((1 << n_dom) - 2, -1, -2)
        ]
        return lax.switch(need[0], branches, states, own_pred, coefs, pick)

    return per_device


def solution(mesh):
    spread = P(("group", "dom"), "row", None)
    return jax.shard_map(
        make(mesh),
        mesh=mesh,
        in_specs=(spread, spread, P("group"), P("group")) + (P(),) * 7,
        out_specs=(spread, spread),
        check_vma=False,
    )
```
